32 devices in a mesh: grp: 2 (over y), wide: 4 (over z), lev: 2 (over x), sub: 2 (over core).
Axes of the slice: x: 2, y: 2, z: 4, core: 2. Of those that a mesh axis runs over, the one named last changes fastest.
Arguments:
- air_state: float32 [8, 32, 512], P('lev', ('grp', 'sub'), 'wide'), parts along dimension 1, may hold values from -6 to 6
- diffusivity: float32 [32, 512], P(('grp', 'sub'), 'wide'), parts along dimension 0, may hold values from 0.25 to 2
- absorber: float32 [7, 8, 32, 512], P(None, 'lev', ('grp', 'sub'), 'wide'), parts along dimension 2, may hold values from 0 to 1
- thickness: float32 [8, 32, 512], P('lev', ('grp', 'sub'), 'wide'), parts along dimension 1, may hold values from 0.5 to 1.5
- cos_zenith: float32 [32, 512], P(('grp', 'sub'), 'wide'), parts along dimension 0, may hold values from 0.1 to 1
- sunlit: int32 [32, 512], P(('grp', 'sub'), 'wide'), parts along dimension 0, may hold values from 0 to 1, as said below
- absorb_coef: float32 [7, 224], replicated, may hold values from 0.0005 to 0.2
- solar_weight: float32 [224], replicated, may hold values from 0.2 to 2
Outputs:
- heating_rate: float32 [8, 32, 512], P('lev', ('grp', 'sub'), 'wide'), parts along dimension 1
- new_state: float32 [8, 32, 512], P('lev', ('grp', 'sub'), 'wide'), parts along dimension 1
The draws below stay inside these ranges and needn't reach their ends.
There are 2 independent parts, one for each index of `grp`. The reference program is written for one: setup_inputs(seed, part) draws one part's arguments, and reference() takes and returns one part's arrays. A program takes and returns all parts, laid end to end along the dimension named above; an argument that names none is the same for every part. Nothing has to cross between parts.
Inputs may be any that keep to these rules, and one draw needn't show every extreme that they name: For the columns of one device's block of 8 x 128 grid points and the block at the same y position half of the x devices away, the two blocks together hold at most 1024 sunlit columns; some block is wholly sunlit and some pair reaches 1024.
All inputs are finite; a program needn't handle non-finite values.
Results may differ from the reference program's by a relative error of at most 0.0003.
Values sent between devices are 32-bit elements; how exact they have to be, the bound alone decides.
No kernel may reach another device: no remote copies, remote signals or barrier semaphores. Data moves between devices by JAX's collectives and lax.ppermute only.
A program may use at most 64 MiB of HBM per device.

```python
import math
import jax
import jax.numpy as jnp
import numpy as np
from jax import lax

G = 224
S = 7
PX = 128
PY = 8
COLS = 1024
KEEP = 512
LEVELS = 8
NX = 512
NY = 16
N_WIDE = 4
N_SUB = 2


def draw_sunlit(key, part):
    key = jax.random.fold_in(key, 11)
    key_side, key_surplus, key_margin, key_order = jax.random.split(key, 4)
    half_wide = N_WIDE // 2
    day_first = jax.random.randint(key_side, (N_SUB, half_wide), 0, 2)
    surplus = jax.random.randint(key_surplus, (N_SUB, half_wide), 0, KEEP + 1)
    surplus = surplus.at[0, 0].set(KEEP)
    margin = jax.random.randint(key_margin, (N_SUB, half_wide), 0, KEEP - surplus + 1)
    margin = margin.at[0, 0].set(0)
    day_count = KEEP + surplus
    night_count = KEEP - surplus - margin
    lower_half = jnp.where(day_first == 1, day_count, night_count)
    upper_half = jnp.where(day_first == 1, night_count, day_count)
    counts = jnp.concatenate([lower_half, upper_half], axis=1)
    device_keys = jax.random.split(key_order, N_SUB * N_WIDE)
    rank_list = jax.vmap(lambda key_one: jax.random.permutation(key_one, COLS))(device_keys)
    rank_list = rank_list.reshape(N_SUB, N_WIDE, COLS)
    lit_cols = (rank_list < counts[:, :, None]).astype(jnp.int32)
    lit_cols = lit_cols.reshape(N_SUB, N_WIDE, PY, PX)
    return jnp.transpose(lit_cols, (0, 2, 1, 3)).reshape(NY, NX)


def level_of(own_key, extent, cuts, least, high):
    factor_of, own = 1.0, jax.random.fold_in(own_key, 6)
    for dim, blocks in cuts:
        draws = jnp.exp(jax.random.uniform(jax.random.fold_in(own, dim), (blocks,), jnp.float32, least / len(cuts), high / len(cuts)))
        factor_of = factor_of * jnp.repeat(draws, extent[dim] // blocks).reshape([-1 if axis == dim else 1 for axis in range(len(extent))])
    return factor_of


def gaussian(stream_key, shape, deviation, bound, cuts=(), kind=jnp.bfloat16):
    factor_of = level_of(stream_key, shape, cuts, -0.22, 0.18) if cuts else 1.0
    values = jax.random.normal(stream_key, shape, jnp.float32) * deviation * factor_of
    return jnp.minimum(jnp.maximum(values, -bound), bound).astype(kind)


def setup_inputs(seed: int = 0, part: int = 0) -> dict:
    key_of = jax.random.split(jax.random.key(seed), 9)
    part_splits = jax.random.split(jax.random.fold_in(key_of[8], part), 9)
    air_state = gaussian(part_splits[0], (LEVELS, NY, NX), 1.0, 6.0, ((0, 2), (1, 2), (2, 4)), jnp.float32)
    diffusivity = jnp.clip(jnp.exp(math.log(2.0) - 2.0794415 * jax.random.uniform(part_splits[1], (NY, NX), jnp.float32) ** level_of(part_splits[1], (NY, NX), ((0, 2), (1, 4)), -0.2, 0.2)), 0.25, 2.0)
    absorber = jnp.clip(1.0 * jax.random.uniform(part_splits[2], (S, LEVELS, NY, NX), jnp.float32) ** level_of(part_splits[2], (S, LEVELS, NY, NX), ((1, 2), (2, 2), (3, 4)), -0.2, 0.2), 0.0, 1.0)
    thickness = jnp.clip(0.5 + 1.0 * jax.random.uniform(part_splits[3], (LEVELS, NY, NX), jnp.float32) ** level_of(part_splits[3], (LEVELS, NY, NX), ((0, 2), (1, 2), (2, 4)), -0.2, 0.2), 0.5, 1.5)
    cos_zenith = jnp.clip(0.1 + 0.9 * jax.random.uniform(part_splits[4], (NY, NX), jnp.float32) ** level_of(part_splits[4], (NY, NX), ((0, 2), (1, 4)), -0.2, 0.2), 0.1, 1.0)
    sunlit = draw_sunlit(jax.random.fold_in(jax.random.fold_in(key_of[8], part), 71), part)
    absorb_coef = jnp.clip(jnp.exp(jax.random.uniform(key_of[6], (S, G), jnp.float32, math.log(0.0005), math.log(0.2))), 0.0005, 0.2)
    solar_weight = jnp.clip(jnp.exp(jax.random.uniform(key_of[7], (G,), jnp.float32, math.log(0.2), math.log(2.0))), 0.2, 2.0)
    return {"air_state": air_state, "diffusivity": diffusivity, "absorber": absorber, "thickness": thickness, "cos_zenith": cos_zenith, "sunlit": sunlit, "absorb_coef": absorb_coef, "solar_weight": solar_weight}


def derivative_table():
    root_five = math.sqrt(5.0)
    outer_big = (5.0 + 5.0 * root_five) / 4.0
    outer_small = (5.0 * root_five - 5.0) / 4.0
    inner_big = (1.0 + root_five) / 4.0
    inner_mid = root_five / 2.0
    inner_small = (root_five - 1.0) / 4.0
    return np.array([[-3.0, outer_big, -outer_small, 0.5], [-inner_big, 0.0, inner_mid, -inner_small], [inner_small, -inner_mid, 0.0, inner_big], [-0.5, outer_small, -outer_big, 3.0]])
gll_weights = np.array([1.0 / 6.0, 5.0 / 6.0, 5.0 / 6.0, 1.0 / 6.0])
mass_points = np.array([1.0 / 3.0, 5.0 / 6.0, 5.0 / 6.0, 1.0 / 3.0])
time_step = 0.004
high = lax.Precision.HIGHEST

def column_heat(amount, layers, zenith, lit, absorb_coef, solar_weight):
    tau = jnp.einsum('skc,sg->kgc', amount, absorb_coef, precision=high)
    trans = jnp.exp(-tau / zenith)
    inclusive = jnp.cumprod(trans, axis=0)
    above = jnp.concatenate([jnp.ones((1,) + trans.shape[1:], trans.dtype), inclusive[:-1]], axis=0)
    absorbed = zenith * above * (1.0 - trans)
    heat = jnp.einsum('kgc,g->kc', absorbed, solar_weight, precision=high) / layers
    return jnp.where(lit[None, :] == 1, heat, jnp.zeros_like(heat))

def residual_field(field, diffusivity):
    levels, rows, width = field.shape
    table = derivative_table()
    points = table.shape[0]
    field5 = field.reshape(levels, rows // points, points, width // points, points)
    kappa5 = diffusivity.reshape(1, rows // points, points, width // points, points)
    deriv = jnp.asarray(table, field.dtype)
    weights = jnp.asarray(gll_weights, field.dtype)
    grad_x = jnp.einsum('qi,lajbi->lajbq', deriv, field5, precision=high)
    flux_x = kappa5 * weights[None, None, None, None, :] * grad_x
    part_x = -weights[None, None, :, None, None] * jnp.einsum('qi,lajbq->lajbi', deriv, flux_x, precision=high)
    grad_y = jnp.einsum('qj,lajbi->laqbi', deriv, field5, precision=high)
    flux_y = kappa5 * weights[None, None, :, None, None] * grad_y
    part_y = -weights[None, None, None, None, :] * jnp.einsum('qj,laqbi->lajbi', deriv, flux_y, precision=high)
    return (part_x + part_y).reshape(levels, rows, width)

def assemble(field):
    points = 4
    width = field.shape[2]
    rows = field.shape[1]
    first_x = (jnp.arange(width) % points == 0).astype(field.dtype)
    last_x = (jnp.arange(width) % points == points - 1).astype(field.dtype)
    first_y = (jnp.arange(rows) % points == 0).astype(field.dtype)[:, None]
    last_y = (jnp.arange(rows) % points == points - 1).astype(field.dtype)[:, None]
    summed = field + first_x * jnp.roll(field, 1, axis=2) + last_x * jnp.roll(field, -1, axis=2)
    return summed + first_y * jnp.roll(summed, 1, axis=1) + last_y * jnp.roll(summed, -1, axis=1)

def tendency(field, diffusivity):
    rows, width = (field.shape[1], field.shape[2])
    points = 4
    mass_x = jnp.asarray(np.tile(mass_points, width // points), field.dtype)
    mass_y = jnp.asarray(np.tile(mass_points, rows // points), field.dtype)
    return assemble(residual_field(field, diffusivity)) / (mass_y[:, None] * mass_x[None, :])

def reference(air_state, diffusivity, absorber, thickness, cos_zenith, sunlit, absorb_coef, solar_weight):
    amount_rows = jnp.transpose(absorber, (2, 0, 1, 3))
    layer_rows = jnp.transpose(thickness, (1, 0, 2))

    def one_row(items):
        return column_heat(items[0], items[1], items[2], items[3], absorb_coef, solar_weight)
    heat_rows = lax.map(one_row, (amount_rows, layer_rows, cos_zenith, sunlit))
    heating_rate = jnp.transpose(heat_rows, (1, 0, 2))
    first = air_state + time_step * (tendency(air_state, diffusivity) + heating_rate)
    new_state = 0.5 * (air_state + first + time_step * (tendency(first, diffusivity) + heating_rate))
    return (heating_rate, new_state)
```

```python
import math

import jax
import jax.numpy as jnp
import numpy as np
from jax import lax
from jax.experimental import pallas as pl
from jax.experimental.pallas import tpu as pltpu
from jax.sharding import PartitionSpec as P

time_step = 0.004
points = 4
log2e = 1.4426950408889634
gll_weights = (1.0 / 6.0, 5.0 / 6.0, 5.0 / 6.0, 1.0 / 6.0)
mass_points = (1.0 / 3.0, 5.0 / 6.0, 5.0 / 6.0, 1.0 / 3.0)


def derivative_table():
    root_five = math.sqrt(5.0)
    outer_big = (5.0 + 5.0 * root_five) / 4.0
    outer_small = (5.0 * root_five - 5.0) / 4.0
    inner_big = (1.0 + root_five) / 4.0
    inner_mid = root_five / 2.0
    inner_small = (root_five - 1.0) / 4.0
    return np.array(
        [
            [-3.0, outer_big, -outer_small, 0.5],
            [-inner_big, 0.0, inner_mid, -inner_small],
            [inner_small, -inner_mid, 0.0, inner_big],
            [-0.5, outer_small, -outer_big, 3.0],
        ]
    )


table = derivative_table()


def by_node(node, values):
    out = jnp.full(node.shape, values[3], jnp.float32)
    for i in (2, 1, 0):
        out = jnp.where(node == i, jnp.float32(values[i]), out)
    return out


class Stencil:
    def __init__(self, rows, width):
        self.shape = (rows, width)
        self.row = lax.broadcasted_iota(jnp.int32, (rows, width), 0)
        self.lane = lax.broadcasted_iota(jnp.int32, (rows, width), 1)
        node_y, node_x = self.row % points, self.lane % points
        self.weight_x = by_node(node_x, gll_weights)
        self.weight_y = by_node(node_y, gll_weights)
        self.coefs = {}
        for name, matrix in (("d", table), ("t", table.T)):
            for axis, node in ((0, node_y), (1, node_x)):
                terms = []
                for step in range(-3, 4):
                    values = [
                        matrix[i, i + step] if 0 <= i + step < points else 0.0
                        for i in range(points)
                    ]
                    terms.append(by_node(node, values))
                self.coefs[name, axis] = terms
        self.inv_mass = by_node(node_y, [1.0 / m for m in mass_points]) * by_node(
            node_x, [1.0 / m for m in mass_points]
        )
        self.first_x = (node_x == 0).astype(jnp.float32)
        self.last_x = (node_x == points - 1).astype(jnp.float32)
        self.first_y = (node_y == 0).astype(jnp.float32)
        self.last_y = (node_y == points - 1).astype(jnp.float32)

    def apply(self, name, axis, field):
        size = self.shape[axis]
        out = None
        for step, coef in zip(range(-3, 4), self.coefs[name, axis]):
            if step == 0 and name == "d":
                moved = field
            else:
                moved = pltpu.roll(field, (-step) % size, field.ndim - 2 + axis)
            term = coef * moved
            out = term if out is None else out + term
        return out

    def shifted(self, field, axis, step):
        size = self.shape[axis]
        index = self.row if axis == 0 else self.lane
        moved = pltpu.roll(field, step % size, field.ndim - 2 + axis)
        if axis == 0:
            other = jnp.concatenate([moved[:, 1:], moved[:, :1]], axis=1)
        else:
            other = jnp.concatenate([moved[:, :, 1:], moved[:, :, :1]], axis=2)
        edge = 0 if step == 1 else size - 1
        return jnp.where(index == edge, other, moved)

    def tendency(self, field, kappa):
        flux_x = kappa * self.weight_x * self.apply("d", 1, field)
        flux_y = kappa * self.weight_y * self.apply("d", 0, field)
        r = -self.weight_y * self.apply("t", 1, flux_x) - self.weight_x * self.apply("t", 0, flux_y)
        r = (
            r
            + self.first_x * self.shifted(r, 1, 1)
            + self.last_x * self.shifted(r, 1, -1)
        )
        r = (
            r
            + self.first_y * self.shifted(r, 0, 1)
            + self.last_y * self.shifted(r, 0, -1)
        )
        return r * self.inv_mass


def split(value, pieces):
    out = []
    for _ in range(pieces):
        high = value.astype(jnp.bfloat16)
        out.append(high)
        value = value - high.astype(jnp.float32)
    return out


def radiate_kernel(
    absorber, upper, zenith, lit, thickness, coef, weight, heat, spread, left
):
    species, levels, rows, width = absorber.shape
    terms = coef.shape[1]
    group = species * rows
    depth = 256
    c_pieces = split(coef[...], 2)
    w_pieces = split(jnp.log2(weight[...]), 3)
    lane = lax.broadcasted_iota(jnp.int32, (rows, depth), 1)
    row = lax.broadcasted_iota(jnp.int32, (rows, depth), 0)
    ones_at = 4 * group
    stack = jnp.concatenate(
        [p.astype(jnp.float32) for p in c_pieces] + [p.astype(jnp.float32) for p in w_pieces],
        axis=0,
    )
    count = stack.shape[0]
    pick_row = lax.broadcasted_iota(jnp.int32, (count, depth), 0)
    pick_lane = lax.broadcasted_iota(jnp.int32, (count, depth), 1)
    kind = pick_lane // group
    wanted = jnp.where(kind == 3, species, 0) + (pick_lane % group) // rows
    wanted = jnp.where(kind >= 4, 2 * species + pick_lane - ones_at, wanted)
    pick = (pick_row == wanted).astype(jnp.bfloat16)
    spread[...] = lax.dot_general(
        stack.astype(jnp.bfloat16),
        pick,
        (((0,), (0,)), ((), ())),
        preferred_element_type=jnp.float32,
    )
    mask = ((lane % rows == row) | (lane >= ones_at)).astype(jnp.float32)
    for g in range(0, terms, 2):
        pair = [jnp.broadcast_to(spread[pl.ds(g + i, 1), :], (rows, depth)) * mask for i in (0, 1)]
        left[pl.ds(g * rows, 2 * rows), :] = jnp.concatenate(pair, axis=0).astype(jnp.bfloat16)

    scale = -log2e / zenith[...]
    total = [upper[s] for s in range(species)]
    blocks = []
    for k in range(levels + 1):
        if k:
            total = [total[s] + absorber[s, k - 1] for s in range(species)]
        value = jnp.concatenate([t * scale for t in total], axis=0)
        hi, mid, lo = (p.astype(jnp.float32) for p in split(value, 3))
        ones = jnp.where(
            lax.broadcasted_iota(jnp.int32, (depth - ones_at, width), 0) < 3, 1.0, 0.0
        )
        blocks.append(jnp.concatenate([hi, mid, lo, hi, ones], axis=0).astype(jnp.bfloat16))
    right = jnp.concatenate(blocks, axis=1)

    chunk = 448
    sums = [jnp.zeros((rows, width), jnp.float32) for _ in range(levels)]
    for start in range(0, terms * rows, chunk):
        out = jnp.exp2(
            jnp.dot(left[pl.ds(start, chunk), :], right, preferred_element_type=jnp.float32)
        )
        for k in range(levels):
            drop = out[:, k * width : (k + 1) * width] - out[:, (k + 1) * width : (k + 2) * width]
            sums[k] = sums[k] + jnp.sum(drop.reshape(chunk // rows, rows, width), axis=0)
    lit_zenith = jnp.where(lit[...] == 1, zenith[...], 0.0)
    for k in range(levels):
        heat[k] = lit_zenith * sums[k] / thickness[k]


def strips(levels):
    return [(i, tile) for i in range(2 * levels + 1) for tile in range(2)]


def pack_kernel(own_state, own_heat, other_state, other_heat, odd_first, even_first):
    levels = own_heat.shape[0]
    rows, width = own_heat.shape[1:]
    edge = 2 * points
    slots = width // edge
    lane = lax.broadcasted_iota(jnp.int32, (rows, width), 1)
    tiles = [(jnp.zeros((rows, width), jnp.float32), jnp.zeros((rows, width), jnp.float32)) for _ in range(own_first_tiles(levels, slots))]
    for j, (i, tile) in enumerate(strips(levels)):
        state, heat = (own_state, own_heat) if tile == 0 else (other_state, other_heat)
        value = state[i] if i <= levels else heat[i - levels - 1]
        n, slot = divmod(j, slots)
        here = lane // edge == slot
        low = pltpu.roll(value, (slot * edge) % width, 1)
        high = pltpu.roll(value, (slot * edge + edge) % width, 1)
        tiles[n] = (jnp.where(here, low, tiles[n][0]), jnp.where(here, high, tiles[n][1]))
    even = lax.axis_index("wide") % 2 == 0
    for n, (low, high) in enumerate(tiles):
        odd_first[n] = jnp.where(even, low, high)
        even_first[n] = jnp.where(even, high, low)


def own_first_tiles(levels, slots):
    return -(-(2 * (2 * levels + 1)) // slots)


def step_kernel(own_state, own_heat, other_state, other_heat, got_one, got_two, out):
    levels = own_heat.shape[0]
    rows, width = own_heat.shape[1:]
    edge = 2 * points
    slots = width // edge
    stencil = Stencil(rows, width)
    even = lax.axis_index("wide") % 2 == 0
    lane = stencil.lane
    halo = {}
    for j, (i, tile) in enumerate(strips(levels)):
        n, slot = divmod(j, slots)
        from_left = jnp.where(even, got_one[n], got_two[n])
        from_right = jnp.where(even, got_two[n], got_one[n])
        after = pltpu.roll(from_right, (-slot * edge) % width, 1)
        before = pltpu.roll(from_left, (-slot * edge - edge) % width, 1)
        value = jnp.where(lane < edge, after, jnp.where(lane >= width - edge, before, 0.0))
        halo[i, tile] = value

    def ring(i):
        parts = []
        for tile in range(2):
            state, heat = (own_state, own_heat) if tile == 0 else (other_state, other_heat)
            main = state[i] if i <= levels else heat[i - levels - 1]
            parts.append(jnp.stack([main, halo[i, tile]], axis=0))
        return jnp.stack(parts, axis=0)

    air = jnp.stack([ring(i) for i in range(levels)], axis=0)
    kappa = ring(levels)[None]
    heat = jnp.stack([ring(levels + 1 + i) for i in range(levels)], axis=0)
    first = air + time_step * (stencil.tendency(air, kappa) + heat)
    new = 0.5 * (air + first + time_step * (stencil.tendency(first, kappa) + heat))
    for k in range(levels):
        out[k] = new[k, 0, 0]


def swap(value, axis, pairs):
    route = [(a, b) for a, b in pairs] + [(b, a) for a, b in pairs]
    return lax.ppermute(value, axis, route)


def shards(
    air_state, diffusivity, absorber, thickness, cos_zenith, sunlit, absorb_coef, solar_weight
):
    levels, rows, width = air_state.shape
    terms = absorb_coef.shape[1]
    tile = lambda n: jax.ShapeDtypeStruct((n, rows, width), jnp.float32)
    big = pltpu.CompilerParams(vmem_limit_bytes=32 * 1024 * 1024)
    own_state = jnp.concatenate([air_state, diffusivity[None]], axis=0)
    other_state = swap(own_state, "sub", [(0, 1)])
    amount = jnp.sum(absorber, axis=1)
    size = lax.axis_size("lev")
    upper = jnp.zeros_like(amount)
    for step in range(1, size):
        upper = upper + lax.ppermute(amount, "lev", [(i, i + step) for i in range(size - step)])
    heat = pl.pallas_call(
        radiate_kernel,
        out_shape=tile(levels),
        scratch_shapes=[
            pltpu.VMEM((terms, 256), jnp.float32),
            pltpu.VMEM((terms * rows, 256), jnp.bfloat16),
        ],
        compiler_params=big,
        name="radiate",
    )(absorber, upper, cos_zenith, sunlit, thickness, absorb_coef, solar_weight[None])
    other_heat = swap(heat, "sub", [(0, 1)])
    tiles = own_first_tiles(levels, width // (2 * points))
    odd_first, even_first = pl.pallas_call(
        pack_kernel, out_shape=(tile(tiles), tile(tiles)), compiler_params=big, name="pack"
    )(own_state, heat, other_state, other_heat)
    wide = lax.axis_size("wide")
    got_one = swap(odd_first, "wide", [(i, (i + 1) % wide) for i in range(1, wide, 2)])
    got_two = swap(even_first, "wide", [(i, i + 1) for i in range(0, wide, 2)])
    new_state = pl.pallas_call(
        step_kernel, out_shape=tile(levels), compiler_params=big, name="step"
    )(own_state, heat, other_state, other_heat, got_one, got_two)
    return (heat, new_state)


def solution(mesh):
    in_specs = (
        P("lev", ("grp", "sub"), "wide"),
        P(("grp", "sub"), "wide"),
        P(None, "lev", ("grp", "sub"), "wide"),
        P("lev", ("grp", "sub"), "wide"),
        P(("grp", "sub"), "wide"),
        P(("grp", "sub"), "wide"),
        P(),
        P(),
    )
    out_specs = (P("lev", ("grp", "sub"), "wide"), P("lev", ("grp", "sub"), "wide"))
    return jax.shard_map(shards, mesh=mesh, in_specs=in_specs, out_specs=out_specs, check_vma=False)
```

```python
import math

import jax
import jax.numpy as jnp
import numpy as np
from jax import lax
from jax.experimental import pallas as pl
from jax.experimental.pallas import tpu as pltpu
from jax.sharding import PartitionSpec as P

time_step = 0.004
points = 4
log2e = 1.4426950408889634
gll_weights = (1.0 / 6.0, 5.0 / 6.0, 5.0 / 6.0, 1.0 / 6.0)
mass_points = (1.0 / 3.0, 5.0 / 6.0, 5.0 / 6.0, 1.0 / 3.0)


def derivative_table():
    root_five = math.sqrt(5.0)
    outer_big = (5.0 + 5.0 * root_five) / 4.0
    outer_small = (5.0 * root_five - 5.0) / 4.0
    inner_big = (1.0 + root_five) / 4.0
    inner_mid = root_five / 2.0
    inner_small = (root_five - 1.0) / 4.0
    return np.array(
        [
            [-3.0, outer_big, -outer_small, 0.5],
            [-inner_big, 0.0, inner_mid, -inner_small],
            [inner_small, -inner_mid, 0.0, inner_big],
            [-0.5, outer_small, -outer_big, 3.0],
        ]
    )


table = derivative_table()


def by_node(node, values):
    out = jnp.full(node.shape, values[3], jnp.float32)
    for i in (2, 1, 0):
        out = jnp.where(node == i, jnp.float32(values[i]), out)
    return out


class Stencil:
    def __init__(self, rows, width):
        self.shape = (rows, width)
        self.row = lax.broadcasted_iota(jnp.int32, (rows, width), 0)
        self.lane = lax.broadcasted_iota(jnp.int32, (rows, width), 1)
        node_y, node_x = self.row % points, self.lane % points
        self.weight_x = by_node(node_x, gll_weights)
        self.weight_y = by_node(node_y, gll_weights)
        self.coefs = {}
        for name, matrix in (("d", table), ("t", table.T)):
            for axis, node in ((0, node_y), (1, node_x)):
                terms = []
                for step in range(-3, 4):
                    values = [
                        matrix[i, i + step] if 0 <= i + step < points else 0.0
                        for i in range(points)
                    ]
                    terms.append(by_node(node, values))
                self.coefs[name, axis] = terms
        self.inv_mass = by_node(node_y, [1.0 / m for m in mass_points]) * by_node(
            node_x, [1.0 / m for m in mass_points]
        )
        self.first_x = (node_x == 0).astype(jnp.float32)
        self.last_x = (node_x == points - 1).astype(jnp.float32)
        self.first_y = (node_y == 0).astype(jnp.float32)
        self.last_y = (node_y == points - 1).astype(jnp.float32)

    def apply(self, name, axis, field):
        size = self.shape[axis]
        out = None
        for step, coef in zip(range(-3, 4), self.coefs[name, axis]):
            if step == 0 and name == "d":
                moved = field
            else:
                moved = pltpu.roll(field, (-step) % size, field.ndim - 2 + axis)
            term = coef * moved
            out = term if out is None else out + term
        return out

    def shifted(self, field, axis, step):
        size = self.shape[axis]
        index = self.row if axis == 0 else self.lane
        moved = pltpu.roll(field, step % size, field.ndim - 2 + axis)
        if axis == 0:
            other = jnp.concatenate([moved[:, 1:], moved[:, :1]], axis=1)
        else:
            other = jnp.concatenate([moved[:, :, 1:], moved[:, :, :1]], axis=2)
        edge = 0 if step == 1 else size - 1
        return jnp.where(index == edge, other, moved)

    def tendency(self, field, kappa):
        flux_x = kappa * self.weight_x * self.apply("d", 1, field)
        flux_y = kappa * self.weight_y * self.apply("d", 0, field)
        r = -self.weight_y * self.apply("t", 1, flux_x) - self.weight_x * self.apply("t", 0, flux_y)
        r = (
            r
            + self.first_x * self.shifted(r, 1, 1)
            + self.last_x * self.shifted(r, 1, -1)
        )
        r = (
            r
            + self.first_y * self.shifted(r, 0, 1)
            + self.last_y * self.shifted(r, 0, -1)
        )
        return r * self.inv_mass


def split(value, pieces):
    out = []
    for _ in range(pieces):
        high = value.astype(jnp.bfloat16)
        out.append(high)
        value = value - high.astype(jnp.float32)
    return out


def amount_rows(totals, scale, depth, ones):
    value = jnp.concatenate([t * scale for t in totals], axis=0)
    hi, mid, lo = (p.astype(jnp.float32) for p in split(value, 3))
    rest = depth - 4 * value.shape[0]
    index = lax.broadcasted_iota(jnp.int32, (rest, value.shape[1]), 0)
    tail = jnp.where(index < ones, 1.0, 0.0)
    return jnp.concatenate([hi, mid, lo, hi, tail], axis=0).astype(jnp.bfloat16)


def layers_kernel(absorber, zenith, coef, weight, left, drops, spread):
    species, levels, rows, width = absorber.shape
    terms = coef.shape[1]
    group = species * rows
    depth = left.shape[1]
    c_pieces = split(coef[...], 2)
    w_pieces = split(jnp.log2(weight[...]), 3)
    lane = lax.broadcasted_iota(jnp.int32, (rows, depth), 1)
    row = lax.broadcasted_iota(jnp.int32, (rows, depth), 0)
    ones_at = 4 * group
    stack = jnp.concatenate([p.astype(jnp.float32) for p in c_pieces + w_pieces], axis=0)
    count = stack.shape[0]
    pick_row = lax.broadcasted_iota(jnp.int32, (count, depth), 0)
    pick_lane = lax.broadcasted_iota(jnp.int32, (count, depth), 1)
    kind = pick_lane // group
    wanted = jnp.where(kind == 3, species, 0) + (pick_lane % group) // rows
    wanted = jnp.where(kind >= 4, 2 * species + pick_lane - ones_at, wanted)
    pick = (pick_row == wanted).astype(jnp.bfloat16)
    spread[...] = lax.dot_general(
        stack.astype(jnp.bfloat16),
        pick,
        (((0,), (0,)), ((), ())),
        preferred_element_type=jnp.float32,
    )
    mask = ((lane % rows == row) | (lane >= ones_at)).astype(jnp.float32)
    for g in range(0, terms, 2):
        pair = [jnp.broadcast_to(spread[pl.ds(g + i, 1), :], (rows, depth)) * mask for i in (0, 1)]
        left[pl.ds(g * rows, 2 * rows), :] = jnp.concatenate(pair, axis=0).astype(jnp.bfloat16)

    scale = -log2e / zenith[...]
    totals = [jnp.zeros((rows, width), jnp.float32)] * species
    blocks = []
    for k in range(levels + 1):
        if k:
            totals = [totals[s] + absorber[s, k - 1] for s in range(species)]
        blocks.append(amount_rows(totals, scale, depth, 3))
    right = jnp.concatenate(blocks, axis=1)
    chunk = 448
    for start in range(0, terms * rows, chunk):
        out = jnp.exp2(
            jnp.dot(left[pl.ds(start, chunk), :], right, preferred_element_type=jnp.float32)
        )
        for k in range(levels):
            drop = out[:, k * width : (k + 1) * width] - out[:, (k + 1) * width : (k + 2) * width]
            drops[k, pl.ds(start, chunk), :] = drop


def radiate_kernel(left, drops, upper, zenith, lit, thickness, heat):
    levels, rows, width = heat.shape
    depth = left.shape[1]
    species = upper.shape[0]
    zen = zenith[...]
    below = lax.axis_index("lev") > 0
    totals = [jnp.where(below, upper[s], 0.0) for s in range(species)]
    right = amount_rows(totals, -log2e / zen, depth, 0)
    chunk = 448
    sums = [jnp.zeros((rows, width), jnp.float32) for _ in range(levels)]
    for start in range(0, left.shape[0], chunk):
        above = jnp.exp2(
            jnp.dot(left[pl.ds(start, chunk), :], right, preferred_element_type=jnp.float32)
        )
        for k in range(levels):
            absorbed = above * drops[k, pl.ds(start, chunk), :]
            sums[k] = sums[k] + jnp.sum(absorbed.reshape(chunk // rows, rows, width), axis=0)
    lit_zenith = jnp.where(lit[...] == 1, zen, 0.0)
    for k in range(levels):
        heat[k] = lit_zenith * sums[k] / thickness[k]


def strips(levels):
    return [(i, tile) for i in range(2 * levels + 1) for tile in range(2)]


def pack_kernel(own_state, own_heat, other_state, other_heat, odd_first, even_first):
    levels = own_heat.shape[0]
    rows, width = own_heat.shape[1:]
    edge = 2 * points
    slots = width // edge
    lane = lax.broadcasted_iota(jnp.int32, (rows, width), 1)
    tiles = [(jnp.zeros((rows, width), jnp.float32), jnp.zeros((rows, width), jnp.float32)) for _ in range(own_first_tiles(levels, slots))]
    for j, (i, tile) in enumerate(strips(levels)):
        state, heat = (own_state, own_heat) if tile == 0 else (other_state, other_heat)
        value = state[i] if i <= levels else heat[i - levels - 1]
        n, slot = divmod(j, slots)
        here = lane // edge == slot
        low = pltpu.roll(value, (slot * edge) % width, 1)
        high = pltpu.roll(value, (slot * edge + edge) % width, 1)
        tiles[n] = (jnp.where(here, low, tiles[n][0]), jnp.where(here, high, tiles[n][1]))
    even = lax.axis_index("wide") % 2 == 0
    for n, (low, high) in enumerate(tiles):
        odd_first[n] = jnp.where(even, low, high)
        even_first[n] = jnp.where(even, high, low)


def own_first_tiles(levels, slots):
    return -(-(2 * (2 * levels + 1)) // slots)


def step_kernel(own_state, own_heat, other_state, other_heat, got_one, got_two, heat_out, out):
    levels = own_heat.shape[0]
    rows, width = own_heat.shape[1:]
    edge = 2 * points
    slots = width // edge
    stencil = Stencil(rows, width)
    even = lax.axis_index("wide") % 2 == 0
    lane = stencil.lane
    halo = {}
    for j, (i, tile) in enumerate(strips(levels)):
        n, slot = divmod(j, slots)
        from_left = jnp.where(even, got_one[n], got_two[n])
        from_right = jnp.where(even, got_two[n], got_one[n])
        after = pltpu.roll(from_right, (-slot * edge) % width, 1)
        before = pltpu.roll(from_left, (-slot * edge - edge) % width, 1)
        value = jnp.where(lane < edge, after, jnp.where(lane >= width - edge, before, 0.0))
        halo[i, tile] = value

    def ring(i):
        parts = []
        for tile in range(2):
            state, heat = (own_state, own_heat) if tile == 0 else (other_state, other_heat)
            main = state[i] if i <= levels else heat[i - levels - 1]
            parts.append(jnp.stack([main, halo[i, tile]], axis=0))
        return jnp.stack(parts, axis=0)

    air = jnp.stack([ring(i) for i in range(levels)], axis=0)
    kappa = ring(levels)[None]
    heat = jnp.stack([ring(levels + 1 + i) for i in range(levels)], axis=0)
    first = air + time_step * (stencil.tendency(air, kappa) + heat)
    new = 0.5 * (air + first + time_step * (stencil.tendency(first, kappa) + heat))
    for k in range(levels):
        out[k] = new[k, 0, 0]
        heat_out[k] = own_heat[k]


def swap(value, axis, pairs):
    route = [(a, b) for a, b in pairs] + [(b, a) for a, b in pairs]
    return lax.ppermute(value, axis, route)


def shards(
    air_state, diffusivity, absorber, thickness, cos_zenith, sunlit, absorb_coef, solar_weight
):
    levels, rows, width = air_state.shape
    terms = absorb_coef.shape[1]
    tile = lambda n: jax.ShapeDtypeStruct((n, rows, width), jnp.float32)
    big = pltpu.CompilerParams(vmem_limit_bytes=32 * 1024 * 1024)
    own_state = jnp.concatenate([air_state, diffusivity[None]], axis=0)
    amount = jnp.sum(absorber, axis=1)
    size = lax.axis_size("lev")
    lev = lax.axis_index("lev")
    upper = None
    for step in range(1, size):
        moved = lax.ppermute(amount, "lev", [(i, (i + step) % size) for i in range(size)])
        if size > 2:
            moved = jnp.where(lev >= step, moved, 0.0)
        upper = moved if upper is None else upper + moved
    if upper is None:
        upper = jnp.zeros_like(amount)
    other_state = swap(own_state, "sub", [(0, 1)])
    left, drops = pl.pallas_call(
        layers_kernel,
        out_shape=(
            jax.ShapeDtypeStruct((terms * rows, 256), jnp.bfloat16),
            jax.ShapeDtypeStruct((levels, terms * rows, width), jnp.float32),
        ),
        scratch_shapes=[pltpu.VMEM((terms, 256), jnp.float32)],
        compiler_params=big,
        name="layers",
    )(absorber, cos_zenith, absorb_coef, solar_weight[None])
    own_heat = pl.pallas_call(
        radiate_kernel, out_shape=tile(levels), compiler_params=big, name="radiate"
    )(left, drops, upper, cos_zenith, sunlit, thickness)
    other_heat = swap(own_heat, "sub", [(0, 1)])
    tiles = own_first_tiles(levels, width // (2 * points))
    odd_first, even_first = pl.pallas_call(
        pack_kernel, out_shape=(tile(tiles), tile(tiles)), compiler_params=big, name="pack"
    )(own_state, own_heat, other_state, other_heat)
    wide = lax.axis_size("wide")
    got_two = swap(even_first, "wide", [(i, i + 1) for i in range(0, wide, 2)])
    got_one = swap(odd_first, "wide", [(i, (i + 1) % wide) for i in range(1, wide, 2)])
    heat, new_state = pl.pallas_call(
        step_kernel, out_shape=(tile(levels), tile(levels)), compiler_params=big, name="step"
    )(own_state, own_heat, other_state, other_heat, got_one, got_two)
    return (heat, new_state)


def solution(mesh):
    in_specs = (
        P("lev", ("grp", "sub"), "wide"),
        P(("grp", "sub"), "wide"),
        P(None, "lev", ("grp", "sub"), "wide"),
        P("lev", ("grp", "sub"), "wide"),
        P(("grp", "sub"), "wide"),
        P(("grp", "sub"), "wide"),
        P(),
        P(),
    )
    out_specs = (P("lev", ("grp", "sub"), "wide"), P("lev", ("grp", "sub"), "wide"))
    return jax.shard_map(shards, mesh=mesh, in_specs=in_specs, out_specs=out_specs, check_vma=False)
```

```python
import math

import jax
import jax.numpy as jnp
import numpy as np
from jax import lax
from jax.experimental import pallas as pl
from jax.experimental.pallas import tpu as pltpu
from jax.sharding import PartitionSpec as P

time_step = 0.004
points = 4
log2e = 1.4426950408889634
gll_weights = (1.0 / 6.0, 5.0 / 6.0, 5.0 / 6.0, 1.0 / 6.0)
mass_points = (1.0 / 3.0, 5.0 / 6.0, 5.0 / 6.0, 1.0 / 3.0)


def derivative_table():
    root_five = math.sqrt(5.0)
    outer_big = (5.0 + 5.0 * root_five) / 4.0
    outer_small = (5.0 * root_five - 5.0) / 4.0
    inner_big = (1.0 + root_five) / 4.0
    inner_mid = root_five / 2.0
    inner_small = (root_five - 1.0) / 4.0
    return np.array(
        [
            [-3.0, outer_big, -outer_small, 0.5],
            [-inner_big, 0.0, inner_mid, -inner_small],
            [inner_small, -inner_mid, 0.0, inner_big],
            [-0.5, outer_small, -outer_big, 3.0],
        ]
    )


table = derivative_table()


def by_node(node, values):
    out = jnp.full(node.shape, values[3], jnp.float32)
    for i in (2, 1, 0):
        out = jnp.where(node == i, jnp.float32(values[i]), out)
    return out


class Stencil:
    def __init__(self, rows, width):
        self.shape = (rows, width)
        self.row = lax.broadcasted_iota(jnp.int32, (rows, width), 0)
        self.lane = lax.broadcasted_iota(jnp.int32, (rows, width), 1)
        node_y, node_x = self.row % points, self.lane % points
        self.weight_x = by_node(node_x, gll_weights)
        self.weight_y = by_node(node_y, gll_weights)
        self.coefs = {}
        for name, matrix in (("d", table), ("t", table.T)):
            for axis, node in ((0, node_y), (1, node_x)):
                terms = []
                for step in range(-3, 4):
                    values = [
                        matrix[i, i + step] if 0 <= i + step < points else 0.0
                        for i in range(points)
                    ]
                    terms.append(by_node(node, values))
                self.coefs[name, axis] = terms
        self.inv_mass = by_node(node_y, [1.0 / m for m in mass_points]) * by_node(
            node_x, [1.0 / m for m in mass_points]
        )
        self.first_x = (node_x == 0).astype(jnp.float32)
        self.last_x = (node_x == points - 1).astype(jnp.float32)
        self.first_y = (node_y == 0).astype(jnp.float32)
        self.last_y = (node_y == points - 1).astype(jnp.float32)

    def apply(self, name, axis, field):
        size = self.shape[axis]
        out = None
        for step, coef in zip(range(-3, 4), self.coefs[name, axis]):
            if step == 0 and name == "d":
                moved = field
            else:
                moved = pltpu.roll(field, (-step) % size, field.ndim - 2 + axis)
            term = coef * moved
            out = term if out is None else out + term
        return out

    def shifted(self, field, axis, step):
        size = self.shape[axis]
        index = self.row if axis == 0 else self.lane
        moved = pltpu.roll(field, step % size, field.ndim - 2 + axis)
        if axis == 0:
            other = jnp.concatenate([moved[:, 1:], moved[:, :1]], axis=1)
        else:
            other = jnp.concatenate([moved[:, :, 1:], moved[:, :, :1]], axis=2)
        edge = 0 if step == 1 else size - 1
        return jnp.where(index == edge, other, moved)

    def tendency(self, field, kappa):
        flux_x = kappa * self.weight_x * self.apply("d", 1, field)
        flux_y = kappa * self.weight_y * self.apply("d", 0, field)
        r = -self.weight_y * self.apply("t", 1, flux_x) - self.weight_x * self.apply("t", 0, flux_y)
        r = (
            r
            + self.first_x * self.shifted(r, 1, 1)
            + self.last_x * self.shifted(r, 1, -1)
        )
        r = (
            r
            + self.first_y * self.shifted(r, 0, 1)
            + self.last_y * self.shifted(r, 0, -1)
        )
        return r * self.inv_mass


def split(value, pieces):
    out = []
    for _ in range(pieces):
        high = value.astype(jnp.bfloat16)
        out.append(high)
        value = value - high.astype(jnp.float32)
    return out


def fetch_kernel(*refs):
    air, diffusivity, absorber, thickness, zenith, lit, coef, weight = refs[:8]
    amount, state, absorber_out, thickness_out, zenith_out, lit_out, coef_out, weight_out, sems = refs[8:]
    levels = air.shape[0]
    copies = [
        pltpu.make_async_copy(absorber, absorber_out, sems.at[0]),
        pltpu.make_async_copy(air, state.at[pl.ds(0, levels)], sems.at[1]),
        pltpu.make_async_copy(diffusivity, state.at[levels], sems.at[2]),
        pltpu.make_async_copy(zenith, zenith_out, sems.at[3]),
        pltpu.make_async_copy(coef, coef_out, sems.at[4]),
        pltpu.make_async_copy(weight, weight_out, sems.at[5]),
        pltpu.make_async_copy(thickness, thickness_out, sems.at[6]),
        pltpu.make_async_copy(lit, lit_out, sems.at[7]),
    ]
    for copy in copies:
        copy.start()
    for copy in copies:
        copy.wait()
    for s in range(absorber_out.shape[0]):
        total = absorber_out[s, 0]
        for k in range(1, levels):
            total = total + absorber_out[s, k]
        amount[s] = total


def amount_rows(totals, scale, depth, ones):
    value = jnp.concatenate([t * scale for t in totals], axis=0)
    hi, mid, lo = (p.astype(jnp.float32) for p in split(value, 3))
    rest = depth - 4 * value.shape[0]
    index = lax.broadcasted_iota(jnp.int32, (rest, value.shape[1]), 0)
    tail = jnp.where(index < ones, 1.0, 0.0)
    return jnp.concatenate([hi, mid, lo, hi, tail], axis=0).astype(jnp.bfloat16)


def layers_kernel(absorber, zenith, coef, weight, left, drops, spread):
    species, levels, rows, width = absorber.shape
    terms = coef.shape[1]
    group = species * rows
    depth = left.shape[1]
    c_pieces = split(coef[...], 2)
    w_pieces = split(jnp.log2(weight[...]), 3)
    lane = lax.broadcasted_iota(jnp.int32, (rows, depth), 1)
    row = lax.broadcasted_iota(jnp.int32, (rows, depth), 0)
    ones_at = 4 * group
    stack = jnp.concatenate([p.astype(jnp.float32) for p in c_pieces + w_pieces], axis=0)
    count = stack.shape[0]
    pick_row = lax.broadcasted_iota(jnp.int32, (count, depth), 0)
    pick_lane = lax.broadcasted_iota(jnp.int32, (count, depth), 1)
    kind = pick_lane // group
    wanted = jnp.where(kind == 3, species, 0) + (pick_lane % group) // rows
    wanted = jnp.where(kind >= 4, 2 * species + pick_lane - ones_at, wanted)
    pick = (pick_row == wanted).astype(jnp.bfloat16)
    spread[...] = lax.dot_general(
        stack.astype(jnp.bfloat16),
        pick,
        (((0,), (0,)), ((), ())),
        preferred_element_type=jnp.float32,
    )
    mask = ((lane % rows == row) | (lane >= ones_at)).astype(jnp.float32)
    for g in range(0, terms, 2):
        pair = [jnp.broadcast_to(spread[pl.ds(g + i, 1), :], (rows, depth)) * mask for i in (0, 1)]
        left[pl.ds(g * rows, 2 * rows), :] = jnp.concatenate(pair, axis=0).astype(jnp.bfloat16)

    scale = -log2e / zenith[...]
    totals = [jnp.zeros((rows, width), jnp.float32)] * species
    blocks = []
    for k in range(levels + 1):
        if k:
            totals = [totals[s] + absorber[s, k - 1] for s in range(species)]
        blocks.append(amount_rows(totals, scale, depth, 3))
    right = jnp.concatenate(blocks, axis=1)
    chunk = 448
    for start in range(0, terms * rows, chunk):
        out = jnp.exp2(
            jnp.dot(left[pl.ds(start, chunk), :], right, preferred_element_type=jnp.float32)
        )
        for k in range(levels):
            drop = out[:, k * width : (k + 1) * width] - out[:, (k + 1) * width : (k + 2) * width]
            drops[k, pl.ds(start, chunk), :] = drop


def radiate_kernel(left, drops, upper, zenith, lit, thickness, heat):
    levels, rows, width = heat.shape
    depth = left.shape[1]
    species = upper.shape[0]
    zen = zenith[...]
    below = lax.axis_index("lev") > 0
    totals = [jnp.where(below, upper[s], 0.0) for s in range(species)]
    right = amount_rows(totals, -log2e / zen, depth, 0)
    chunk = 448
    sums = [jnp.zeros((rows, width), jnp.float32) for _ in range(levels)]
    for start in range(0, left.shape[0], chunk):
        above = jnp.exp2(
            jnp.dot(left[pl.ds(start, chunk), :], right, preferred_element_type=jnp.float32)
        )
        for k in range(levels):
            absorbed = above * drops[k, pl.ds(start, chunk), :]
            sums[k] = sums[k] + jnp.sum(absorbed.reshape(chunk // rows, rows, width), axis=0)
    lit_zenith = jnp.where(lit[...] == 1, zen, 0.0)
    for k in range(levels):
        heat[k] = lit_zenith * sums[k] / thickness[k]


def strips(levels):
    return [(i, tile) for i in range(2 * levels + 1) for tile in range(2)]


def pack_kernel(own_state, own_heat, other_state, other_heat, even_first, odd_first):
    levels = own_heat.shape[0]
    rows, width = own_heat.shape[1:]
    edge = 2 * points
    slots = width // edge
    lane = lax.broadcasted_iota(jnp.int32, (rows, width), 1)
    tiles = [(jnp.zeros((rows, width), jnp.float32), jnp.zeros((rows, width), jnp.float32)) for _ in range(own_first_tiles(levels, slots))]
    for j, (i, tile) in enumerate(strips(levels)):
        state, heat = (own_state, own_heat) if tile == 0 else (other_state, other_heat)
        value = state[i] if i <= levels else heat[i - levels - 1]
        n, slot = divmod(j, slots)
        here = lane // edge == slot
        low = pltpu.roll(value, (slot * edge) % width, 1)
        high = pltpu.roll(value, (slot * edge + edge) % width, 1)
        tiles[n] = (jnp.where(here, low, tiles[n][0]), jnp.where(here, high, tiles[n][1]))
    even = lax.axis_index("wide") % 2 == 0
    for n, (low, high) in enumerate(tiles):
        odd_first[n] = jnp.where(even, low, high)
        even_first[n] = jnp.where(even, high, low)


def own_first_tiles(levels, slots):
    return -(-(2 * (2 * levels + 1)) // slots)


def step_kernel(own_state, own_heat, other_state, other_heat, got_two, got_one, heat_out, out):
    levels = own_heat.shape[0]
    rows, width = own_heat.shape[1:]
    edge = 2 * points
    slots = width // edge
    stencil = Stencil(rows, width)
    even = lax.axis_index("wide") % 2 == 0
    lane = stencil.lane
    halo = {}
    for j, (i, tile) in enumerate(strips(levels)):
        n, slot = divmod(j, slots)
        from_left = jnp.where(even, got_one[n], got_two[n])
        from_right = jnp.where(even, got_two[n], got_one[n])
        after = pltpu.roll(from_right, (-slot * edge) % width, 1)
        before = pltpu.roll(from_left, (-slot * edge - edge) % width, 1)
        value = jnp.where(lane < edge, after, jnp.where(lane >= width - edge, before, 0.0))
        halo[i, tile] = value

    def ring(i):
        parts = []
        for tile in range(2):
            state, heat = (own_state, own_heat) if tile == 0 else (other_state, other_heat)
            main = state[i] if i <= levels else heat[i - levels - 1]
            parts.append(jnp.stack([main, halo[i, tile]], axis=0))
        return jnp.stack(parts, axis=0)

    air = jnp.stack([ring(i) for i in range(levels)], axis=0)
    kappa = ring(levels)[None]
    heat = jnp.stack([ring(levels + 1 + i) for i in range(levels)], axis=0)
    first = air + time_step * (stencil.tendency(air, kappa) + heat)
    new = 0.5 * (air + first + time_step * (stencil.tendency(first, kappa) + heat))
    for k in range(levels):
        out[k] = new[k, 0, 0]
        heat_out[k] = own_heat[k]


def swap(value, axis, pairs):
    route = [(a, b) for a, b in pairs] + [(b, a) for a, b in pairs]
    return lax.ppermute(value, axis, route)


def shards(
    air_state, diffusivity, absorber, thickness, cos_zenith, sunlit, absorb_coef, solar_weight
):
    levels, rows, width = air_state.shape
    terms = absorb_coef.shape[1]
    tile = lambda n: jax.ShapeDtypeStruct((n, rows, width), jnp.float32)
    big = pltpu.CompilerParams(vmem_limit_bytes=32 * 1024 * 1024)
    weight = solar_weight[None]
    args = (air_state, diffusivity, absorber, thickness, cos_zenith, sunlit, absorb_coef, weight)
    same = lambda x: jax.ShapeDtypeStruct(x.shape, x.dtype)
    amount, own_state, absorber, thickness, cos_zenith, sunlit, absorb_coef, weight = pl.pallas_call(
        fetch_kernel,
        out_shape=(tile(absorber.shape[0]), tile(levels + 1)) + tuple(same(x) for x in args[2:]),
        in_specs=[pl.BlockSpec(memory_space=pltpu.HBM)] * len(args),
        scratch_shapes=[pltpu.SemaphoreType.DMA((len(args),))],
        compiler_params=pltpu.CompilerParams(vmem_limit_bytes=32 * 1024 * 1024),
        name="fetch",
    )(*args)
    size = lax.axis_size("lev")
    lev = lax.axis_index("lev")
    upper = None
    for step in range(1, size):
        moved = lax.ppermute(amount, "lev", [(i, (i + step) % size) for i in range(size)])
        if size > 2:
            moved = jnp.where(lev >= step, moved, 0.0)
        upper = moved if upper is None else upper + moved
    if upper is None:
        upper = jnp.zeros_like(amount)
    other_state = swap(own_state, "sub", [(0, 1)])
    left, drops = pl.pallas_call(
        layers_kernel,
        out_shape=(
            jax.ShapeDtypeStruct((terms * rows, 256), jnp.bfloat16),
            jax.ShapeDtypeStruct((levels, terms * rows, width), jnp.float32),
        ),
        scratch_shapes=[pltpu.VMEM((terms, 256), jnp.float32)],
        compiler_params=big,
        name="layers",
    )(absorber, cos_zenith, absorb_coef, weight)
    own_heat = pl.pallas_call(
        radiate_kernel, out_shape=tile(levels), compiler_params=big, name="radiate"
    )(left, drops, upper, cos_zenith, sunlit, thickness)
    other_heat = swap(own_heat, "sub", [(0, 1)])
    tiles = own_first_tiles(levels, width // (2 * points))
    even_first, odd_first = pl.pallas_call(
        pack_kernel, out_shape=(tile(tiles), tile(tiles)), compiler_params=big, name="pack"
    )(own_state, own_heat, other_state, other_heat)
    wide = lax.axis_size("wide")
    got_two = swap(even_first, "wide", [(i, i + 1) for i in range(0, wide, 2)])
    got_one = swap(odd_first, "wide", [(i, (i + 1) % wide) for i in range(1, wide, 2)])
    heat, new_state = pl.pallas_call(
        step_kernel, out_shape=(tile(levels), tile(levels)), compiler_params=big, name="step"
    )(own_state, own_heat, other_state, other_heat, got_two, got_one)
    return (heat, new_state)


def solution(mesh):
    in_specs = (
        P("lev", ("grp", "sub"), "wide"),
        P(("grp", "sub"), "wide"),
        P(None, "lev", ("grp", "sub"), "wide"),
        P("lev", ("grp", "sub"), "wide"),
        P(("grp", "sub"), "wide"),
        P(("grp", "sub"), "wide"),
        P(),
        P(),
    )
    out_specs = (P("lev", ("grp", "sub"), "wide"), P("lev", ("grp", "sub"), "wide"))
    return jax.shard_map(shards, mesh=mesh, in_specs=in_specs, out_specs=out_specs, check_vma=False)
```

```python
import math

import jax
import jax.numpy as jnp
import numpy as np
from jax import lax
from jax.experimental import pallas as pl
from jax.experimental.pallas import tpu as pltpu
from jax.sharding import PartitionSpec as P

time_step = 0.004
points = 4
log2e = 1.4426950408889634
gll_weights = (1.0 / 6.0, 5.0 / 6.0, 5.0 / 6.0, 1.0 / 6.0)
mass_points = (1.0 / 3.0, 5.0 / 6.0, 5.0 / 6.0, 1.0 / 3.0)


def derivative_table():
    root_five = math.sqrt(5.0)
    outer_big = (5.0 + 5.0 * root_five) / 4.0
    outer_small = (5.0 * root_five - 5.0) / 4.0
    inner_big = (1.0 + root_five) / 4.0
    inner_mid = root_five / 2.0
    inner_small = (root_five - 1.0) / 4.0
    return np.array(
        [
            [-3.0, outer_big, -outer_small, 0.5],
            [-inner_big, 0.0, inner_mid, -inner_small],
            [inner_small, -inner_mid, 0.0, inner_big],
            [-0.5, outer_small, -outer_big, 3.0],
        ]
    )


table = derivative_table()


def by_node(node, values):
    out = jnp.full(node.shape, values[3], jnp.float32)
    for i in (2, 1, 0):
        out = jnp.where(node == i, jnp.float32(values[i]), out)
    return out


class Stencil:
    def __init__(self, rows, width):
        self.shape = (rows, width)
        self.row = lax.broadcasted_iota(jnp.int32, (rows, width), 0)
        self.lane = lax.broadcasted_iota(jnp.int32, (rows, width), 1)
        node_y, node_x = self.row % points, self.lane % points
        self.weight_x = by_node(node_x, gll_weights)
        self.weight_y = by_node(node_y, gll_weights)
        self.coefs = {}
        for name, matrix in (("d", table), ("t", table.T)):
            for axis, node in ((0, node_y), (1, node_x)):
                terms = []
                for step in range(-3, 4):
                    values = [
                        matrix[i, i + step] if 0 <= i + step < points else 0.0
                        for i in range(points)
                    ]
                    terms.append(by_node(node, values))
                self.coefs[name, axis] = terms
        self.inv_mass = by_node(node_y, [1.0 / m for m in mass_points]) * by_node(
            node_x, [1.0 / m for m in mass_points]
        )
        self.first_x = (node_x == 0).astype(jnp.float32)
        self.last_x = (node_x == points - 1).astype(jnp.float32)
        self.first_y = (node_y == 0).astype(jnp.float32)
        self.last_y = (node_y == points - 1).astype(jnp.float32)

    def apply(self, name, axis, field):
        size = self.shape[axis]
        out = None
        for step, coef in zip(range(-3, 4), self.coefs[name, axis]):
            if step == 0 and name == "d":
                moved = field
            else:
                moved = pltpu.roll(field, (-step) % size, field.ndim - 2 + axis)
            term = coef * moved
            out = term if out is None else out + term
        return out

    def shifted(self, field, axis, step):
        size = self.shape[axis]
        index = self.row if axis == 0 else self.lane
        moved = pltpu.roll(field, step % size, field.ndim - 2 + axis)
        if axis == 0:
            other = jnp.concatenate([moved[:, 1:], moved[:, :1]], axis=1)
        else:
            other = jnp.concatenate([moved[:, :, 1:], moved[:, :, :1]], axis=2)
        edge = 0 if step == 1 else size - 1
        return jnp.where(index == edge, other, moved)

    def tendency(self, field, kappa):
        flux_x = kappa * self.weight_x * self.apply("d", 1, field)
        flux_y = kappa * self.weight_y * self.apply("d", 0, field)
        r = -self.weight_y * self.apply("t", 1, flux_x) - self.weight_x * self.apply("t", 0, flux_y)
        r = (
            r
            + self.first_x * self.shifted(r, 1, 1)
            + self.last_x * self.shifted(r, 1, -1)
        )
        r = (
            r
            + self.first_y * self.shifted(r, 0, 1)
            + self.last_y * self.shifted(r, 0, -1)
        )
        return r * self.inv_mass


def split(value, pieces):
    out = []
    for _ in range(pieces):
        high = value.astype(jnp.bfloat16)
        out.append(high)
        value = value - high.astype(jnp.float32)
    return out


def fetch_kernel(*refs):
    air, diffusivity, absorber, thickness, zenith, lit, coef, weight = refs[:8]
    amount, state, absorber_out, thickness_out, zenith_out, lit_out, coef_out, weight_out, sems = refs[8:]
    levels = air.shape[0]
    copies = [
        pltpu.make_async_copy(absorber, absorber_out, sems.at[0]),
        pltpu.make_async_copy(air, state.at[pl.ds(0, levels)], sems.at[1]),
        pltpu.make_async_copy(diffusivity, state.at[levels], sems.at[2]),
        pltpu.make_async_copy(zenith, zenith_out, sems.at[3]),
        pltpu.make_async_copy(coef, coef_out, sems.at[4]),
        pltpu.make_async_copy(weight, weight_out, sems.at[5]),
        pltpu.make_async_copy(thickness, thickness_out, sems.at[6]),
        pltpu.make_async_copy(lit, lit_out, sems.at[7]),
    ]
    for copy in copies:
        copy.start()
    for copy in copies:
        copy.wait()
    for s in range(absorber_out.shape[0]):
        total = absorber_out[s, 0]
        for k in range(1, levels):
            total = total + absorber_out[s, k]
        amount[s] = total


def amount_rows(totals, scale, depth, ones):
    value = jnp.concatenate([t * scale for t in totals], axis=0)
    hi, mid, lo = (p.astype(jnp.float32) for p in split(value, 3))
    rest = depth - 4 * value.shape[0]
    index = lax.broadcasted_iota(jnp.int32, (rest, value.shape[1]), 0)
    tail = jnp.where(index < ones, 1.0, 0.0)
    return jnp.concatenate([hi, mid, lo, hi, tail], axis=0).astype(jnp.bfloat16)


def layers_kernel(absorber, zenith, coef, weight, left, drops, spread):
    species, levels, rows, width = absorber.shape
    terms = coef.shape[1]
    group = species * rows
    depth = left.shape[1]
    c_pieces = split(coef[...], 2)
    w_pieces = split(jnp.log2(weight[...]), 3)
    lane = lax.broadcasted_iota(jnp.int32, (rows, depth), 1)
    row = lax.broadcasted_iota(jnp.int32, (rows, depth), 0)
    ones_at = 4 * group
    stack = jnp.concatenate([p.astype(jnp.float32) for p in c_pieces + w_pieces], axis=0)
    count = stack.shape[0]
    pick_row = lax.broadcasted_iota(jnp.int32, (count, depth), 0)
    pick_lane = lax.broadcasted_iota(jnp.int32, (count, depth), 1)
    kind = pick_lane // group
    wanted = jnp.where(kind == 3, species, 0) + (pick_lane % group) // rows
    wanted = jnp.where(kind >= 4, 2 * species + pick_lane - ones_at, wanted)
    pick = (pick_row == wanted).astype(jnp.bfloat16)
    spread[...] = lax.dot_general(
        stack.astype(jnp.bfloat16),
        pick,
        (((0,), (0,)), ((), ())),
        preferred_element_type=jnp.float32,
    )
    mask = ((lane % rows == row) | (lane >= ones_at)).astype(jnp.float32)
    for g in range(0, terms, 2):
        pair = [jnp.broadcast_to(spread[pl.ds(g + i, 1), :], (rows, depth)) * mask for i in (0, 1)]
        left[pl.ds(g * rows, 2 * rows), :] = jnp.concatenate(pair, axis=0).astype(jnp.bfloat16)

    scale = -log2e / zenith[...]
    totals = [jnp.zeros((rows, width), jnp.float32)] * species
    blocks = []
    for k in range(levels + 1):
        if k:
            totals = [totals[s] + absorber[s, k - 1] for s in range(species)]
        blocks.append(amount_rows(totals, scale, depth, 3))
    right = jnp.concatenate(blocks, axis=1)
    chunk = 448
    for start in range(0, terms * rows, chunk):
        out = jnp.exp2(
            jnp.dot(left[pl.ds(start, chunk), :], right, preferred_element_type=jnp.float32)
        )
        for k in range(levels):
            drop = out[:, k * width : (k + 1) * width] - out[:, (k + 1) * width : (k + 2) * width]
            drops[k, pl.ds(start, chunk), :] = drop


def radiate_kernel(left, drops, upper, zenith, lit, thickness, heat):
    levels, rows, width = heat.shape
    depth = left.shape[1]
    species = upper.shape[0]
    zen = zenith[...]
    below = lax.axis_index("lev") > 0
    totals = [jnp.where(below, upper[s], 0.0) for s in range(species)]
    right = amount_rows(totals, -log2e / zen, depth, 0)
    chunk = 448
    sums = [jnp.zeros((rows, width), jnp.float32) for _ in range(levels)]
    for start in range(0, left.shape[0], chunk):
        above = jnp.exp2(
            jnp.dot(left[pl.ds(start, chunk), :], right, preferred_element_type=jnp.float32)
        )
        for k in range(levels):
            absorbed = above * drops[k, pl.ds(start, chunk), :]
            sums[k] = sums[k] + jnp.sum(absorbed.reshape(chunk // rows, rows, width), axis=0)
    lit_zenith = jnp.where(lit[...] == 1, zen, 0.0)
    for k in range(levels):
        heat[k] = lit_zenith * sums[k] / thickness[k]


def strips(levels):
    return [(i, tile) for i in range(2 * levels + 1) for tile in range(2)]


def pack_kernel(own_state, own_heat, other_state, other_heat, even_first, odd_first):
    levels = own_heat.shape[0]
    rows, width = own_heat.shape[1:]
    edge = 2 * points
    slots = width // edge
    lane = lax.broadcasted_iota(jnp.int32, (rows, width), 1)
    tiles = [(jnp.zeros((rows, width), jnp.float32), jnp.zeros((rows, width), jnp.float32)) for _ in range(own_first_tiles(levels, slots))]
    for j, (i, tile) in enumerate(strips(levels)):
        state, heat = (own_state, own_heat) if tile == 0 else (other_state, other_heat)
        value = state[i] if i <= levels else heat[i - levels - 1]
        n, slot = divmod(j, slots)
        here = lane // edge == slot
        low = pltpu.roll(value, (slot * edge) % width, 1)
        high = pltpu.roll(value, (slot * edge + edge) % width, 1)
        tiles[n] = (jnp.where(here, low, tiles[n][0]), jnp.where(here, high, tiles[n][1]))
    even = lax.axis_index("wide") % 2 == 0
    for n, (low, high) in enumerate(tiles):
        odd_first[n] = jnp.where(even, low, high)
        even_first[n] = jnp.where(even, high, low)


def own_first_tiles(levels, slots):
    return -(-(2 * (2 * levels + 1)) // slots)


def step_kernel(own_state, own_heat, other_state, other_heat, got_two, got_one, heat_out, out):
    levels = own_heat.shape[0]
    rows, width = own_heat.shape[1:]
    edge = 2 * points
    slots = width // edge
    stencil = Stencil(rows, width)
    even = lax.axis_index("wide") % 2 == 0
    lane = stencil.lane
    halo = {}
    for j, (i, tile) in enumerate(strips(levels)):
        n, slot = divmod(j, slots)
        from_left = jnp.where(even, got_one[n], got_two[n])
        from_right = jnp.where(even, got_two[n], got_one[n])
        after = pltpu.roll(from_right, (-slot * edge) % width, 1)
        before = pltpu.roll(from_left, (-slot * edge - edge) % width, 1)
        value = jnp.where(lane < edge, after, jnp.where(lane >= width - edge, before, 0.0))
        halo[i, tile] = value

    def ring(i):
        parts = []
        for tile in range(2):
            state, heat = (own_state, own_heat) if tile == 0 else (other_state, other_heat)
            main = state[i] if i <= levels else heat[i - levels - 1]
            parts.append(jnp.stack([main, halo[i, tile]], axis=0))
        return jnp.stack(parts, axis=0)

    air = jnp.stack([ring(i) for i in range(levels)], axis=0)
    kappa = ring(levels)[None]
    heat = jnp.stack([ring(levels + 1 + i) for i in range(levels)], axis=0)
    first = air + time_step * (stencil.tendency(air, kappa) + heat)
    new = 0.5 * (air + first + time_step * (stencil.tendency(first, kappa) + heat))
    for k in range(levels):
        out[k] = new[k, 0, 0]
        heat_out[k] = own_heat[k]


def swap(value, axis, pairs):
    route = [(a, b) for a, b in pairs] + [(b, a) for a, b in pairs]
    return lax.ppermute(value, axis, route)


def shards(
    air_state, diffusivity, absorber, thickness, cos_zenith, sunlit, absorb_coef, solar_weight
):
    levels, rows, width = air_state.shape
    terms = absorb_coef.shape[1]
    tile = lambda n: jax.ShapeDtypeStruct((n, rows, width), jnp.float32)
    big = pltpu.CompilerParams(vmem_limit_bytes=32 * 1024 * 1024)
    weight = solar_weight[None]
    args = (air_state, diffusivity, absorber, thickness, cos_zenith, sunlit, absorb_coef, weight)
    args = tuple(pltpu.with_memory_space_constraint(x, pltpu.HBM) for x in args)
    same = lambda x: jax.ShapeDtypeStruct(x.shape, x.dtype)
    amount, own_state, absorber, thickness, cos_zenith, sunlit, absorb_coef, weight = pl.pallas_call(
        fetch_kernel,
        out_shape=(tile(absorber.shape[0]), tile(levels + 1)) + tuple(same(x) for x in args[2:]),
        in_specs=[pl.BlockSpec(memory_space=pltpu.HBM)] * len(args),
        scratch_shapes=[pltpu.SemaphoreType.DMA((len(args),))],
        compiler_params=pltpu.CompilerParams(vmem_limit_bytes=32 * 1024 * 1024),
        name="fetch",
    )(*args)
    size = lax.axis_size("lev")
    lev = lax.axis_index("lev")
    upper = None
    for step in range(1, size):
        moved = lax.ppermute(amount, "lev", [(i, (i + step) % size) for i in range(size)])
        if size > 2:
            moved = jnp.where(lev >= step, moved, 0.0)
        upper = moved if upper is None else upper + moved
    if upper is None:
        upper = jnp.zeros_like(amount)
    other_state = swap(own_state, "sub", [(0, 1)])
    left, drops = pl.pallas_call(
        layers_kernel,
        out_shape=(
            jax.ShapeDtypeStruct((terms * rows, 256), jnp.bfloat16),
            jax.ShapeDtypeStruct((levels, terms * rows, width), jnp.float32),
        ),
        scratch_shapes=[pltpu.VMEM((terms, 256), jnp.float32)],
        compiler_params=big,
        name="layers",
    )(absorber, cos_zenith, absorb_coef, weight)
    own_heat = pl.pallas_call(
        radiate_kernel, out_shape=tile(levels), compiler_params=big, name="radiate"
    )(left, drops, upper, cos_zenith, sunlit, thickness)
    other_heat = swap(own_heat, "sub", [(0, 1)])
    tiles = own_first_tiles(levels, width // (2 * points))
    even_first, odd_first = pl.pallas_call(
        pack_kernel, out_shape=(tile(tiles), tile(tiles)), compiler_params=big, name="pack"
    )(own_state, own_heat, other_state, other_heat)
    wide = lax.axis_size("wide")
    got_two = swap(even_first, "wide", [(i, i + 1) for i in range(0, wide, 2)])
    got_one = swap(odd_first, "wide", [(i, (i + 1) % wide) for i in range(1, wide, 2)])
    heat, new_state = pl.pallas_call(
        step_kernel, out_shape=(tile(levels), tile(levels)), compiler_params=big, name="step"
    )(own_state, own_heat, other_state, other_heat, got_two, got_one)
    return (heat, new_state)


def solution(mesh):
    in_specs = (
        P("lev", ("grp", "sub"), "wide"),
        P(("grp", "sub"), "wide"),
        P(None, "lev", ("grp", "sub"), "wide"),
        P("lev", ("grp", "sub"), "wide"),
        P(("grp", "sub"), "wide"),
        P(("grp", "sub"), "wide"),
        P(),
        P(),
    )
    out_specs = (P("lev", ("grp", "sub"), "wide"), P("lev", ("grp", "sub"), "wide"))
    return jax.shard_map(shards, mesh=mesh, in_specs=in_specs, out_specs=out_specs, check_vma=False)
```

```python
import math

import jax
import jax.numpy as jnp
import numpy as np
from jax import lax
from jax.experimental import pallas as pl
from jax.experimental.pallas import tpu as pltpu
from jax.sharding import PartitionSpec as P

time_step = 0.004
points = 4
log2e = 1.4426950408889634
gll_weights = (1.0 / 6.0, 5.0 / 6.0, 5.0 / 6.0, 1.0 / 6.0)
mass_points = (1.0 / 3.0, 5.0 / 6.0, 5.0 / 6.0, 1.0 / 3.0)


def derivative_table():
    root_five = math.sqrt(5.0)
    outer_big = (5.0 + 5.0 * root_five) / 4.0
    outer_small = (5.0 * root_five - 5.0) / 4.0
    inner_big = (1.0 + root_five) / 4.0
    inner_mid = root_five / 2.0
    inner_small = (root_five - 1.0) / 4.0
    return np.array(
        [
            [-3.0, outer_big, -outer_small, 0.5],
            [-inner_big, 0.0, inner_mid, -inner_small],
            [inner_small, -inner_mid, 0.0, inner_big],
            [-0.5, outer_small, -outer_big, 3.0],
        ]
    )


table = derivative_table()


def by_node(node, values):
    out = jnp.full(node.shape, values[3], jnp.float32)
    for i in (2, 1, 0):
        out = jnp.where(node == i, jnp.float32(values[i]), out)
    return out


class Stencil:
    def __init__(self, rows, width):
        self.shape = (rows, width)
        self.row = lax.broadcasted_iota(jnp.int32, (rows, width), 0)
        self.lane = lax.broadcasted_iota(jnp.int32, (rows, width), 1)
        node_y, node_x = self.row % points, self.lane % points
        self.weight_x = by_node(node_x, gll_weights)
        self.weight_y = by_node(node_y, gll_weights)
        self.coefs = {}
        for name, matrix in (("d", table), ("t", table.T)):
            for axis, node in ((0, node_y), (1, node_x)):
                terms = []
                for step in range(-3, 4):
                    values = [
                        matrix[i, i + step] if 0 <= i + step < points else 0.0
                        for i in range(points)
                    ]
                    terms.append(by_node(node, values))
                self.coefs[name, axis] = terms
        self.inv_mass = by_node(node_y, [1.0 / m for m in mass_points]) * by_node(
            node_x, [1.0 / m for m in mass_points]
        )
        self.first_x = (node_x == 0).astype(jnp.float32)
        self.last_x = (node_x == points - 1).astype(jnp.float32)
        self.first_y = (node_y == 0).astype(jnp.float32)
        self.last_y = (node_y == points - 1).astype(jnp.float32)

    def apply(self, name, axis, field):
        size = self.shape[axis]
        out = None
        for step, coef in zip(range(-3, 4), self.coefs[name, axis]):
            if step == 0 and name == "d":
                moved = field
            else:
                moved = pltpu.roll(field, (-step) % size, field.ndim - 2 + axis)
            term = coef * moved
            out = term if out is None else out + term
        return out

    def shifted(self, field, axis, step):
        size = self.shape[axis]
        index = self.row if axis == 0 else self.lane
        moved = pltpu.roll(field, step % size, field.ndim - 2 + axis)
        if axis == 0:
            other = jnp.concatenate([moved[:, 1:], moved[:, :1]], axis=1)
        else:
            other = jnp.concatenate([moved[:, :, 1:], moved[:, :, :1]], axis=2)
        edge = 0 if step == 1 else size - 1
        return jnp.where(index == edge, other, moved)

    def tendency(self, field, kappa):
        flux_x = kappa * self.weight_x * self.apply("d", 1, field)
        flux_y = kappa * self.weight_y * self.apply("d", 0, field)
        r = -self.weight_y * self.apply("t", 1, flux_x) - self.weight_x * self.apply("t", 0, flux_y)
        r = (
            r
            + self.first_x * self.shifted(r, 1, 1)
            + self.last_x * self.shifted(r, 1, -1)
        )
        r = (
            r
            + self.first_y * self.shifted(r, 0, 1)
            + self.last_y * self.shifted(r, 0, -1)
        )
        return r * self.inv_mass


def split(value, pieces):
    out = []
    for _ in range(pieces):
        high = value.astype(jnp.bfloat16)
        out.append(high)
        value = value - high.astype(jnp.float32)
    return out


def fetch_kernel(*refs):
    air, diffusivity, absorber, thickness, zenith, lit, coef, weight = refs[:8]
    amount, state, absorber_out, thickness_out, zenith_out, lit_out, coef_out, weight_out, sems = refs[8:]
    levels = air.shape[0]
    copies = [
        pltpu.make_async_copy(absorber, absorber_out, sems.at[0]),
        pltpu.make_async_copy(air, state.at[pl.ds(0, levels)], sems.at[1]),
        pltpu.make_async_copy(diffusivity, state.at[levels], sems.at[2]),
        pltpu.make_async_copy(zenith, zenith_out, sems.at[3]),
        pltpu.make_async_copy(coef, coef_out, sems.at[4]),
        pltpu.make_async_copy(weight, weight_out, sems.at[5]),
        pltpu.make_async_copy(thickness, thickness_out, sems.at[6]),
        pltpu.make_async_copy(lit, lit_out, sems.at[7]),
    ]
    for copy in copies:
        copy.start()
    for copy in copies:
        copy.wait()
    for s in range(absorber_out.shape[0]):
        total = absorber_out[s, 0]
        for k in range(1, levels):
            total = total + absorber_out[s, k]
        amount[s] = total


def amount_rows(totals, scale, depth, ones):
    value = jnp.concatenate([t * scale for t in totals], axis=0)
    hi, mid, lo = (p.astype(jnp.float32) for p in split(value, 3))
    rest = depth - 4 * value.shape[0]
    index = lax.broadcasted_iota(jnp.int32, (rest, value.shape[1]), 0)
    tail = jnp.where(index < ones, 1.0, 0.0)
    return jnp.concatenate([hi, mid, lo, hi, tail], axis=0).astype(jnp.bfloat16)


def layers_kernel(absorber, zenith, coef, weight, left, drops, spread):
    species, levels, rows, width = absorber.shape
    terms = coef.shape[1]
    group = species * rows
    depth = left.shape[1]
    c_pieces = split(coef[...], 2)
    w_pieces = split(jnp.log2(weight[...]), 3)
    lane = lax.broadcasted_iota(jnp.int32, (rows, depth), 1)
    row = lax.broadcasted_iota(jnp.int32, (rows, depth), 0)
    ones_at = 4 * group
    stack = jnp.concatenate([p.astype(jnp.float32) for p in c_pieces + w_pieces], axis=0)
    count = stack.shape[0]
    pick_row = lax.broadcasted_iota(jnp.int32, (count, depth), 0)
    pick_lane = lax.broadcasted_iota(jnp.int32, (count, depth), 1)
    kind = pick_lane // group
    wanted = jnp.where(kind == 3, species, 0) + (pick_lane % group) // rows
    wanted = jnp.where(kind >= 4, 2 * species + pick_lane - ones_at, wanted)
    pick = (pick_row == wanted).astype(jnp.bfloat16)
    spread[...] = lax.dot_general(
        stack.astype(jnp.bfloat16),
        pick,
        (((0,), (0,)), ((), ())),
        preferred_element_type=jnp.float32,
    )
    mask = ((lane % rows == row) | (lane >= ones_at)).astype(jnp.float32)
    for g in range(0, terms, 2):
        pair = [jnp.broadcast_to(spread[pl.ds(g + i, 1), :], (rows, depth)) * mask for i in (0, 1)]
        left[pl.ds(g * rows, 2 * rows), :] = jnp.concatenate(pair, axis=0).astype(jnp.bfloat16)

    scale = -log2e / zenith[...]
    totals = [jnp.zeros((rows, width), jnp.float32)] * species
    blocks = []
    for k in range(levels + 1):
        if k:
            totals = [totals[s] + absorber[s, k - 1] for s in range(species)]
        blocks.append(amount_rows(totals, scale, depth, 3))
    right = jnp.concatenate(blocks, axis=1)
    chunk = 448
    for start in range(0, terms * rows, chunk):
        out = jnp.exp2(
            jnp.dot(left[pl.ds(start, chunk), :], right, preferred_element_type=jnp.float32)
        )
        for k in range(levels):
            drop = out[:, k * width : (k + 1) * width] - out[:, (k + 1) * width : (k + 2) * width]
            drops[k, pl.ds(start, chunk), :] = drop


def radiate_kernel(left, drops, upper, zenith, lit, thickness, heat):
    levels, rows, width = heat.shape
    depth = left.shape[1]
    species = upper.shape[0]
    zen = zenith[...]
    below = lax.axis_index("lev") > 0
    totals = [jnp.where(below, upper[s], 0.0) for s in range(species)]
    right = amount_rows(totals, -log2e / zen, depth, 0)
    chunk = 448
    sums = [jnp.zeros((rows, width), jnp.float32) for _ in range(levels)]
    for start in range(0, left.shape[0], chunk):
        above = jnp.exp2(
            jnp.dot(left[pl.ds(start, chunk), :], right, preferred_element_type=jnp.float32)
        )
        for k in range(levels):
            absorbed = above * drops[k, pl.ds(start, chunk), :]
            sums[k] = sums[k] + jnp.sum(absorbed.reshape(chunk // rows, rows, width), axis=0)
    lit_zenith = jnp.where(lit[...] == 1, zen, 0.0)
    for k in range(levels):
        heat[k] = lit_zenith * sums[k] / thickness[k]


def strips(levels):
    return [(i, tile) for i in range(2 * levels + 1) for tile in range(2)]


def pack_kernel(own_state, own_heat, other_state, other_heat, packed):
    levels = own_heat.shape[0]
    rows, width = own_heat.shape[1:]
    edge = 2 * points
    slots = width // edge
    lane = lax.broadcasted_iota(jnp.int32, (rows, width), 1)
    tiles = [(jnp.zeros((rows, width), jnp.float32), jnp.zeros((rows, width), jnp.float32)) for _ in range(own_first_tiles(levels, slots))]
    for j, (i, tile) in enumerate(strips(levels)):
        state, heat = (own_state, own_heat) if tile == 0 else (other_state, other_heat)
        value = state[i] if i <= levels else heat[i - levels - 1]
        n, slot = divmod(j, slots)
        here = lane // edge == slot
        low = pltpu.roll(value, (slot * edge) % width, 1)
        high = pltpu.roll(value, (slot * edge + edge) % width, 1)
        tiles[n] = (jnp.where(here, low, tiles[n][0]), jnp.where(here, high, tiles[n][1]))
    wide = packed.shape[0]
    me = lax.axis_index("wide")
    packed[...] = jnp.zeros(packed.shape, jnp.float32)
    before, after = lax.rem(me + wide - 1, wide), lax.rem(me + 1, wide)
    for n, (low, high) in enumerate(tiles):
        packed[before, n] = low
        packed[after, n] = high


def own_first_tiles(levels, slots):
    return -(-(2 * (2 * levels + 1)) // slots)


def step_kernel(own_state, own_heat, other_state, other_heat, got, heat_out, out):
    levels = own_heat.shape[0]
    rows, width = own_heat.shape[1:]
    edge = 2 * points
    slots = width // edge
    stencil = Stencil(rows, width)
    wide = got.shape[0]
    me = lax.axis_index("wide")
    left_mate, right_mate = lax.rem(me + wide - 1, wide), lax.rem(me + 1, wide)
    lane = stencil.lane
    halo = {}
    for j, (i, tile) in enumerate(strips(levels)):
        n, slot = divmod(j, slots)
        from_left = got[left_mate, n]
        from_right = got[right_mate, n]
        after = pltpu.roll(from_right, (-slot * edge) % width, 1)
        before = pltpu.roll(from_left, (-slot * edge - edge) % width, 1)
        value = jnp.where(lane < edge, after, jnp.where(lane >= width - edge, before, 0.0))
        halo[i, tile] = value

    def ring(i):
        parts = []
        for tile in range(2):
            state, heat = (own_state, own_heat) if tile == 0 else (other_state, other_heat)
            main = state[i] if i <= levels else heat[i - levels - 1]
            parts.append(jnp.stack([main, halo[i, tile]], axis=0))
        return jnp.stack(parts, axis=0)

    air = jnp.stack([ring(i) for i in range(levels)], axis=0)
    kappa = ring(levels)[None]
    heat = jnp.stack([ring(levels + 1 + i) for i in range(levels)], axis=0)
    first = air + time_step * (stencil.tendency(air, kappa) + heat)
    new = 0.5 * (air + first + time_step * (stencil.tendency(first, kappa) + heat))
    for k in range(levels):
        out[k] = new[k, 0, 0]
        heat_out[k] = own_heat[k]


def swap(value, axis, pairs):
    route = [(a, b) for a, b in pairs] + [(b, a) for a, b in pairs]
    return lax.ppermute(value, axis, route)


def shards(
    air_state, diffusivity, absorber, thickness, cos_zenith, sunlit, absorb_coef, solar_weight
):
    levels, rows, width = air_state.shape
    terms = absorb_coef.shape[1]
    tile = lambda n: jax.ShapeDtypeStruct((n, rows, width), jnp.float32)
    big = pltpu.CompilerParams(vmem_limit_bytes=32 * 1024 * 1024)
    weight = solar_weight[None]
    args = (air_state, diffusivity, absorber, thickness, cos_zenith, sunlit, absorb_coef, weight)
    args = tuple(pltpu.with_memory_space_constraint(x, pltpu.HBM) for x in args)
    same = lambda x: jax.ShapeDtypeStruct(x.shape, x.dtype)
    amount, own_state, absorber, thickness, cos_zenith, sunlit, absorb_coef, weight = pl.pallas_call(
        fetch_kernel,
        out_shape=(tile(absorber.shape[0]), tile(levels + 1)) + tuple(same(x) for x in args[2:]),
        in_specs=[pl.BlockSpec(memory_space=pltpu.HBM)] * len(args),
        scratch_shapes=[pltpu.SemaphoreType.DMA((len(args),))],
        compiler_params=pltpu.CompilerParams(vmem_limit_bytes=32 * 1024 * 1024),
        name="fetch",
    )(*args)
    size = lax.axis_size("lev")
    lev = lax.axis_index("lev")
    upper = None
    for step in range(1, size):
        moved = lax.ppermute(amount, "lev", [(i, (i + step) % size) for i in range(size)])
        if size > 2:
            moved = jnp.where(lev >= step, moved, 0.0)
        upper = moved if upper is None else upper + moved
    if upper is None:
        upper = jnp.zeros_like(amount)
    other_state = swap(own_state, "sub", [(0, 1)])
    left, drops = pl.pallas_call(
        layers_kernel,
        out_shape=(
            jax.ShapeDtypeStruct((terms * rows, 256), jnp.bfloat16),
            jax.ShapeDtypeStruct((levels, terms * rows, width), jnp.float32),
        ),
        scratch_shapes=[pltpu.VMEM((terms, 256), jnp.float32)],
        compiler_params=big,
        name="layers",
    )(absorber, cos_zenith, absorb_coef, weight)
    own_heat = pl.pallas_call(
        radiate_kernel, out_shape=tile(levels), compiler_params=big, name="radiate"
    )(left, drops, upper, cos_zenith, sunlit, thickness)
    other_heat = swap(own_heat, "sub", [(0, 1)])
    tiles = own_first_tiles(levels, width // (2 * points))
    wide = lax.axis_size("wide")
    packed = pl.pallas_call(
        pack_kernel,
        out_shape=jax.ShapeDtypeStruct((wide, tiles, rows, width), jnp.float32),
        compiler_params=big,
        name="pack",
    )(own_state, own_heat, other_state, other_heat)
    got = lax.all_to_all(packed, "wide", 0, 0)
    heat, new_state = pl.pallas_call(
        step_kernel, out_shape=(tile(levels), tile(levels)), compiler_params=big, name="step"
    )(own_state, own_heat, other_state, other_heat, got)
    return (heat, new_state)


def solution(mesh):
    in_specs = (
        P("lev", ("grp", "sub"), "wide"),
        P(("grp", "sub"), "wide"),
        P(None, "lev", ("grp", "sub"), "wide"),
        P("lev", ("grp", "sub"), "wide"),
        P(("grp", "sub"), "wide"),
        P(("grp", "sub"), "wide"),
        P(),
        P(),
    )
    out_specs = (P("lev", ("grp", "sub"), "wide"), P("lev", ("grp", "sub"), "wide"))
    return jax.shard_map(shards, mesh=mesh, in_specs=in_specs, out_specs=out_specs, check_vma=False)
```

```python
import math

import jax
import jax.numpy as jnp
import numpy as np
from jax import lax
from jax.experimental import pallas as pl
from jax.experimental.pallas import tpu as pltpu
from jax.sharding import PartitionSpec as P

time_step = 0.004
points = 4
log2e = 1.4426950408889634
gll_weights = (1.0 / 6.0, 5.0 / 6.0, 5.0 / 6.0, 1.0 / 6.0)
mass_points = (1.0 / 3.0, 5.0 / 6.0, 5.0 / 6.0, 1.0 / 3.0)


def derivative_table():
    root_five = math.sqrt(5.0)
    outer_big = (5.0 + 5.0 * root_five) / 4.0
    outer_small = (5.0 * root_five - 5.0) / 4.0
    inner_big = (1.0 + root_five) / 4.0
    inner_mid = root_five / 2.0
    inner_small = (root_five - 1.0) / 4.0
    return np.array(
        [
            [-3.0, outer_big, -outer_small, 0.5],
            [-inner_big, 0.0, inner_mid, -inner_small],
            [inner_small, -inner_mid, 0.0, inner_big],
            [-0.5, outer_small, -outer_big, 3.0],
        ]
    )


table = derivative_table()


def by_node(node, values):
    out = jnp.full(node.shape, values[3], jnp.float32)
    for i in (2, 1, 0):
        out = jnp.where(node == i, jnp.float32(values[i]), out)
    return out


class Stencil:
    def __init__(self, rows, width):
        self.shape = (rows, width)
        self.row = lax.broadcasted_iota(jnp.int32, (rows, width), 0)
        self.lane = lax.broadcasted_iota(jnp.int32, (rows, width), 1)
        node_y, node_x = self.row % points, self.lane % points
        self.nodes = (node_y, node_x)
        self.weight_x = by_node(node_x, gll_weights)
        self.weight_y = by_node(node_y, gll_weights)
        self.inv_mass_y = by_node(node_y, [1.0 / m for m in mass_points])
        self.inv_mass = self.inv_mass_y * by_node(node_x, [1.0 / m for m in mass_points])
        inner_first = (node_x == 0) & (self.lane > 0)
        inner_last = (node_x == points - 1) & (self.lane < width - 1)
        self.first_x = inner_first.astype(jnp.float32)
        self.last_x = inner_last.astype(jnp.float32)
        self.first_y = (node_y == 0).astype(jnp.float32)
        self.last_y = (node_y == points - 1).astype(jnp.float32)
        self.coefs = {}

    def coef(self, name, axis):
        if (name, axis) not in self.coefs:
            matrix = table if name == "d" else table.T
            self.coefs[name, axis] = [
                by_node(
                    self.nodes[axis],
                    [matrix[i, i + step] if 0 <= i + step < points else 0.0 for i in range(points)],
                )
                for step in range(-3, 4)
            ]
        return self.coefs[name, axis]

    def apply(self, name, axis, field):
        size = self.shape[axis]
        out = None
        for step, coef in zip(range(-3, 4), self.coef(name, axis)):
            moved = field if step == 0 else pltpu.roll(field, (-step) % size, field.ndim - 2 + axis)
            term = coef * moved
            out = term if out is None else out + term
        return out

    def residual(self, field, kappa):
        flux_x = kappa * self.weight_x * self.apply("d", 1, field)
        flux_y = kappa * self.weight_y * self.apply("d", 0, field)
        part_x = self.weight_y * self.apply("t", 1, flux_x)
        return -part_x - self.weight_x * self.apply("t", 0, flux_y)

    def rows_joined(self, own, other):
        rows = self.shape[0]
        axis = own.ndim - 2
        before = jnp.where(self.row == 0, pltpu.roll(other, 1, axis), pltpu.roll(own, 1, axis))
        after = jnp.where(
            self.row == rows - 1, pltpu.roll(other, rows - 1, axis), pltpu.roll(own, rows - 1, axis)
        )
        return own + self.first_y * before + self.last_y * after

    def columns_joined(self, field):
        width = self.shape[1]
        axis = field.ndim - 1
        before = pltpu.roll(field, 1, axis)
        after = pltpu.roll(field, width - 1, axis)
        return field + self.first_x * before + self.last_x * after


def split(value, pieces):
    out = []
    for _ in range(pieces):
        high = value.astype(jnp.bfloat16)
        out.append(high)
        value = value - high.astype(jnp.float32)
    return out


def fetch_kernel(*refs):
    air, diffusivity, absorber, thickness, zenith, lit, coef, weight = refs[:8]
    amount, state, absorber_out, thickness_out, zenith_out, lit_out, coef_out, weight_out, sems = refs[8:]
    levels = air.shape[0]
    copies = [
        pltpu.make_async_copy(absorber, absorber_out, sems.at[0]),
        pltpu.make_async_copy(air, state.at[pl.ds(0, levels)], sems.at[1]),
        pltpu.make_async_copy(diffusivity, state.at[levels], sems.at[2]),
        pltpu.make_async_copy(zenith, zenith_out, sems.at[3]),
        pltpu.make_async_copy(coef, coef_out, sems.at[4]),
        pltpu.make_async_copy(weight, weight_out, sems.at[5]),
        pltpu.make_async_copy(thickness, thickness_out, sems.at[6]),
        pltpu.make_async_copy(lit, lit_out, sems.at[7]),
    ]
    for copy in copies:
        copy.start()
    for copy in copies:
        copy.wait()
    for s in range(absorber_out.shape[0]):
        total = absorber_out[s, 0]
        for k in range(1, levels):
            total = total + absorber_out[s, k]
        amount[s] = total


def amount_rows(totals, scale, depth, ones):
    value = jnp.concatenate([t * scale for t in totals], axis=0)
    hi, mid, lo = (p.astype(jnp.float32) for p in split(value, 3))
    rest = depth - 4 * value.shape[0]
    index = lax.broadcasted_iota(jnp.int32, (rest, value.shape[1]), 0)
    tail = jnp.where(index < ones, 1.0, 0.0)
    return jnp.concatenate([hi, mid, lo, hi, tail], axis=0).astype(jnp.bfloat16)


def layers_kernel(absorber, zenith, coef, weight, left, drops, spread):
    species, levels, rows, width = absorber.shape
    terms = coef.shape[1]
    group = species * rows
    depth = left.shape[1]
    c_pieces = split(coef[...], 2)
    w_pieces = split(jnp.log2(weight[...]), 3)
    lane = lax.broadcasted_iota(jnp.int32, (rows, depth), 1)
    row = lax.broadcasted_iota(jnp.int32, (rows, depth), 0)
    ones_at = 4 * group
    stack = jnp.concatenate([p.astype(jnp.float32) for p in c_pieces + w_pieces], axis=0)
    count = stack.shape[0]
    pick_row = lax.broadcasted_iota(jnp.int32, (count, depth), 0)
    pick_lane = lax.broadcasted_iota(jnp.int32, (count, depth), 1)
    kind = pick_lane // group
    wanted = jnp.where(kind == 3, species, 0) + (pick_lane % group) // rows
    wanted = jnp.where(kind >= 4, 2 * species + pick_lane - ones_at, wanted)
    pick = (pick_row == wanted).astype(jnp.bfloat16)
    spread[...] = lax.dot_general(
        stack.astype(jnp.bfloat16),
        pick,
        (((0,), (0,)), ((), ())),
        preferred_element_type=jnp.float32,
    )
    mask = ((lane % rows == row) | (lane >= ones_at)).astype(jnp.float32)
    for g in range(0, terms, 2):
        pair = [jnp.broadcast_to(spread[pl.ds(g + i, 1), :], (rows, depth)) * mask for i in (0, 1)]
        left[pl.ds(g * rows, 2 * rows), :] = jnp.concatenate(pair, axis=0).astype(jnp.bfloat16)

    scale = -log2e / zenith[...]
    totals = [jnp.zeros((rows, width), jnp.float32)] * species
    blocks = []
    for k in range(levels + 1):
        if k:
            totals = [totals[s] + absorber[s, k - 1] for s in range(species)]
        blocks.append(amount_rows(totals, scale, depth, 3))
    right = jnp.concatenate(blocks, axis=1)
    chunk = 448
    for start in range(0, terms * rows, chunk):
        out = jnp.exp2(
            jnp.dot(left[pl.ds(start, chunk), :], right, preferred_element_type=jnp.float32)
        )
        for k in range(levels):
            drop = out[:, k * width : (k + 1) * width] - out[:, (k + 1) * width : (k + 2) * width]
            drops[k, pl.ds(start, chunk), :] = drop


def radiate_kernel(left, drops, upper, zenith, lit, thickness, heat):
    levels, rows, width = heat.shape
    depth = left.shape[1]
    species = upper.shape[0]
    zen = zenith[...]
    below = lax.axis_index("lev") > 0
    totals = [jnp.where(below, upper[s], 0.0) for s in range(species)]
    right = amount_rows(totals, -log2e / zen, depth, 0)
    chunk = 448
    sums = [jnp.zeros((rows, width), jnp.float32) for _ in range(levels)]
    for start in range(0, left.shape[0], chunk):
        above = jnp.exp2(
            jnp.dot(left[pl.ds(start, chunk), :], right, preferred_element_type=jnp.float32)
        )
        for k in range(levels):
            absorbed = above * drops[k, pl.ds(start, chunk), :]
            sums[k] = sums[k] + jnp.sum(absorbed.reshape(chunk // rows, rows, width), axis=0)
    lit_zenith = jnp.where(lit[...] == 1, zen, 0.0)
    for k in range(levels):
        heat[k] = lit_zenith * sums[k] / thickness[k]


def to_edge_tile(stencil, edge, kind, columns):
    width = stencil.shape[1]
    half = width // 2
    count = len(columns)
    for j, value in enumerate(columns):
        at = kind * count + j
        low = pltpu.roll(value, at, 1) if at else value
        high = pltpu.roll(value, (half + at + 1) % width, 1)
        edge = jnp.where(stencil.lane == at, low, edge)
        edge = jnp.where(stencil.lane == half + at, high, edge)
    return edge


def tiles_of(field):
    return [field[l, t] for t in range(2) for l in range(field.shape[0])]


def state_kernel(own_state, other_state, first_tend, second, edge_out, span_out):
    levels = own_state.shape[0] - 1
    rows, width = own_state.shape[1:]
    stencil = Stencil(rows, width)
    air = jnp.stack([own_state[:levels], other_state[:levels]], axis=1)
    kappa = jnp.stack([own_state[levels], other_state[levels]], axis=0)
    r = stencil.residual(air, kappa)
    joined = stencil.rows_joined(r, jnp.concatenate([r[:, 1:], r[:, :1]], axis=1))
    tend = stencil.inv_mass * stencil.columns_joined(joined)
    first_tend[...] = tend[:, 0]
    second[...] = stencil.residual(tend, kappa)
    left_side = stencil.lane < width // 2
    node_x = stencil.nodes[1]
    to_edge = jnp.where(left_side, by_node(node_x, table[:, 0]), by_node(node_x, table[:, 3]))
    span = stencil.apply("t", 1, kappa * stencil.weight_x * to_edge)
    in_edge = (stencil.lane < points) | (stencil.lane >= width - points)
    span = jnp.where(in_edge, span, 0.0)
    span_out[...] = span
    edge = jnp.zeros((rows, width), jnp.float32)
    edge = to_edge_tile(stencil, edge, 0, tiles_of(joined))
    edge = to_edge_tile(stencil, edge, 2, [span[t] for t in range(2) for _ in range(levels)])
    edge_out[...] = to_edge_tile(stencil, edge, 3, [kappa[t] for t in range(2) for _ in range(levels)])


def edge_kernel(own_state, other_state, own_heat, other_heat, second, edge_in, joined_out, edge_out):
    levels, rows, width = own_heat.shape
    stencil = Stencil(rows, width)
    heat = jnp.stack([own_heat[...], other_heat[...]], axis=1)
    kappa = jnp.stack([own_state[levels], other_state[levels]], axis=0)
    r = second[...] + stencil.residual(heat, kappa)
    joined = stencil.rows_joined(r, jnp.concatenate([r[:, 1:], r[:, :1]], axis=1))
    joined_out[...] = joined[:, 0]
    edge_out[...] = to_edge_tile(stencil, edge_in[...], 1, tiles_of(joined))


def base_kernel(own_state, own_heat, first_tend, joined, heat_out, base):
    levels, rows, width = own_heat.shape
    stencil = Stencil(rows, width)
    heat = own_heat[...]
    heat_out[...] = heat
    second = stencil.inv_mass * stencil.columns_joined(joined[...])
    base[...] = (
        own_state[:levels]
        + time_step * (first_tend[...] + heat)
        + (0.5 * time_step * time_step) * second
    )


def step_kernel(base, span, own_edge, from_before, from_after, out):
    levels, rows, width = base.shape
    half = width // 2
    count = 2 * levels
    stencil = Stencil(rows, width)
    row, lane = stencil.row, stencil.lane
    own = own_edge[...]
    mates = pltpu.roll(jnp.where(lane >= half, from_before[...], from_after[...]), half, 1)

    def kind(tile, n):
        return pltpu.roll(tile, (-n * count) % width, 1)

    def along_y(kappa, value):
        flux = stencil.weight_y * kappa * stencil.apply("d", 0, value)
        return -gll_weights[0] * stencil.apply("t", 0, flux)

    def joined(value):
        other = jnp.where(
            lane % count < levels,
            pltpu.roll(value, width - levels, 1),
            pltpu.roll(value, levels, 1),
        )
        return stencil.rows_joined(value, other)

    edge_mass = stencil.inv_mass_y * (1.0 / mass_points[0])
    change = edge_mass * mates
    mates_change = edge_mass * own
    in_mates = along_y(kind(mates, 3), mates_change) - stencil.weight_y * kind(mates, 2) * mates_change
    add = kind(mates, 1) + joined(along_y(kind(own, 3), change) + in_mates)
    at_left, at_right = lane == 0, lane == width - 1

    def spread(tile, j):
        low = jnp.broadcast_to(tile[:, j : j + 1], (rows, width))
        high = jnp.broadcast_to(tile[:, half + j : half + j + 1], (rows, width))
        return jnp.where(lane < half, low, high)

    for l in range(levels):
        changes = [spread(change, t * levels + l) for t in range(2)]
        r = [-stencil.weight_y * span[t] * changes[t] for t in range(2)]
        moved = stencil.columns_joined(stencil.rows_joined(r[0], r[1]))
        edges = at_left | at_right
        moved = moved + jnp.where(edges, spread(add, l), 0.0)
        out[l] = (
            base[l]
            + time_step * jnp.where(edges, changes[0], 0.0)
            + (0.5 * time_step * time_step) * stencil.inv_mass * moved
        )


def swap(value, axis, pairs):
    route = [(a, b) for a, b in pairs] + [(b, a) for a, b in pairs]
    return lax.ppermute(value, axis, route)


def shards(
    air_state, diffusivity, absorber, thickness, cos_zenith, sunlit, absorb_coef, solar_weight
):
    levels, rows, width = air_state.shape
    terms = absorb_coef.shape[1]
    tile = lambda n: jax.ShapeDtypeStruct((n, rows, width), jnp.float32)
    big = pltpu.CompilerParams(vmem_limit_bytes=32 * 1024 * 1024)
    weight = solar_weight[None]
    args = (air_state, diffusivity, absorber, thickness, cos_zenith, sunlit, absorb_coef, weight)
    args = tuple(pltpu.with_memory_space_constraint(x, pltpu.HBM) for x in args)
    same = lambda x: jax.ShapeDtypeStruct(x.shape, x.dtype)
    amount, own_state, absorber, thickness, cos_zenith, sunlit, absorb_coef, weight = pl.pallas_call(
        fetch_kernel,
        out_shape=(tile(absorber.shape[0]), tile(levels + 1)) + tuple(same(x) for x in args[2:]),
        in_specs=[pl.BlockSpec(memory_space=pltpu.HBM)] * len(args),
        scratch_shapes=[pltpu.SemaphoreType.DMA((len(args),))],
        compiler_params=pltpu.CompilerParams(vmem_limit_bytes=32 * 1024 * 1024),
        name="fetch",
    )(*args)
    size = lax.axis_size("lev")
    lev = lax.axis_index("lev")
    upper = None
    for step in range(1, size):
        moved = lax.ppermute(amount, "lev", [(i, (i + step) % size) for i in range(size)])
        if size > 2:
            moved = jnp.where(lev >= step, moved, 0.0)
        upper = moved if upper is None else upper + moved
    if upper is None:
        upper = jnp.zeros_like(amount)
    other_state = swap(own_state, "sub", [(0, 1)])
    left, drops = pl.pallas_call(
        layers_kernel,
        out_shape=(
            jax.ShapeDtypeStruct((terms * rows, 256), jnp.bfloat16),
            jax.ShapeDtypeStruct((levels, terms * rows, width), jnp.float32),
        ),
        scratch_shapes=[pltpu.VMEM((terms, 256), jnp.float32)],
        compiler_params=big,
        name="layers",
    )(absorber, cos_zenith, absorb_coef, weight)
    own_heat = pl.pallas_call(
        radiate_kernel, out_shape=tile(levels), compiler_params=big, name="radiate"
    )(left, drops, upper, cos_zenith, sunlit, thickness)
    other_heat = swap(own_heat, "sub", [(0, 1)])
    pair = jax.ShapeDtypeStruct((levels, 2, rows, width), jnp.float32)
    plane = jax.ShapeDtypeStruct((rows, width), jnp.float32)
    first_tend, second, edge, span = pl.pallas_call(
        state_kernel,
        out_shape=(tile(levels), pair, plane, tile(2)),
        compiler_params=big,
        name="state",
    )(own_state, other_state)
    joined, edge = pl.pallas_call(
        edge_kernel, out_shape=(tile(levels), plane), compiler_params=big, name="edges"
    )(own_state, other_state, own_heat, other_heat, second, edge)
    wide = lax.axis_size("wide")
    from_before = lax.ppermute(edge, "wide", [(i, (i + 1) % wide) for i in range(wide)])
    from_after = lax.ppermute(edge, "wide", [((i + 1) % wide, i) for i in range(wide)])
    heat, base = pl.pallas_call(
        base_kernel, out_shape=(tile(levels), tile(levels)), compiler_params=big, name="base"
    )(own_state, own_heat, first_tend, joined)
    new_state = pl.pallas_call(
        step_kernel, out_shape=tile(levels), compiler_params=big, name="step"
    )(base, span, edge, from_before, from_after)
    return (heat, new_state)


def solution(mesh):
    in_specs = (
        P("lev", ("grp", "sub"), "wide"),
        P(("grp", "sub"), "wide"),
        P(None, "lev", ("grp", "sub"), "wide"),
        P("lev", ("grp", "sub"), "wide"),
        P(("grp", "sub"), "wide"),
        P(("grp", "sub"), "wide"),
        P(),
        P(),
    )
    out_specs = (P("lev", ("grp", "sub"), "wide"), P("lev", ("grp", "sub"), "wide"))
    return jax.shard_map(shards, mesh=mesh, in_specs=in_specs, out_specs=out_specs, check_vma=False)
```

```python
import math

import jax
import jax.numpy as jnp
import numpy as np
from jax import lax
from jax.experimental import pallas as pl
from jax.experimental.pallas import tpu as pltpu
from jax.sharding import PartitionSpec as P

time_step = 0.004
points = 4
strip = 2 * points
log2e = 1.4426950408889634
gll_weights = (1.0 / 6.0, 5.0 / 6.0, 5.0 / 6.0, 1.0 / 6.0)
mass_points = (1.0 / 3.0, 5.0 / 6.0, 5.0 / 6.0, 1.0 / 3.0)


def derivative_table():
    root_five = math.sqrt(5.0)
    outer_big = (5.0 + 5.0 * root_five) / 4.0
    outer_small = (5.0 * root_five - 5.0) / 4.0
    inner_big = (1.0 + root_five) / 4.0
    inner_mid = root_five / 2.0
    inner_small = (root_five - 1.0) / 4.0
    return np.array(
        [
            [-3.0, outer_big, -outer_small, 0.5],
            [-inner_big, 0.0, inner_mid, -inner_small],
            [inner_small, -inner_mid, 0.0, inner_big],
            [-0.5, outer_small, -outer_big, 3.0],
        ]
    )


table = derivative_table()


def by_node(node, values):
    out = jnp.full(node.shape, values[3], jnp.float32)
    for i in (2, 1, 0):
        out = jnp.where(node == i, jnp.float32(values[i]), out)
    return out


class Stencil:
    def __init__(self, rows, width):
        self.shape = (rows, width)
        self.row = lax.broadcasted_iota(jnp.int32, (rows, width), 0)
        self.lane = lax.broadcasted_iota(jnp.int32, (rows, width), 1)
        node_y, node_x = self.row % points, self.lane % points
        self.nodes = (node_y, node_x)
        self.weight_x = by_node(node_x, gll_weights)
        self.weight_y = by_node(node_y, gll_weights)
        self.inv_mass_y = by_node(node_y, [1.0 / m for m in mass_points])
        self.inv_mass = self.inv_mass_y * by_node(node_x, [1.0 / m for m in mass_points])
        inner_first = (node_x == 0) & (self.lane > 0)
        inner_last = (node_x == points - 1) & (self.lane < width - 1)
        self.first_x = inner_first.astype(jnp.float32)
        self.last_x = inner_last.astype(jnp.float32)
        self.first_y = (node_y == 0).astype(jnp.float32)
        self.last_y = (node_y == points - 1).astype(jnp.float32)
        self.coefs = {}

    def coef(self, name, axis):
        if (name, axis) not in self.coefs:
            matrix = table if name == "d" else table.T
            self.coefs[name, axis] = [
                by_node(
                    self.nodes[axis],
                    [matrix[i, i + step] if 0 <= i + step < points else 0.0 for i in range(points)],
                )
                for step in range(-3, 4)
            ]
        return self.coefs[name, axis]

    def apply(self, name, axis, field):
        size = self.shape[axis]
        out = None
        for step, coef in zip(range(-3, 4), self.coef(name, axis)):
            moved = field if step == 0 else pltpu.roll(field, (-step) % size, field.ndim - 2 + axis)
            term = coef * moved
            out = term if out is None else out + term
        return out

    def residual(self, field, kappa):
        flux_x = kappa * self.weight_x * self.apply("d", 1, field)
        flux_y = kappa * self.weight_y * self.apply("d", 0, field)
        part_x = self.weight_y * self.apply("t", 1, flux_x)
        return -part_x - self.weight_x * self.apply("t", 0, flux_y)

    def rows_joined(self, own, other):
        rows = self.shape[0]
        axis = own.ndim - 2
        before = jnp.where(self.row == 0, pltpu.roll(other, 1, axis), pltpu.roll(own, 1, axis))
        after = jnp.where(
            self.row == rows - 1, pltpu.roll(other, rows - 1, axis), pltpu.roll(own, rows - 1, axis)
        )
        return own + self.first_y * before + self.last_y * after

    def columns_joined(self, field):
        width = self.shape[1]
        axis = field.ndim - 1
        before = pltpu.roll(field, 1, axis)
        after = pltpu.roll(field, width - 1, axis)
        return field + self.first_x * before + self.last_x * after


def to_strips(lane, start, values):
    width = lane.shape[1]
    for n, value in enumerate(values):
        if value is not None:
            moved = pltpu.roll(value, strip * n + points, 1)
            start = jnp.where(lane // strip == n, moved, start)
    return start


def split(value, pieces):
    out = []
    for _ in range(pieces):
        high = value.astype(jnp.bfloat16)
        out.append(high)
        value = value - high.astype(jnp.float32)
    return out


def fetch_kernel(*refs):
    air, diffusivity, absorber, thickness, zenith, lit, coef, weight = refs[:8]
    amount, state, absorber_out, thickness_out, zenith_out, lit_out, coef_out, weight_out, sems = refs[8:]
    levels = air.shape[0]
    copies = [
        pltpu.make_async_copy(absorber, absorber_out, sems.at[0]),
        pltpu.make_async_copy(air, state.at[pl.ds(0, levels)], sems.at[1]),
        pltpu.make_async_copy(diffusivity, state.at[levels], sems.at[2]),
        pltpu.make_async_copy(zenith, zenith_out, sems.at[3]),
        pltpu.make_async_copy(coef, coef_out, sems.at[4]),
        pltpu.make_async_copy(weight, weight_out, sems.at[5]),
        pltpu.make_async_copy(thickness, thickness_out, sems.at[6]),
        pltpu.make_async_copy(lit, lit_out, sems.at[7]),
    ]
    for copy in copies:
        copy.start()
    for copy in copies:
        copy.wait()
    for s in range(absorber_out.shape[0]):
        total = absorber_out[s, 0]
        for k in range(1, levels):
            total = total + absorber_out[s, k]
        amount[s] = total


def amount_rows(totals, scale, depth, ones):
    value = jnp.concatenate([t * scale for t in totals], axis=0)
    hi, mid, lo = (p.astype(jnp.float32) for p in split(value, 3))
    rest = depth - 4 * value.shape[0]
    index = lax.broadcasted_iota(jnp.int32, (rest, value.shape[1]), 0)
    tail = jnp.where(index < ones, 1.0, 0.0)
    return jnp.concatenate([hi, mid, lo, hi, tail], axis=0).astype(jnp.bfloat16)


def layers_kernel(absorber, zenith, coef, weight, left, drops, spread):
    species, levels, rows, width = absorber.shape
    terms = coef.shape[1]
    group = species * rows
    depth = left.shape[1]
    c_pieces = split(coef[...], 2)
    w_pieces = split(jnp.log2(weight[...]), 3)
    lane = lax.broadcasted_iota(jnp.int32, (rows, depth), 1)
    row = lax.broadcasted_iota(jnp.int32, (rows, depth), 0)
    ones_at = 4 * group
    stack = jnp.concatenate([p.astype(jnp.float32) for p in c_pieces + w_pieces], axis=0)
    count = stack.shape[0]
    pick_row = lax.broadcasted_iota(jnp.int32, (count, depth), 0)
    pick_lane = lax.broadcasted_iota(jnp.int32, (count, depth), 1)
    kind = pick_lane // group
    wanted = jnp.where(kind == 3, species, 0) + (pick_lane % group) // rows
    wanted = jnp.where(kind >= 4, 2 * species + pick_lane - ones_at, wanted)
    pick = (pick_row == wanted).astype(jnp.bfloat16)
    spread[...] = lax.dot_general(
        stack.astype(jnp.bfloat16),
        pick,
        (((0,), (0,)), ((), ())),
        preferred_element_type=jnp.float32,
    )
    mask = ((lane % rows == row) | (lane >= ones_at)).astype(jnp.float32)
    for g in range(0, terms, 2):
        pair = [jnp.broadcast_to(spread[pl.ds(g + i, 1), :], (rows, depth)) * mask for i in (0, 1)]
        left[pl.ds(g * rows, 2 * rows), :] = jnp.concatenate(pair, axis=0).astype(jnp.bfloat16)

    scale = -log2e / zenith[...]
    totals = [jnp.zeros((rows, width), jnp.float32)] * species
    blocks = []
    for k in range(levels + 1):
        if k:
            totals = [totals[s] + absorber[s, k - 1] for s in range(species)]
        blocks.append(amount_rows(totals, scale, depth, 3))
    right = jnp.concatenate(blocks, axis=1)
    chunk = 448
    for start in range(0, terms * rows, chunk):
        out = jnp.exp2(
            jnp.dot(left[pl.ds(start, chunk), :], right, preferred_element_type=jnp.float32)
        )
        for k in range(levels):
            drop = out[:, k * width : (k + 1) * width] - out[:, (k + 1) * width : (k + 2) * width]
            drops[k, pl.ds(start, chunk), :] = drop


def radiate_kernel(
    left, drops, upper, upper_strips, packet, zenith, lit, thickness, second, kappa, fixed, heat, edge
):
    levels, rows, width = heat.shape
    depth = left.shape[1]
    species = upper.shape[0]
    stencil = Stencil(rows, width)
    zen = zenith[...]
    below = lax.axis_index("lev") > 0
    totals = [jnp.where(below, upper[s], 0.0) for s in range(species)]
    raw = levels + 1
    strip_totals = []
    for s in range(species):
        layer = packet[raw + s]
        total = jnp.where(below, upper_strips[s], 0.0)
        for k in range(levels):
            total = total + pltpu.roll(layer, strip * (k + 1), 1)
        strip_totals.append(total)
    right = jnp.concatenate(
        [
            amount_rows(totals, -log2e / zen, depth, 0),
            amount_rows(strip_totals, -log2e / packet[raw + species], depth, 3),
        ],
        axis=1,
    )
    chunk = 448
    lanes = 4
    zero = jnp.zeros((rows, width), jnp.float32)
    sums = [[zero] * lanes for _ in range(levels)]
    strip_sums = [zero] * lanes
    for start in range(0, left.shape[0], chunk):
        above = jnp.exp2(
            jnp.dot(left[pl.ds(start, chunk), :], right, preferred_element_type=jnp.float32)
        )
        for i in range(chunk // rows):
            at, n = i * rows, i % lanes
            main = above[at : at + rows, :width]
            strip_sums[n] = strip_sums[n] + above[at : at + rows, width:]
            for k in range(levels):
                sums[k][n] = sums[k][n] + main * drops[k, pl.ds(start + at, rows), :]

    def total_of(parts):
        return (parts[0] + parts[1]) + (parts[2] + parts[3])

    lit_zenith = jnp.where(lit[...] == 1, zen, 0.0)
    heats = [lit_zenith * total_of(sums[k]) / thickness[k] for k in range(levels)]
    for k in range(levels):
        heat[k] = heats[k]
    passed = total_of(strip_sums)
    other = packet[raw + species + 1] * (passed - pltpu.roll(passed, width - strip, 1))
    strips = to_strips(stencil.lane, zero, heats) + pltpu.roll(other, width // 2, 1)
    r = second[...] + stencil.residual(strips, kappa[...])
    joined = stencil.rows_joined(r, pltpu.roll(r, width // 2, 1))
    node = stencil.lane % strip
    edge[...] = jnp.where((node == points - 1) | (node == points), joined, fixed[...])


def tiles_of(field):
    gap = [None] * (8 - field.shape[0])
    return [t for n in range(2) for t in [field[l, n] for l in range(field.shape[0])] + gap]


def strips_kernel(own_state, absorber, zenith, lit, thickness, amount, packet, upper_strips):
    species, levels, rows, width = absorber.shape
    lane = lax.broadcasted_iota(jnp.int32, (rows, width), 1)
    zero = jnp.zeros((rows, width), jnp.float32)
    raw = levels + 1

    def everywhere(value, count):
        out = to_strips(lane, zero, [value])
        step = strip
        while step < strip * count:
            out = out + pltpu.roll(out, step, 1)
            step *= 2
        return out

    for s in range(species):
        upper_strips[s] = everywhere(amount[s], 8)
        packet[raw + s] = to_strips(lane, zero, [absorber[s, k] for k in range(levels)])
    for i in range(raw):
        packet[i] = own_state[i]
    zen = zenith[...]
    packet[raw + species] = everywhere(zen, 16)
    lit_zenith = jnp.where(lit[...] == 1, zen, 0.0)
    packet[raw + species + 1] = to_strips(
        lane, zero, [lit_zenith / thickness[k] for k in range(levels)]
    )


def state_kernel(own_state, packet, first_tend, second, span_out, second_strips, kappa_strips, fixed, mine):
    levels = own_state.shape[0] - 1
    rows, width = own_state.shape[1:]
    stencil = Stencil(rows, width)
    lane = stencil.lane
    zero = jnp.zeros((rows, width), jnp.float32)
    air = jnp.stack([own_state[:levels], packet[:levels]], axis=1)
    kappa = jnp.stack([own_state[levels], packet[levels]], axis=0)
    r = stencil.residual(air, kappa)
    joined = stencil.rows_joined(r, jnp.concatenate([r[:, 1:], r[:, :1]], axis=1))
    tend = stencil.inv_mass * stencil.columns_joined(joined)
    first_tend[...] = tend[:, 0]
    r = stencil.residual(tend, kappa)
    second[...] = r
    second_strips[...] = to_strips(lane, zero, tiles_of(r))
    left_side = lane < width // 2
    node_x = stencil.nodes[1]
    to_edge = jnp.where(left_side, by_node(node_x, table[:, 0]), by_node(node_x, table[:, 3]))
    span = stencil.apply("t", 1, kappa * stencil.weight_x * to_edge)
    in_edge = (lane < points) | (lane >= width - points)
    span = jnp.where(in_edge, span, 0.0)
    span_out[...] = span
    own = to_strips(lane, zero, tiles_of(joined))
    by_level = lambda field: to_strips(
        lane, zero, tiles_of(jnp.broadcast_to(field[None], (levels,) + field.shape))
    )
    kappa_edge = by_level(kappa)
    kappa_strips[...] = kappa_edge
    out = zero
    node = lane % strip
    for step, value in ((1, own), (2, by_level(span)), (3, kappa_edge)):
        out = jnp.where(node == points - 1 - step, pltpu.roll(value, width - step, 1), out)
        out = jnp.where(node == points + step, pltpu.roll(value, step, 1), out)
    fixed[...] = out
    change = stencil.inv_mass_y * (1.0 / mass_points[0]) * own
    mine[0] = change
    mine[1] = stencil.weight_y * stencil.apply("d", 0, change)


def base_kernel(own_state, packet, own_heat, other_heat, first_tend, second, heat_out, base):
    levels, rows, width = own_heat.shape
    stencil = Stencil(rows, width)
    own = own_heat[...]
    heat_out[...] = own
    heat = jnp.stack([own, other_heat[...]], axis=1)
    kappa = jnp.stack([own_state[levels], packet[levels]], axis=0)
    r = second[...] + stencil.residual(heat, kappa)
    joined = stencil.rows_joined(r[:, 0], r[:, 1])
    base[...] = (
        own_state[:levels]
        + time_step * (first_tend[...] + own)
        + (0.5 * time_step * time_step) * (stencil.inv_mass * stencil.columns_joined(joined))
    )


def step_kernel(base, span, kappa, mine, from_before, from_after, out):
    levels, rows, width = base.shape
    half = width // 2
    stencil = Stencil(rows, width)
    lane = stencil.lane
    before, after = from_before[...], from_after[...]
    at_first = lane % strip == points

    def of_mates(step):
        return jnp.where(at_first, pltpu.roll(before, step, 1), pltpu.roll(after, width - step, 1))

    change = stencil.inv_mass_y * (1.0 / mass_points[0]) * of_mates(2)
    flux = of_mates(4) * mine[1] + stencil.weight_y * kappa[...] * stencil.apply("d", 0, change)
    r = -gll_weights[0] * stencil.apply("t", 0, flux) - stencil.weight_y * of_mates(3) * mine[0]
    add = of_mates(1) + stencil.rows_joined(r, pltpu.roll(r, half, 1))
    edges = (lane == 0) | (lane == width - 1)

    def spread(tile, at):
        low = jnp.broadcast_to(tile[:, at + points : at + points + 1], (rows, width))
        high = jnp.broadcast_to(tile[:, at + points - 1 : at + points], (rows, width))
        return jnp.where(lane < half, low, high)

    for l in range(levels):
        changes = [spread(change, t * half + strip * l) for t in range(2)]
        r = [-stencil.weight_y * span[t] * changes[t] for t in range(2)]
        moved = stencil.columns_joined(stencil.rows_joined(r[0], r[1]))
        moved = moved + jnp.where(edges, spread(add, strip * l), 0.0)
        out[l] = (
            base[l]
            + time_step * jnp.where(edges, changes[0], 0.0)
            + (0.5 * time_step * time_step) * stencil.inv_mass * moved
        )


def swap(value, axis, pairs):
    route = [(a, b) for a, b in pairs] + [(b, a) for a, b in pairs]
    return lax.ppermute(value, axis, route)


def shards(
    air_state, diffusivity, absorber, thickness, cos_zenith, sunlit, absorb_coef, solar_weight
):
    levels, rows, width = air_state.shape
    terms = absorb_coef.shape[1]
    tile = lambda n: jax.ShapeDtypeStruct((n, rows, width), jnp.float32)
    big = pltpu.CompilerParams(vmem_limit_bytes=32 * 1024 * 1024)
    weight = solar_weight[None]
    args = (air_state, diffusivity, absorber, thickness, cos_zenith, sunlit, absorb_coef, weight)
    args = tuple(pltpu.with_memory_space_constraint(x, pltpu.HBM) for x in args)
    same = lambda x: jax.ShapeDtypeStruct(x.shape, x.dtype)
    amount, own_state, absorber, thickness, cos_zenith, sunlit, absorb_coef, weight = pl.pallas_call(
        fetch_kernel,
        out_shape=(tile(absorber.shape[0]), tile(levels + 1)) + tuple(same(x) for x in args[2:]),
        in_specs=[pl.BlockSpec(memory_space=pltpu.HBM)] * len(args),
        scratch_shapes=[pltpu.SemaphoreType.DMA((len(args),))],
        compiler_params=pltpu.CompilerParams(vmem_limit_bytes=32 * 1024 * 1024),
        name="fetch",
    )(*args)
    species = absorber.shape[0]
    packet, strip_amount = pl.pallas_call(
        strips_kernel,
        out_shape=(tile(levels + 1 + species + 2), tile(species)),
        compiler_params=big,
        name="strips",
    )(own_state, absorber, cos_zenith, sunlit, thickness, amount)
    size = lax.axis_size("lev")
    lev = lax.axis_index("lev")
    upper = upper_strips = None
    for step in range(1, size):
        straight = [(i, (i + step) % size) for i in range(size)]
        crossed = [(2 * i + c, 2 * j + 1 - c) for i, j in straight for c in range(2)]
        moved = lax.ppermute(amount, "lev", straight)
        moved_strips = lax.ppermute(strip_amount, ("lev", "sub"), crossed)
        if size > 2:
            moved = jnp.where(lev >= step, moved, 0.0)
            moved_strips = jnp.where(lev >= step, moved_strips, 0.0)
        upper = moved if upper is None else upper + moved
        upper_strips = moved_strips if upper_strips is None else upper_strips + moved_strips
    if upper is None:
        upper, upper_strips = jnp.zeros_like(amount), jnp.zeros_like(amount)
    other_packet = swap(packet, "sub", [(0, 1)])
    left, drops = pl.pallas_call(
        layers_kernel,
        out_shape=(
            jax.ShapeDtypeStruct((terms * rows, 256), jnp.bfloat16),
            jax.ShapeDtypeStruct((levels, terms * rows, width), jnp.float32),
        ),
        scratch_shapes=[pltpu.VMEM((terms, 256), jnp.float32)],
        compiler_params=big,
        name="layers",
    )(absorber, cos_zenith, absorb_coef, weight)
    pair = jax.ShapeDtypeStruct((levels, 2, rows, width), jnp.float32)
    plane = jax.ShapeDtypeStruct((rows, width), jnp.float32)
    first_tend, second, span, second_strips, kappa_strips, fixed, mine = pl.pallas_call(
        state_kernel,
        out_shape=(tile(levels), pair, tile(2), plane, plane, plane, tile(2)),
        compiler_params=big,
        name="state",
    )(own_state, other_packet)
    own_heat, edge = pl.pallas_call(
        radiate_kernel, out_shape=(tile(levels), plane), compiler_params=big, name="radiate"
    )(
        left,
        drops,
        upper,
        upper_strips,
        other_packet,
        cos_zenith,
        sunlit,
        thickness,
        second_strips,
        kappa_strips,
        fixed,
    )
    wide = lax.axis_size("wide")
    from_before = lax.ppermute(edge, "wide", [(i, (i + 1) % wide) for i in range(wide)])
    from_after = lax.ppermute(edge, "wide", [((i + 1) % wide, i) for i in range(wide)])
    other_heat = swap(own_heat, "sub", [(0, 1)])
    heat, base = pl.pallas_call(
        base_kernel, out_shape=(tile(levels), tile(levels)), compiler_params=big, name="base"
    )(own_state, other_packet, own_heat, other_heat, first_tend, second)
    new_state = pl.pallas_call(
        step_kernel, out_shape=tile(levels), compiler_params=big, name="step"
    )(base, span, kappa_strips, mine, from_before, from_after)
    return (heat, new_state)


def solution(mesh):
    in_specs = (
        P("lev", ("grp", "sub"), "wide"),
        P(("grp", "sub"), "wide"),
        P(None, "lev", ("grp", "sub"), "wide"),
        P("lev", ("grp", "sub"), "wide"),
        P(("grp", "sub"), "wide"),
        P(("grp", "sub"), "wide"),
        P(),
        P(),
    )
    out_specs = (P("lev", ("grp", "sub"), "wide"), P("lev", ("grp", "sub"), "wide"))
    return jax.shard_map(shards, mesh=mesh, in_specs=in_specs, out_specs=out_specs, check_vma=False)
```

```python
import functools
import math

import jax
import jax.numpy as jnp
import numpy as np
from jax import lax
from jax.experimental import pallas as pl
from jax.experimental.pallas import tpu as pltpu
from jax.sharding import PartitionSpec as P

time_step = 0.004
points = 4
strip = 2 * points
log2e = 1.4426950408889634
gll_weights = (1.0 / 6.0, 5.0 / 6.0, 5.0 / 6.0, 1.0 / 6.0)
mass_points = (1.0 / 3.0, 5.0 / 6.0, 5.0 / 6.0, 1.0 / 3.0)


def derivative_table():
    root_five = math.sqrt(5.0)
    outer_big = (5.0 + 5.0 * root_five) / 4.0
    outer_small = (5.0 * root_five - 5.0) / 4.0
    inner_big = (1.0 + root_five) / 4.0
    inner_mid = root_five / 2.0
    inner_small = (root_five - 1.0) / 4.0
    return np.array(
        [
            [-3.0, outer_big, -outer_small, 0.5],
            [-inner_big, 0.0, inner_mid, -inner_small],
            [inner_small, -inner_mid, 0.0, inner_big],
            [-0.5, outer_small, -outer_big, 3.0],
        ]
    )


table = derivative_table()


def by_node(node, values):
    out = jnp.full(node.shape, values[3], jnp.float32)
    for i in (2, 1, 0):
        out = jnp.where(node == i, jnp.float32(values[i]), out)
    return out


class Stencil:
    def __init__(self, rows, width):
        self.shape = (rows, width)
        self.row = lax.broadcasted_iota(jnp.int32, (rows, width), 0)
        self.lane = lax.broadcasted_iota(jnp.int32, (rows, width), 1)
        node_y, node_x = self.row % points, self.lane % points
        self.nodes = (node_y, node_x)
        self.weight_x = by_node(node_x, gll_weights)
        self.weight_y = by_node(node_y, gll_weights)
        self.inv_mass_y = by_node(node_y, [1.0 / m for m in mass_points])
        self.inv_mass = self.inv_mass_y * by_node(node_x, [1.0 / m for m in mass_points])
        inner_first = (node_x == 0) & (self.lane > 0)
        inner_last = (node_x == points - 1) & (self.lane < width - 1)
        self.first_x = inner_first.astype(jnp.float32)
        self.last_x = inner_last.astype(jnp.float32)
        self.first_y = (node_y == 0).astype(jnp.float32)
        self.last_y = (node_y == points - 1).astype(jnp.float32)
        self.coefs = {}

    def coef(self, name, axis):
        if (name, axis) not in self.coefs:
            matrix = table if name == "d" else table.T
            self.coefs[name, axis] = [
                by_node(
                    self.nodes[axis],
                    [matrix[i, i + step] if 0 <= i + step < points else 0.0 for i in range(points)],
                )
                for step in range(-3, 4)
            ]
        return self.coefs[name, axis]

    def apply(self, name, axis, field):
        size = self.shape[axis]
        out = None
        for step, coef in zip(range(-3, 4), self.coef(name, axis)):
            moved = field if step == 0 else pltpu.roll(field, (-step) % size, field.ndim - 2 + axis)
            term = coef * moved
            out = term if out is None else out + term
        return out

    def residual(self, field, kappa):
        flux_x = kappa * self.weight_x * self.apply("d", 1, field)
        flux_y = kappa * self.weight_y * self.apply("d", 0, field)
        part_x = self.weight_y * self.apply("t", 1, flux_x)
        return -part_x - self.weight_x * self.apply("t", 0, flux_y)

    def rows_joined(self, own, other):
        rows = self.shape[0]
        axis = own.ndim - 2
        before = jnp.where(self.row == 0, pltpu.roll(other, 1, axis), pltpu.roll(own, 1, axis))
        after = jnp.where(
            self.row == rows - 1, pltpu.roll(other, rows - 1, axis), pltpu.roll(own, rows - 1, axis)
        )
        return own + self.first_y * before + self.last_y * after

    def columns_joined(self, field):
        width = self.shape[1]
        axis = field.ndim - 1
        before = pltpu.roll(field, 1, axis)
        after = pltpu.roll(field, width - 1, axis)
        return field + self.first_x * before + self.last_x * after


def to_strips(lane, start, values):
    width = lane.shape[1]
    for n, value in enumerate(values):
        if value is not None:
            moved = pltpu.roll(value, strip * n + points, 1)
            start = jnp.where(lane // strip == n, moved, start)
    return start


def split(value, pieces):
    out = []
    for _ in range(pieces):
        high = value.astype(jnp.bfloat16)
        out.append(high)
        value = value - high.astype(jnp.float32)
    return out


def fetch_kernel(*refs):
    air, diffusivity, absorber, thickness, zenith, lit, coef, weight = refs[:8]
    amount, state, absorber_out, thickness_out, zenith_out, lit_out, coef_out, weight_out, sems = refs[8:]
    levels = air.shape[0]
    copies = [
        pltpu.make_async_copy(absorber, absorber_out, sems.at[0]),
        pltpu.make_async_copy(air, state.at[pl.ds(0, levels)], sems.at[1]),
        pltpu.make_async_copy(diffusivity, state.at[levels], sems.at[2]),
        pltpu.make_async_copy(zenith, zenith_out, sems.at[3]),
        pltpu.make_async_copy(coef, coef_out, sems.at[4]),
        pltpu.make_async_copy(weight, weight_out, sems.at[5]),
        pltpu.make_async_copy(thickness, thickness_out, sems.at[6]),
        pltpu.make_async_copy(lit, lit_out, sems.at[7]),
    ]
    for copy in copies:
        copy.start()
    for copy in copies:
        copy.wait()
    for s in range(absorber_out.shape[0]):
        total = absorber_out[s, 0]
        for k in range(1, levels):
            total = total + absorber_out[s, k]
        amount[s] = total


def amount_rows(totals, scale, depth, ones):
    value = jnp.concatenate([t * scale for t in totals], axis=0)
    hi, mid, lo = (p.astype(jnp.float32) for p in split(value, 3))
    rest = depth - 4 * value.shape[0]
    index = lax.broadcasted_iota(jnp.int32, (rest, value.shape[1]), 0)
    tail = jnp.where(index < ones, 1.0, 0.0)
    return jnp.concatenate([hi, mid, lo, hi, tail], axis=0).astype(jnp.bfloat16)


def layers_kernel(
    own_state, absorber, zenith, lit, thickness, coef, weight, left, drops, strips, factor, kappa, spread
):
    species, levels, rows, width = absorber.shape
    terms = coef.shape[1]
    group = species * rows
    depth = left.shape[1]
    c_pieces = split(coef[...], 2)
    w_pieces = split(jnp.log2(weight[...]), 3)
    lane = lax.broadcasted_iota(jnp.int32, (rows, depth), 1)
    row = lax.broadcasted_iota(jnp.int32, (rows, depth), 0)
    ones_at = 4 * group
    stack = jnp.concatenate([p.astype(jnp.float32) for p in c_pieces + w_pieces], axis=0)
    count = stack.shape[0]
    pick_row = lax.broadcasted_iota(jnp.int32, (count, depth), 0)
    pick_lane = lax.broadcasted_iota(jnp.int32, (count, depth), 1)
    kind = pick_lane // group
    wanted = jnp.where(kind == 3, species, 0) + (pick_lane % group) // rows
    wanted = jnp.where(kind >= 4, 2 * species + pick_lane - ones_at, wanted)
    pick = (pick_row == wanted).astype(jnp.bfloat16)
    spread[...] = lax.dot_general(
        stack.astype(jnp.bfloat16),
        pick,
        (((0,), (0,)), ((), ())),
        preferred_element_type=jnp.float32,
    )
    mask = ((lane % rows == row) | (lane >= ones_at)).astype(jnp.float32)
    for g in range(0, terms, 2):
        pair = [jnp.broadcast_to(spread[pl.ds(g + i, 1), :], (rows, depth)) * mask for i in (0, 1)]
        left[pl.ds(g * rows, 2 * rows), :] = jnp.concatenate(pair, axis=0).astype(jnp.bfloat16)

    scale = -log2e / zenith[...]
    totals = [jnp.zeros((rows, width), jnp.float32)] * species
    blocks = []
    for k in range(levels + 1):
        if k:
            totals = [totals[s] + absorber[s, k - 1] for s in range(species)]
        blocks.append(amount_rows(totals, scale, depth, 3))
    right = jnp.concatenate(blocks, axis=1)
    chunk = 448
    for start in range(0, terms * rows, chunk):
        out = jnp.exp2(
            jnp.dot(left[pl.ds(start, chunk), :], right, preferred_element_type=jnp.float32)
        )
        for k in range(levels):
            drop = out[:, k * width : (k + 1) * width] - out[:, (k + 1) * width : (k + 2) * width]
            drops[k, pl.ds(start, chunk), :] = drop

    place = lax.broadcasted_iota(jnp.int32, (rows, width), 1)
    zero = jnp.zeros((rows, width), jnp.float32)
    for s in range(species):
        total, sums = zero, [None]
        for k in range(levels):
            total = total + absorber[s, k]
            sums.append(total)
        strips[s] = to_strips(place, zero, sums)
    strips[species] = to_strips(place, zero - 1.0, [scale] * (levels + 1))
    lit_zenith = jnp.where(lit[...] == 1, zenith[...], 0.0)
    factor[...] = to_strips(place, zero, [lit_zenith / thickness[k] for k in range(levels)])
    kappa[...] = to_strips(place, zero, [own_state[levels]] * levels)


def radiate_kernel(left, drops, upper, zenith, lit, thickness, after, heat):
    levels, rows, width = heat.shape
    depth = left.shape[1]
    species = upper.shape[0]
    zen = zenith[...]
    below = lax.axis_index("lev") > 0
    totals = [jnp.where(below, upper[s], 0.0) for s in range(species)]
    right = amount_rows(totals, -log2e / zen, depth, 0)
    chunk = 448
    sums = [jnp.zeros((rows, width), jnp.float32) for _ in range(levels)]
    for start in range(0, left.shape[0], chunk):
        above = jnp.exp2(
            jnp.dot(left[pl.ds(start, chunk), :], right, preferred_element_type=jnp.float32)
        )
        for k in range(levels):
            absorbed = above * drops[k, pl.ds(start, chunk), :]
            sums[k] = sums[k] + jnp.sum(absorbed.reshape(chunk // rows, rows, width), axis=0)
    lit_zenith = jnp.where(lit[...] == 1, zen, 0.0)
    for k in range(levels):
        heat[k] = lit_zenith * sums[k] / thickness[k]


def edge_heat_kernel(levels, left, upper, layers, factor, kappa, second, out):
    species = upper.shape[0]
    rows, width = factor.shape
    stencil = Stencil(rows, width)
    lane = stencil.lane
    below = lax.axis_index("lev") > 0
    totals = []
    for s in range(species):
        above = jnp.where(below & (lane < strip), pltpu.roll(upper[s], points, 1), 0.0)
        total = layers[s] + above
        for k in range(1, levels + 1):
            total = total + pltpu.roll(above, strip * k, 1)
        totals.append(total)
    right = amount_rows(totals, layers[species], left.shape[1], 3)
    passed = jnp.exp2(jnp.dot(left[...], right, preferred_element_type=jnp.float32))
    passed = sum_rows(passed, rows)
    heat = factor[...] * (passed - pltpu.roll(passed, width - strip, 1))
    out[...] = stencil.residual(heat, kappa[...]) + jnp.where(lane < width // 2, second[...], 0.0)


def sum_rows(value, rows):
    parts = [value[i : i + rows] for i in range(0, value.shape[0], rows)]
    sums = parts[:8]
    for i in range(8, len(parts)):
        sums[i % 8] = sums[i % 8] + parts[i]
    while len(sums) > 1:
        sums = [sum(sums[i : i + 2]) for i in range(0, len(sums), 2)]
    return sums[0]


def join_kernel(own, other, fixed, heat, edge, heat_out):
    rows, width = own.shape
    stencil = Stencil(rows, width)
    r = own[...] + pltpu.roll(other[...], width // 2, 1)
    joined = stencil.rows_joined(r, pltpu.roll(r, width // 2, 1))
    node = stencil.lane % strip
    edge[...] = jnp.where((node == points - 1) | (node == points), joined, fixed[...])
    heat_out[...] = heat[...]


def tiles_of(field):
    gap = [None] * (8 - field.shape[0])
    return [t for n in range(2) for t in [field[l, n] for l in range(field.shape[0])] + gap]


def state_kernel(own_state, other_state, first_tend, second, span_out, second_strips, kappa_strips, fixed, mine):
    levels = own_state.shape[0] - 1
    rows, width = own_state.shape[1:]
    stencil = Stencil(rows, width)
    lane = stencil.lane
    zero = jnp.zeros((rows, width), jnp.float32)
    air = jnp.stack([own_state[:levels], other_state[:levels]], axis=1)
    kappa = jnp.stack([own_state[levels], other_state[levels]], axis=0)
    r = stencil.residual(air, kappa)
    joined = stencil.rows_joined(r, jnp.concatenate([r[:, 1:], r[:, :1]], axis=1))
    tend = stencil.inv_mass * stencil.columns_joined(joined)
    first_tend[...] = tend[:, 0]
    r = stencil.residual(tend, kappa)
    second[...] = r
    second_strips[...] = to_strips(lane, zero, tiles_of(r))
    left_side = lane < width // 2
    node_x = stencil.nodes[1]
    to_edge = jnp.where(left_side, by_node(node_x, table[:, 0]), by_node(node_x, table[:, 3]))
    span = stencil.apply("t", 1, kappa * stencil.weight_x * to_edge)
    in_edge = (lane < points) | (lane >= width - points)
    span = jnp.where(in_edge, span, 0.0)
    span_out[...] = span
    own = to_strips(lane, zero, tiles_of(joined))
    by_level = lambda field: to_strips(
        lane, zero, tiles_of(jnp.broadcast_to(field[None], (levels,) + field.shape))
    )
    kappa_edge = by_level(kappa)
    kappa_strips[...] = kappa_edge
    out = zero
    node = lane % strip
    for step, value in ((1, own), (2, by_level(span)), (3, kappa_edge)):
        out = jnp.where(node == points - 1 - step, pltpu.roll(value, width - step, 1), out)
        out = jnp.where(node == points + step, pltpu.roll(value, step, 1), out)
    fixed[...] = out
    change = stencil.inv_mass_y * (1.0 / mass_points[0]) * own
    mine[0] = change
    mine[1] = stencil.weight_y * stencil.apply("d", 0, change)


def base_kernel(own_state, other_state, own_heat, other_heat, first_tend, second, heat_out, base):
    levels, rows, width = own_heat.shape
    stencil = Stencil(rows, width)
    own = own_heat[...]
    heat_out[...] = own
    heat = jnp.stack([own, other_heat[...]], axis=1)
    kappa = jnp.stack([own_state[levels], other_state[levels]], axis=0)
    r = second[...] + stencil.residual(heat, kappa)
    joined = stencil.rows_joined(r[:, 0], r[:, 1])
    base[...] = (
        own_state[:levels]
        + time_step * (first_tend[...] + own)
        + (0.5 * time_step * time_step) * (stencil.inv_mass * stencil.columns_joined(joined))
    )


def step_kernel(base, span, kappa, mine, from_before, from_after, out):
    levels, rows, width = base.shape
    half = width // 2
    stencil = Stencil(rows, width)
    lane = stencil.lane
    before, after = from_before[...], from_after[...]
    at_first = lane % strip == points

    def of_mates(step):
        return jnp.where(at_first, pltpu.roll(before, step, 1), pltpu.roll(after, width - step, 1))

    change = stencil.inv_mass_y * (1.0 / mass_points[0]) * of_mates(2)
    flux = of_mates(4) * mine[1] + stencil.weight_y * kappa[...] * stencil.apply("d", 0, change)
    r = -gll_weights[0] * stencil.apply("t", 0, flux) - stencil.weight_y * of_mates(3) * mine[0]
    add = of_mates(1) + stencil.rows_joined(r, pltpu.roll(r, half, 1))
    edges = (lane == 0) | (lane == width - 1)

    def spread(tile, at):
        low = jnp.broadcast_to(tile[:, at + points : at + points + 1], (rows, width))
        high = jnp.broadcast_to(tile[:, at + points - 1 : at + points], (rows, width))
        return jnp.where(lane < half, low, high)

    for l in range(levels):
        changes = [spread(change, t * half + strip * l) for t in range(2)]
        r = [-stencil.weight_y * span[t] * changes[t] for t in range(2)]
        moved = stencil.columns_joined(stencil.rows_joined(r[0], r[1]))
        moved = moved + jnp.where(edges, spread(add, strip * l), 0.0)
        out[l] = (
            base[l]
            + time_step * jnp.where(edges, changes[0], 0.0)
            + (0.5 * time_step * time_step) * stencil.inv_mass * moved
        )


def swap(value, axis, pairs):
    route = [(a, b) for a, b in pairs] + [(b, a) for a, b in pairs]
    return lax.ppermute(value, axis, route)


def shards(
    air_state, diffusivity, absorber, thickness, cos_zenith, sunlit, absorb_coef, solar_weight
):
    levels, rows, width = air_state.shape
    terms = absorb_coef.shape[1]
    tile = lambda n: jax.ShapeDtypeStruct((n, rows, width), jnp.float32)
    big = pltpu.CompilerParams(vmem_limit_bytes=32 * 1024 * 1024)
    weight = solar_weight[None]
    args = (air_state, diffusivity, absorber, thickness, cos_zenith, sunlit, absorb_coef, weight)
    args = tuple(pltpu.with_memory_space_constraint(x, pltpu.HBM) for x in args)
    same = lambda x: jax.ShapeDtypeStruct(x.shape, x.dtype)
    amount, own_state, absorber, thickness, cos_zenith, sunlit, absorb_coef, weight = pl.pallas_call(
        fetch_kernel,
        out_shape=(tile(absorber.shape[0]), tile(levels + 1)) + tuple(same(x) for x in args[2:]),
        in_specs=[pl.BlockSpec(memory_space=pltpu.HBM)] * len(args),
        scratch_shapes=[pltpu.SemaphoreType.DMA((len(args),))],
        compiler_params=pltpu.CompilerParams(vmem_limit_bytes=32 * 1024 * 1024),
        name="fetch",
    )(*args)
    species = absorber.shape[0]
    size = lax.axis_size("lev")
    lev = lax.axis_index("lev")
    upper = None
    for step in range(1, size):
        moved = lax.ppermute(amount, "lev", [(i, (i + step) % size) for i in range(size)])
        if size > 2:
            moved = jnp.where(lev >= step, moved, 0.0)
        upper = moved if upper is None else upper + moved
    if upper is None:
        upper = jnp.zeros_like(amount)
    other_state = swap(own_state, "sub", [(0, 1)])
    plane = jax.ShapeDtypeStruct((rows, width), jnp.float32)
    left, drops, strips, factor, kappa = pl.pallas_call(
        layers_kernel,
        out_shape=(
            jax.ShapeDtypeStruct((terms * rows, 256), jnp.bfloat16),
            jax.ShapeDtypeStruct((levels, terms * rows, width), jnp.float32),
            tile(species + 1),
            plane,
            plane,
        ),
        scratch_shapes=[pltpu.VMEM((terms, 256), jnp.float32)],
        compiler_params=big,
        name="layers",
    )(own_state, absorber, cos_zenith, sunlit, thickness, absorb_coef, weight)
    pair = jax.ShapeDtypeStruct((levels, 2, rows, width), jnp.float32)
    first_tend, second, span, second_strips, kappa_strips, fixed, mine = pl.pallas_call(
        state_kernel,
        out_shape=(tile(levels), pair, tile(2), plane, plane, plane, tile(2)),
        compiler_params=big,
        name="state",
    )(own_state, other_state)
    own_r = pl.pallas_call(
        functools.partial(edge_heat_kernel, levels),
        out_shape=plane,
        compiler_params=big,
        name="edge_heat",
    )(left, upper, strips, factor, kappa, second_strips)
    other_r = swap(own_r, "sub", [(0, 1)])
    own_heat = pl.pallas_call(
        radiate_kernel, out_shape=tile(levels), compiler_params=big, name="radiate"
    )(left, drops, upper, cos_zenith, sunlit, thickness, own_r)
    edge, own_heat = pl.pallas_call(
        join_kernel, out_shape=(plane, tile(levels)), compiler_params=big, name="join"
    )(own_r, other_r, fixed, own_heat)
    wide = lax.axis_size("wide")
    from_before = lax.ppermute(edge, "wide", [(i, (i + 1) % wide) for i in range(wide)])
    from_after = lax.ppermute(edge, "wide", [((i + 1) % wide, i) for i in range(wide)])
    other_heat = swap(own_heat, "sub", [(0, 1)])
    heat, base = pl.pallas_call(
        base_kernel, out_shape=(tile(levels), tile(levels)), compiler_params=big, name="base"
    )(own_state, other_state, own_heat, other_heat, first_tend, second)
    new_state = pl.pallas_call(
        step_kernel, out_shape=tile(levels), compiler_params=big, name="step"
    )(base, span, kappa_strips, mine, from_before, from_after)
    return (heat, new_state)


def solution(mesh):
    in_specs = (
        P("lev", ("grp", "sub"), "wide"),
        P(("grp", "sub"), "wide"),
        P(None, "lev", ("grp", "sub"), "wide"),
        P("lev", ("grp", "sub"), "wide"),
        P(("grp", "sub"), "wide"),
        P(("grp", "sub"), "wide"),
        P(),
        P(),
    )
    out_specs = (P("lev", ("grp", "sub"), "wide"), P("lev", ("grp", "sub"), "wide"))
    return jax.shard_map(shards, mesh=mesh, in_specs=in_specs, out_specs=out_specs, check_vma=False)
```

```python
import math

import jax
import jax.numpy as jnp
import numpy as np
from jax import lax
from jax.experimental import pallas as pl
from jax.experimental.pallas import tpu as pltpu
from jax.sharding import PartitionSpec as P

time_step = 0.004
points = 4
strip = 2 * points
log2e = 1.4426950408889634
gll_weights = (1.0 / 6.0, 5.0 / 6.0, 5.0 / 6.0, 1.0 / 6.0)
mass_points = (1.0 / 3.0, 5.0 / 6.0, 5.0 / 6.0, 1.0 / 3.0)


def derivative_table():
    root_five = math.sqrt(5.0)
    outer_big = (5.0 + 5.0 * root_five) / 4.0
    outer_small = (5.0 * root_five - 5.0) / 4.0
    inner_big = (1.0 + root_five) / 4.0
    inner_mid = root_five / 2.0
    inner_small = (root_five - 1.0) / 4.0
    return np.array(
        [
            [-3.0, outer_big, -outer_small, 0.5],
            [-inner_big, 0.0, inner_mid, -inner_small],
            [inner_small, -inner_mid, 0.0, inner_big],
            [-0.5, outer_small, -outer_big, 3.0],
        ]
    )


table = derivative_table()


def by_node(node, values):
    out = jnp.full(node.shape, values[3], jnp.float32)
    for i in (2, 1, 0):
        out = jnp.where(node == i, jnp.float32(values[i]), out)
    return out


class Stencil:
    def __init__(self, rows, width):
        self.shape = (rows, width)
        self.row = lax.broadcasted_iota(jnp.int32, (rows, width), 0)
        self.lane = lax.broadcasted_iota(jnp.int32, (rows, width), 1)
        node_y, node_x = self.row % points, self.lane % points
        self.nodes = (node_y, node_x)
        self.weight_x = by_node(node_x, gll_weights)
        self.weight_y = by_node(node_y, gll_weights)
        self.inv_mass_y = by_node(node_y, [1.0 / m for m in mass_points])
        self.inv_mass = self.inv_mass_y * by_node(node_x, [1.0 / m for m in mass_points])
        inner_first = (node_x == 0) & (self.lane > 0)
        inner_last = (node_x == points - 1) & (self.lane < width - 1)
        self.first_x = inner_first.astype(jnp.float32)
        self.last_x = inner_last.astype(jnp.float32)
        self.first_y = (node_y == 0).astype(jnp.float32)
        self.last_y = (node_y == points - 1).astype(jnp.float32)
        self.coefs = {}

    def coef(self, name, axis):
        if (name, axis) not in self.coefs:
            matrix = table if name == "d" else table.T
            self.coefs[name, axis] = [
                by_node(
                    self.nodes[axis],
                    [matrix[i, i + step] if 0 <= i + step < points else 0.0 for i in range(points)],
                )
                for step in range(-3, 4)
            ]
        return self.coefs[name, axis]

    def apply(self, name, axis, field):
        size = self.shape[axis]
        out = None
        for step, coef in zip(range(-3, 4), self.coef(name, axis)):
            moved = field if step == 0 else pltpu.roll(field, (-step) % size, field.ndim - 2 + axis)
            term = coef * moved
            out = term if out is None else out + term
        return out

    def residual(self, field, kappa):
        flux_x = kappa * self.weight_x * self.apply("d", 1, field)
        flux_y = kappa * self.weight_y * self.apply("d", 0, field)
        part_x = self.weight_y * self.apply("t", 1, flux_x)
        return -part_x - self.weight_x * self.apply("t", 0, flux_y)

    def rows_joined(self, own, other):
        rows = self.shape[0]
        axis = own.ndim - 2
        before = jnp.where(self.row == 0, pltpu.roll(other, 1, axis), pltpu.roll(own, 1, axis))
        after = jnp.where(
            self.row == rows - 1, pltpu.roll(other, rows - 1, axis), pltpu.roll(own, rows - 1, axis)
        )
        return own + self.first_y * before + self.last_y * after

    def columns_joined(self, field):
        width = self.shape[1]
        axis = field.ndim - 1
        before = pltpu.roll(field, 1, axis)
        after = pltpu.roll(field, width - 1, axis)
        return field + self.first_x * before + self.last_x * after


def to_strips(lane, start, values):
    width = lane.shape[1]
    for n, value in enumerate(values):
        if value is not None:
            moved = pltpu.roll(value, strip * n + points, 1)
            start = jnp.where(lane // strip == n, moved, start)
    return start


def split(value, pieces):
    out = []
    for _ in range(pieces):
        high = value.astype(jnp.bfloat16)
        out.append(high)
        value = value - high.astype(jnp.float32)
    return out


def fetch_kernel(*refs):
    air, diffusivity, absorber, thickness, zenith, lit, coef, weight = refs[:8]
    amount, state, absorber_out, thickness_out, zenith_out, lit_out, coef_out, weight_out, sems = refs[8:]
    levels = air.shape[0]
    copies = [
        pltpu.make_async_copy(absorber, absorber_out, sems.at[0]),
        pltpu.make_async_copy(air, state.at[pl.ds(0, levels)], sems.at[1]),
        pltpu.make_async_copy(diffusivity, state.at[levels], sems.at[2]),
        pltpu.make_async_copy(zenith, zenith_out, sems.at[3]),
        pltpu.make_async_copy(coef, coef_out, sems.at[4]),
        pltpu.make_async_copy(weight, weight_out, sems.at[5]),
        pltpu.make_async_copy(thickness, thickness_out, sems.at[6]),
        pltpu.make_async_copy(lit, lit_out, sems.at[7]),
    ]
    for copy in copies:
        copy.start()
    for copy in copies:
        copy.wait()
    for s in range(absorber_out.shape[0]):
        total = absorber_out[s, 0]
        for k in range(1, levels):
            total = total + absorber_out[s, k]
        amount[s] = total


def amount_rows(totals, scale, depth, ones):
    value = jnp.concatenate([t * scale for t in totals], axis=0)
    hi, mid, lo = (p.astype(jnp.float32) for p in split(value, 3))
    rest = depth - 4 * value.shape[0]
    index = lax.broadcasted_iota(jnp.int32, (rest, value.shape[1]), 0)
    tail = jnp.where(index < ones, 1.0, 0.0)
    return jnp.concatenate([hi, mid, lo, hi, tail], axis=0).astype(jnp.bfloat16)


def layers_kernel(absorber, zenith, coef, weight, left, drops, spread):
    species, levels, rows, width = absorber.shape
    terms = coef.shape[1]
    group = species * rows
    depth = left.shape[1]
    c_pieces = split(coef[...], 2)
    w_pieces = split(jnp.log2(weight[...]), 3)
    lane = lax.broadcasted_iota(jnp.int32, (rows, depth), 1)
    row = lax.broadcasted_iota(jnp.int32, (rows, depth), 0)
    ones_at = 4 * group
    stack = jnp.concatenate([p.astype(jnp.float32) for p in c_pieces + w_pieces], axis=0)
    count = stack.shape[0]
    pick_row = lax.broadcasted_iota(jnp.int32, (count, depth), 0)
    pick_lane = lax.broadcasted_iota(jnp.int32, (count, depth), 1)
    kind = pick_lane // group
    wanted = jnp.where(kind == 3, species, 0) + (pick_lane % group) // rows
    wanted = jnp.where(kind >= 4, 2 * species + pick_lane - ones_at, wanted)
    pick = (pick_row == wanted).astype(jnp.bfloat16)
    spread[...] = lax.dot_general(
        stack.astype(jnp.bfloat16),
        pick,
        (((0,), (0,)), ((), ())),
        preferred_element_type=jnp.float32,
    )
    mask = ((lane % rows == row) | (lane >= ones_at)).astype(jnp.float32)
    for g in range(0, terms, 2):
        pair = [jnp.broadcast_to(spread[pl.ds(g + i, 1), :], (rows, depth)) * mask for i in (0, 1)]
        left[pl.ds(g * rows, 2 * rows), :] = jnp.concatenate(pair, axis=0).astype(jnp.bfloat16)

    scale = -log2e / zenith[...]
    totals = [jnp.zeros((rows, width), jnp.float32)] * species
    blocks = []
    for k in range(levels + 1):
        if k:
            totals = [totals[s] + absorber[s, k - 1] for s in range(species)]
        blocks.append(amount_rows(totals, scale, depth, 3))
    right = jnp.concatenate(blocks, axis=1)
    chunk = 448
    for start in range(0, terms * rows, chunk):
        out = jnp.exp2(
            jnp.dot(left[pl.ds(start, chunk), :], right, preferred_element_type=jnp.float32)
        )
        for k in range(levels):
            drop = out[:, k * width : (k + 1) * width] - out[:, (k + 1) * width : (k + 2) * width]
            drops[k, pl.ds(start, chunk), :] = drop


def radiate_kernel(left, drops, upper, zenith, lit, thickness, heat):
    levels, rows, width = heat.shape
    depth = left.shape[1]
    species = upper.shape[0]
    zen = zenith[...]
    below = lax.axis_index("lev") > 0
    totals = [jnp.where(below, upper[s], 0.0) for s in range(species)]
    right = amount_rows(totals, -log2e / zen, depth, 0)
    lit_zenith = jnp.where(lit[...] == 1, zen, 0.0)
    factors = [lit_zenith / thickness[k] for k in range(levels)]
    chunk = 448
    zero = jnp.zeros((rows, width), jnp.float32)
    sums = [[zero, zero] for _ in range(levels)]
    for start in range(0, left.shape[0], chunk):
        above = jnp.exp2(
            jnp.dot(left[pl.ds(start, chunk), :], right, preferred_element_type=jnp.float32)
        )
        for n, at in enumerate(range(0, chunk, rows)):
            part = above[at : at + rows]
            for k in range(levels):
                drop = drops[k, pl.ds(start + at, rows), :]
                sums[k][n % 2] = sums[k][n % 2] + part * drop
    for k in range(levels):
        heat[k] = factors[k] * (sums[k][0] + sums[k][1])


def edge_kernel(own_heat, other_heat, second, kappa, fixed, edge):
    levels, rows, width = own_heat.shape
    stencil = Stencil(rows, width)
    heats = [own_heat[k] for k in range(levels)] + [None] * (8 - levels)
    heats = heats + [other_heat[k] for k in range(levels)]
    strips = to_strips(stencil.lane, jnp.zeros((rows, width), jnp.float32), heats)
    r = second[...] + stencil.residual(strips, kappa[...])
    joined = stencil.rows_joined(r, pltpu.roll(r, width // 2, 1))
    node = stencil.lane % strip
    edge[...] = jnp.where((node == points - 1) | (node == points), joined, fixed[...])


def tiles_of(field):
    gap = [None] * (8 - field.shape[0])
    return [t for n in range(2) for t in [field[l, n] for l in range(field.shape[0])] + gap]


def state_kernel(own_state, other_state, first_tend, second, span_out, second_strips, kappa_strips, fixed, mine):
    levels = own_state.shape[0] - 1
    rows, width = own_state.shape[1:]
    stencil = Stencil(rows, width)
    lane = stencil.lane
    zero = jnp.zeros((rows, width), jnp.float32)
    air = jnp.stack([own_state[:levels], other_state[:levels]], axis=1)
    kappa = jnp.stack([own_state[levels], other_state[levels]], axis=0)
    r = stencil.residual(air, kappa)
    joined = stencil.rows_joined(r, jnp.concatenate([r[:, 1:], r[:, :1]], axis=1))
    tend = stencil.inv_mass * stencil.columns_joined(joined)
    first_tend[...] = tend[:, 0]
    r = stencil.residual(tend, kappa)
    second[...] = r
    second_strips[...] = to_strips(lane, zero, tiles_of(r))
    left_side = lane < width // 2
    node_x = stencil.nodes[1]
    to_edge = jnp.where(left_side, by_node(node_x, table[:, 0]), by_node(node_x, table[:, 3]))
    span = stencil.apply("t", 1, kappa * stencil.weight_x * to_edge)
    in_edge = (lane < points) | (lane >= width - points)
    span = jnp.where(in_edge, span, 0.0)
    span_out[...] = span
    own = to_strips(lane, zero, tiles_of(joined))
    by_level = lambda field: to_strips(
        lane, zero, tiles_of(jnp.broadcast_to(field[None], (levels,) + field.shape))
    )
    kappa_edge = by_level(kappa)
    kappa_strips[...] = kappa_edge
    out = zero
    node = lane % strip
    for step, value in ((1, own), (2, by_level(span)), (3, kappa_edge)):
        out = jnp.where(node == points - 1 - step, pltpu.roll(value, width - step, 1), out)
        out = jnp.where(node == points + step, pltpu.roll(value, step, 1), out)
    fixed[...] = out
    change = stencil.inv_mass_y * (1.0 / mass_points[0]) * own
    mine[0] = change
    mine[1] = stencil.weight_y * stencil.apply("d", 0, change)


def base_kernel(own_state, other_state, own_heat, other_heat, first_tend, second, heat_out, base):
    levels, rows, width = own_heat.shape
    stencil = Stencil(rows, width)
    own = own_heat[...]
    heat_out[...] = own
    heat = jnp.stack([own, other_heat[...]], axis=1)
    kappa = jnp.stack([own_state[levels], other_state[levels]], axis=0)
    r = second[...] + stencil.residual(heat, kappa)
    joined = stencil.rows_joined(r[:, 0], r[:, 1])
    base[...] = (
        own_state[:levels]
        + time_step * (first_tend[...] + own)
        + (0.5 * time_step * time_step) * (stencil.inv_mass * stencil.columns_joined(joined))
    )


def step_kernel(base, span, kappa, mine, from_before, from_after, out):
    levels, rows, width = base.shape
    half = width // 2
    stencil = Stencil(rows, width)
    lane = stencil.lane
    before, after = from_before[...], from_after[...]
    at_first = lane % strip == points

    def of_mates(step):
        return jnp.where(at_first, pltpu.roll(before, step, 1), pltpu.roll(after, width - step, 1))

    change = stencil.inv_mass_y * (1.0 / mass_points[0]) * of_mates(2)
    flux = of_mates(4) * mine[1] + stencil.weight_y * kappa[...] * stencil.apply("d", 0, change)
    r = -gll_weights[0] * stencil.apply("t", 0, flux) - stencil.weight_y * of_mates(3) * mine[0]
    add = of_mates(1) + stencil.rows_joined(r, pltpu.roll(r, half, 1))
    edges = (lane == 0) | (lane == width - 1)

    def spread(tile, at):
        low = jnp.broadcast_to(tile[:, at + points : at + points + 1], (rows, width))
        high = jnp.broadcast_to(tile[:, at + points - 1 : at + points], (rows, width))
        return jnp.where(lane < half, low, high)

    for l in range(levels):
        changes = [spread(change, t * half + strip * l) for t in range(2)]
        r = [-stencil.weight_y * span[t] * changes[t] for t in range(2)]
        moved = stencil.columns_joined(stencil.rows_joined(r[0], r[1]))
        moved = moved + jnp.where(edges, spread(add, strip * l), 0.0)
        out[l] = (
            base[l]
            + time_step * jnp.where(edges, changes[0], 0.0)
            + (0.5 * time_step * time_step) * stencil.inv_mass * moved
        )


def swap(value, axis, pairs):
    route = [(a, b) for a, b in pairs] + [(b, a) for a, b in pairs]
    return lax.ppermute(value, axis, route)


def shards(
    air_state, diffusivity, absorber, thickness, cos_zenith, sunlit, absorb_coef, solar_weight
):
    levels, rows, width = air_state.shape
    terms = absorb_coef.shape[1]
    tile = lambda n: jax.ShapeDtypeStruct((n, rows, width), jnp.float32)
    big = pltpu.CompilerParams(vmem_limit_bytes=32 * 1024 * 1024)
    weight = solar_weight[None]
    args = (air_state, diffusivity, absorber, thickness, cos_zenith, sunlit, absorb_coef, weight)
    args = tuple(pltpu.with_memory_space_constraint(x, pltpu.HBM) for x in args)
    same = lambda x: jax.ShapeDtypeStruct(x.shape, x.dtype)
    amount, own_state, absorber, thickness, cos_zenith, sunlit, absorb_coef, weight = pl.pallas_call(
        fetch_kernel,
        out_shape=(tile(absorber.shape[0]), tile(levels + 1)) + tuple(same(x) for x in args[2:]),
        in_specs=[pl.BlockSpec(memory_space=pltpu.HBM)] * len(args),
        scratch_shapes=[pltpu.SemaphoreType.DMA((len(args),))],
        compiler_params=pltpu.CompilerParams(vmem_limit_bytes=32 * 1024 * 1024),
        name="fetch",
    )(*args)
    size = lax.axis_size("lev")
    lev = lax.axis_index("lev")
    upper = None
    for step in range(1, size):
        moved = lax.ppermute(amount, "lev", [(i, (i + step) % size) for i in range(size)])
        if size > 2:
            moved = jnp.where(lev >= step, moved, 0.0)
        upper = moved if upper is None else upper + moved
    if upper is None:
        upper = jnp.zeros_like(amount)
    other_state = swap(own_state, "sub", [(0, 1)])
    plane = jax.ShapeDtypeStruct((rows, width), jnp.float32)
    left, drops = pl.pallas_call(
        layers_kernel,
        out_shape=(
            jax.ShapeDtypeStruct((terms * rows, 256), jnp.bfloat16),
            jax.ShapeDtypeStruct((levels, terms * rows, width), jnp.float32),
        ),
        scratch_shapes=[pltpu.VMEM((terms, 256), jnp.float32)],
        compiler_params=big,
        name="layers",
    )(absorber, cos_zenith, absorb_coef, weight)
    own_heat = pl.pallas_call(
        radiate_kernel, out_shape=tile(levels), compiler_params=big, name="radiate"
    )(left, drops, upper, cos_zenith, sunlit, thickness)
    other_heat = swap(own_heat, "sub", [(0, 1)])
    pair = jax.ShapeDtypeStruct((levels, 2, rows, width), jnp.float32)
    first_tend, second, span, second_strips, kappa_strips, fixed, mine = pl.pallas_call(
        state_kernel,
        out_shape=(tile(levels), pair, tile(2), plane, plane, plane, tile(2)),
        compiler_params=big,
        name="state",
    )(own_state, other_state)
    edge = pl.pallas_call(edge_kernel, out_shape=plane, compiler_params=big, name="edges")(
        own_heat, other_heat, second_strips, kappa_strips, fixed
    )
    wide = lax.axis_size("wide")
    from_before = lax.ppermute(edge, "wide", [(i, (i + 1) % wide) for i in range(wide)])
    from_after = lax.ppermute(edge, "wide", [((i + 1) % wide, i) for i in range(wide)])
    heat, base = pl.pallas_call(
        base_kernel, out_shape=(tile(levels), tile(levels)), compiler_params=big, name="base"
    )(own_state, other_state, own_heat, other_heat, first_tend, second)
    new_state = pl.pallas_call(
        step_kernel, out_shape=tile(levels), compiler_params=big, name="step"
    )(base, span, kappa_strips, mine, from_before, from_after)
    return (heat, new_state)


def solution(mesh):
    in_specs = (
        P("lev", ("grp", "sub"), "wide"),
        P(("grp", "sub"), "wide"),
        P(None, "lev", ("grp", "sub"), "wide"),
        P("lev", ("grp", "sub"), "wide"),
        P(("grp", "sub"), "wide"),
        P(("grp", "sub"), "wide"),
        P(),
        P(),
    )
    out_specs = (P("lev", ("grp", "sub"), "wide"), P("lev", ("grp", "sub"), "wide"))
    return jax.shard_map(shards, mesh=mesh, in_specs=in_specs, out_specs=out_specs, check_vma=False)
```

```python
import functools
import math

import jax
import jax.numpy as jnp
import numpy as np
from jax import lax
from jax.experimental import pallas as pl
from jax.experimental.pallas import tpu as pltpu
from jax.sharding import PartitionSpec as P

time_step = 0.004
points = 4
strip = 2 * points
log2e = 1.4426950408889634
gll_weights = (1.0 / 6.0, 5.0 / 6.0, 5.0 / 6.0, 1.0 / 6.0)
mass_points = (1.0 / 3.0, 5.0 / 6.0, 5.0 / 6.0, 1.0 / 3.0)


def derivative_table():
    root_five = math.sqrt(5.0)
    outer_big = (5.0 + 5.0 * root_five) / 4.0
    outer_small = (5.0 * root_five - 5.0) / 4.0
    inner_big = (1.0 + root_five) / 4.0
    inner_mid = root_five / 2.0
    inner_small = (root_five - 1.0) / 4.0
    return np.array(
        [
            [-3.0, outer_big, -outer_small, 0.5],
            [-inner_big, 0.0, inner_mid, -inner_small],
            [inner_small, -inner_mid, 0.0, inner_big],
            [-0.5, outer_small, -outer_big, 3.0],
        ]
    )


table = derivative_table()


def by_node(node, values):
    out = jnp.full(node.shape, values[3], jnp.float32)
    for i in (2, 1, 0):
        out = jnp.where(node == i, jnp.float32(values[i]), out)
    return out


class Stencil:
    def __init__(self, rows, width):
        self.shape = (rows, width)
        self.row = lax.broadcasted_iota(jnp.int32, (rows, width), 0)
        self.lane = lax.broadcasted_iota(jnp.int32, (rows, width), 1)
        node_y, node_x = self.row % points, self.lane % points
        self.nodes = (node_y, node_x)
        self.weight_x = by_node(node_x, gll_weights)
        self.weight_y = by_node(node_y, gll_weights)
        self.inv_mass_y = by_node(node_y, [1.0 / m for m in mass_points])
        self.inv_mass = self.inv_mass_y * by_node(node_x, [1.0 / m for m in mass_points])
        inner_first = (node_x == 0) & (self.lane > 0)
        inner_last = (node_x == points - 1) & (self.lane < width - 1)
        self.first_x = inner_first.astype(jnp.float32)
        self.last_x = inner_last.astype(jnp.float32)
        self.first_y = (node_y == 0).astype(jnp.float32)
        self.last_y = (node_y == points - 1).astype(jnp.float32)
        self.coefs = {}

    def coef(self, name, axis):
        if (name, axis) not in self.coefs:
            matrix = table if name == "d" else table.T
            self.coefs[name, axis] = [
                by_node(
                    self.nodes[axis],
                    [matrix[i, i + step] if 0 <= i + step < points else 0.0 for i in range(points)],
                )
                for step in range(-3, 4)
            ]
        return self.coefs[name, axis]

    def apply(self, name, axis, field):
        size = self.shape[axis]
        out = None
        for step, coef in zip(range(-3, 4), self.coef(name, axis)):
            moved = field if step == 0 else pltpu.roll(field, (-step) % size, field.ndim - 2 + axis)
            term = coef * moved
            out = term if out is None else out + term
        return out

    def residual(self, field, kappa):
        flux_x = kappa * self.weight_x * self.apply("d", 1, field)
        flux_y = kappa * self.weight_y * self.apply("d", 0, field)
        part_x = self.weight_y * self.apply("t", 1, flux_x)
        return -part_x - self.weight_x * self.apply("t", 0, flux_y)

    def rows_joined(self, own, other):
        rows = self.shape[0]
        axis = own.ndim - 2
        before = jnp.where(self.row == 0, pltpu.roll(other, 1, axis), pltpu.roll(own, 1, axis))
        after = jnp.where(
            self.row == rows - 1, pltpu.roll(other, rows - 1, axis), pltpu.roll(own, rows - 1, axis)
        )
        return own + self.first_y * before + self.last_y * after

    def columns_joined(self, field):
        width = self.shape[1]
        axis = field.ndim - 1
        before = pltpu.roll(field, 1, axis)
        after = pltpu.roll(field, width - 1, axis)
        return field + self.first_x * before + self.last_x * after


def to_strips(lane, start, values):
    width = lane.shape[1]
    for n, value in enumerate(values):
        if value is not None:
            moved = pltpu.roll(value, strip * n + points, 1)
            start = jnp.where(lane // strip == n, moved, start)
    return start


def split(value, pieces):
    out = []
    for _ in range(pieces):
        high = value.astype(jnp.bfloat16)
        out.append(high)
        value = value - high.astype(jnp.float32)
    return out


def fetch_kernel(*refs):
    air, diffusivity, absorber, thickness, zenith, lit, coef, weight = refs[:8]
    amount, packet, absorber_out, thickness_out, zenith_out, lit_out, coef_out, weight_out = refs[8:16]
    packed, sems = refs[16:]
    levels = air.shape[0]
    copies = [
        pltpu.make_async_copy(absorber, absorber_out, sems.at[0]),
        pltpu.make_async_copy(air, packet.at[pl.ds(0, levels)], sems.at[1]),
        pltpu.make_async_copy(diffusivity, packet.at[levels], sems.at[2]),
        pltpu.make_async_copy(zenith, zenith_out, sems.at[3]),
        pltpu.make_async_copy(coef, coef_out, sems.at[4]),
        pltpu.make_async_copy(weight, weight_out, sems.at[5]),
        pltpu.make_async_copy(thickness, thickness_out, sems.at[6]),
        pltpu.make_async_copy(lit, lit_out, sems.at[7]),
    ]
    for copy in copies:
        copy.start()
    for copy in copies:
        copy.wait()
    species = absorber_out.shape[0]
    lane = lax.broadcasted_iota(jnp.int32, packed.shape, 1)
    zero = jnp.zeros(packed.shape, jnp.float32)
    raw = levels + 1
    totals = []
    for s in range(species):
        total = absorber_out[s, 0]
        sums = [None, total]
        for k in range(1, levels):
            total = total + absorber_out[s, k]
            sums.append(total)
        amount[s] = total
        totals.append(total)
        packet[raw + s] = to_strips(lane, zero, sums)
    packed[...] = to_strips(lane, zero, totals)
    zen = zenith_out[...]
    packet[raw + species] = to_strips(lane, zero - 1.0, [-log2e / zen] * (levels + 1))
    lit_zenith = jnp.where(lit_out[...] == 1, zen, 0.0)
    packet[raw + species + 1] = to_strips(
        lane, zero, [lit_zenith / thickness_out[k] for k in range(levels)]
    )


def amount_rows(totals, scale, depth, ones):
    value = jnp.concatenate([t * scale for t in totals], axis=0)
    hi, mid, lo = (p.astype(jnp.float32) for p in split(value, 3))
    rest = depth - 4 * value.shape[0]
    index = lax.broadcasted_iota(jnp.int32, (rest, value.shape[1]), 0)
    tail = jnp.where(index < ones, 1.0, 0.0)
    return jnp.concatenate([hi, mid, lo, hi, tail], axis=0).astype(jnp.bfloat16)


def layers_kernel(absorber, zenith, coef, weight, left, drops, spread):
    species, levels, rows, width = absorber.shape
    terms = coef.shape[1]
    group = species * rows
    depth = left.shape[1]
    c_pieces = split(coef[...], 2)
    w_pieces = split(jnp.log2(weight[...]), 3)
    lane = lax.broadcasted_iota(jnp.int32, (rows, depth), 1)
    row = lax.broadcasted_iota(jnp.int32, (rows, depth), 0)
    ones_at = 4 * group
    stack = jnp.concatenate([p.astype(jnp.float32) for p in c_pieces + w_pieces], axis=0)
    count = stack.shape[0]
    pick_row = lax.broadcasted_iota(jnp.int32, (count, depth), 0)
    pick_lane = lax.broadcasted_iota(jnp.int32, (count, depth), 1)
    kind = pick_lane // group
    wanted = jnp.where(kind == 3, species, 0) + (pick_lane % group) // rows
    wanted = jnp.where(kind >= 4, 2 * species + pick_lane - ones_at, wanted)
    pick = (pick_row == wanted).astype(jnp.bfloat16)
    spread[...] = lax.dot_general(
        stack.astype(jnp.bfloat16),
        pick,
        (((0,), (0,)), ((), ())),
        preferred_element_type=jnp.float32,
    )
    mask = ((lane % rows == row) | (lane >= ones_at)).astype(jnp.float32)
    for g in range(0, terms, 2):
        pair = [jnp.broadcast_to(spread[pl.ds(g + i, 1), :], (rows, depth)) * mask for i in (0, 1)]
        left[pl.ds(g * rows, 2 * rows), :] = jnp.concatenate(pair, axis=0).astype(jnp.bfloat16)

    scale = -log2e / zenith[...]
    totals = [jnp.zeros((rows, width), jnp.float32)] * species
    blocks = []
    for k in range(levels + 1):
        if k:
            totals = [totals[s] + absorber[s, k - 1] for s in range(species)]
        blocks.append(amount_rows(totals, scale, depth, 3))
    right = jnp.concatenate(blocks, axis=1)
    chunk = 448
    for start in range(0, terms * rows, chunk):
        out = jnp.exp2(
            jnp.dot(left[pl.ds(start, chunk), :], right, preferred_element_type=jnp.float32)
        )
        for k in range(levels):
            drop = out[:, k * width : (k + 1) * width] - out[:, (k + 1) * width : (k + 2) * width]
            drops[k, pl.ds(start, chunk), :] = drop


def radiate_kernel(left, drops, upper, zenith, lit, thickness, after, heat):
    levels, rows, width = heat.shape
    depth = left.shape[1]
    species = upper.shape[0]
    zen = zenith[...]
    below = lax.axis_index("lev") > 0
    totals = [jnp.where(below, upper[s], 0.0) for s in range(species)]
    right = amount_rows(totals, -log2e / zen, depth, 0)
    lit_zenith = jnp.where(lit[...] == 1, zen, 0.0)
    factors = [lit_zenith / thickness[k] for k in range(levels)]
    chunk = 448
    zero = jnp.zeros((rows, width), jnp.float32)
    sums = [[zero, zero] for _ in range(levels)]
    for start in range(0, left.shape[0], chunk):
        above = jnp.exp2(
            jnp.dot(left[pl.ds(start, chunk), :], right, preferred_element_type=jnp.float32)
        )
        for n, at in enumerate(range(0, chunk, rows)):
            part = above[at : at + rows]
            for k in range(levels):
                drop = drops[k, pl.ds(start + at, rows), :]
                sums[k][n % 2] = sums[k][n % 2] + part * drop
    for k in range(levels):
        heat[k] = factors[k] * (sums[k][0] + sums[k][1])


def sum_rows(value, rows):
    parts = [value[i : i + rows] for i in range(0, value.shape[0], rows)]
    sums = parts[:8]
    for i in range(8, len(parts)):
        sums[i % 8] = sums[i % 8] + parts[i]
    while len(sums) > 1:
        sums = [sum(sums[i : i + 2]) for i in range(0, len(sums), 2)]
    return sums[0]


def edge_kernel(levels, upper, upper_other, left, layers, factor, second, kappa, fixed, edge):
    species = upper.shape[0]
    rows, width = factor.shape
    half = width // 2
    stencil = Stencil(rows, width)
    lane = stencil.lane
    below = lax.axis_index("lev") > 0
    crossed = upper_other[...]
    totals = []
    for s in range(species):
        other = pltpu.roll(crossed, (half - strip * s) % width, 1)
        above = jnp.where(below & (lane < strip), pltpu.roll(upper[s], points, 1), 0.0)
        above = jnp.where(below & (lane >= half) & (lane < half + strip), other, above)
        total = layers[s] + above
        for k in range(1, levels + 1):
            total = total + pltpu.roll(above, strip * k, 1)
        totals.append(total)
    right = amount_rows(totals, layers[species], left.shape[1], 3)
    passed = jnp.exp2(jnp.dot(left[...], right, preferred_element_type=jnp.float32))
    passed = sum_rows(passed, rows)
    heat = factor[...] * (passed - pltpu.roll(passed, width - strip, 1))
    r = second[...] + stencil.residual(heat, kappa[...])
    joined = stencil.rows_joined(r, pltpu.roll(r, half, 1))
    node = lane % strip
    edge[...] = jnp.where((node == points - 1) | (node == points), joined, fixed[...])


def tiles_of(field):
    gap = [None] * (8 - field.shape[0])
    return [t for n in range(2) for t in [field[l, n] for l in range(field.shape[0])] + gap]


def state_kernel(
    own_state, other_state, first_tend, second, span_out, second_strips, kappa_strips, fixed, mine, layers, factor
):
    species = layers.shape[0] - 1
    levels = own_state.shape[0] - species - 3
    rows, width = own_state.shape[1:]
    stencil = Stencil(rows, width)
    lane = stencil.lane
    for i in range(species + 1):
        at = levels + 1 + i
        other = pltpu.roll(other_state[at], width // 2, 1)
        layers[i] = jnp.where(lane < width // 2, own_state[at], other)
    at = levels + species + 2
    factor[...] = own_state[at] + pltpu.roll(other_state[at], width // 2, 1)
    zero = jnp.zeros((rows, width), jnp.float32)
    air = jnp.stack([own_state[:levels], other_state[:levels]], axis=1)
    kappa = jnp.stack([own_state[levels], other_state[levels]], axis=0)
    r = stencil.residual(air, kappa)
    joined = stencil.rows_joined(r, jnp.concatenate([r[:, 1:], r[:, :1]], axis=1))
    tend = stencil.inv_mass * stencil.columns_joined(joined)
    first_tend[...] = tend[:, 0]
    r = stencil.residual(tend, kappa)
    second[...] = r
    second_strips[...] = to_strips(lane, zero, tiles_of(r))
    left_side = lane < width // 2
    node_x = stencil.nodes[1]
    to_edge = jnp.where(left_side, by_node(node_x, table[:, 0]), by_node(node_x, table[:, 3]))
    span = stencil.apply("t", 1, kappa * stencil.weight_x * to_edge)
    in_edge = (lane < points) | (lane >= width - points)
    span = jnp.where(in_edge, span, 0.0)
    span_out[...] = span
    own = to_strips(lane, zero, tiles_of(joined))
    by_level = lambda field: to_strips(
        lane, zero, tiles_of(jnp.broadcast_to(field[None], (levels,) + field.shape))
    )
    kappa_edge = by_level(kappa)
    kappa_strips[...] = kappa_edge
    out = zero
    node = lane % strip
    for step, value in ((1, own), (2, by_level(span)), (3, kappa_edge)):
        out = jnp.where(node == points - 1 - step, pltpu.roll(value, width - step, 1), out)
        out = jnp.where(node == points + step, pltpu.roll(value, step, 1), out)
    fixed[...] = out
    change = stencil.inv_mass_y * (1.0 / mass_points[0]) * own
    mine[0] = change
    mine[1] = stencil.weight_y * stencil.apply("d", 0, change)


def base_kernel(own_state, other_state, own_heat, other_heat, first_tend, second, base):
    levels, rows, width = own_heat.shape
    stencil = Stencil(rows, width)
    own = own_heat[...]
    heat = jnp.stack([own, other_heat[...]], axis=1)
    kappa = jnp.stack([own_state[levels], other_state[levels]], axis=0)
    r = second[...] + stencil.residual(heat, kappa)
    joined = stencil.rows_joined(r[:, 0], r[:, 1])
    base[...] = (
        own_state[:levels]
        + time_step * (first_tend[...] + own)
        + (0.5 * time_step * time_step) * (stencil.inv_mass * stencil.columns_joined(joined))
    )


def step_kernel(from_before, from_after, span, kappa, mine, base, heat, heat_out, out):
    levels, rows, width = base.shape
    half = width // 2
    stencil = Stencil(rows, width)
    lane = stencil.lane
    heat_out[...] = heat[...]
    before, after = from_before[...], from_after[...]
    at_first = lane % strip == points

    def of_mates(step):
        return jnp.where(at_first, pltpu.roll(before, step, 1), pltpu.roll(after, width - step, 1))

    change = stencil.inv_mass_y * (1.0 / mass_points[0]) * of_mates(2)
    flux = of_mates(4) * mine[1] + stencil.weight_y * kappa[...] * stencil.apply("d", 0, change)
    r = -gll_weights[0] * stencil.apply("t", 0, flux) - stencil.weight_y * of_mates(3) * mine[0]
    add = of_mates(1) + stencil.rows_joined(r, pltpu.roll(r, half, 1))
    edges = (lane == 0) | (lane == width - 1)

    def spread(tile, at):
        low = jnp.broadcast_to(tile[:, at + points : at + points + 1], (rows, width))
        high = jnp.broadcast_to(tile[:, at + points - 1 : at + points], (rows, width))
        return jnp.where(lane < half, low, high)

    for l in range(levels):
        changes = [spread(change, t * half + strip * l) for t in range(2)]
        r = [-stencil.weight_y * span[t] * changes[t] for t in range(2)]
        moved = stencil.columns_joined(stencil.rows_joined(r[0], r[1]))
        moved = moved + jnp.where(edges, spread(add, strip * l), 0.0)
        out[l] = (
            base[l]
            + time_step * jnp.where(edges, changes[0], 0.0)
            + (0.5 * time_step * time_step) * stencil.inv_mass * moved
        )


def swap(value, axis, pairs):
    route = [(a, b) for a, b in pairs] + [(b, a) for a, b in pairs]
    return lax.ppermute(value, axis, route)


def shards(
    air_state, diffusivity, absorber, thickness, cos_zenith, sunlit, absorb_coef, solar_weight
):
    levels, rows, width = air_state.shape
    terms = absorb_coef.shape[1]
    tile = lambda n: jax.ShapeDtypeStruct((n, rows, width), jnp.float32)
    big = pltpu.CompilerParams(vmem_limit_bytes=32 * 1024 * 1024)
    weight = solar_weight[None]
    args = (air_state, diffusivity, absorber, thickness, cos_zenith, sunlit, absorb_coef, weight)
    args = tuple(pltpu.with_memory_space_constraint(x, pltpu.HBM) for x in args)
    same = lambda x: jax.ShapeDtypeStruct(x.shape, x.dtype)
    plane = jax.ShapeDtypeStruct((rows, width), jnp.float32)
    fetched = pl.pallas_call(
        fetch_kernel,
        out_shape=(tile(absorber.shape[0]), tile(levels + absorber.shape[0] + 3)) + tuple(same(x) for x in args[2:])
        + (plane,),
        in_specs=[pl.BlockSpec(memory_space=pltpu.HBM)] * len(args),
        scratch_shapes=[pltpu.SemaphoreType.DMA((len(args),))],
        compiler_params=pltpu.CompilerParams(vmem_limit_bytes=32 * 1024 * 1024),
        name="fetch",
    )(*args)
    amount, packet, absorber, thickness, cos_zenith, sunlit, absorb_coef, weight, packed = fetched
    species = absorber.shape[0]
    size = lax.axis_size("lev")
    lev = lax.axis_index("lev")
    upper = upper_other = None
    for step in range(1, size):
        straight = [(i, (i + step) % size) for i in range(size)]
        crossed = [(2 * i + c, 2 * j + 1 - c) for i, j in straight for c in range(2)]
        moved = lax.ppermute(amount, "lev", straight)
        moved_other = lax.ppermute(packed, ("lev", "sub"), crossed)
        if size > 2:
            moved = jnp.where(lev >= step, moved, 0.0)
            moved_other = jnp.where(lev >= step, moved_other, 0.0)
        upper = moved if upper is None else upper + moved
        upper_other = moved_other if upper_other is None else upper_other + moved_other
    if upper is None:
        upper, upper_other = jnp.zeros_like(amount), jnp.zeros_like(packed)
    other_packet = swap(packet, "sub", [(0, 1)])
    left, drops = pl.pallas_call(
        layers_kernel,
        out_shape=(
            jax.ShapeDtypeStruct((terms * rows, 256), jnp.bfloat16),
            jax.ShapeDtypeStruct((levels, terms * rows, width), jnp.float32),
        ),
        scratch_shapes=[pltpu.VMEM((terms, 256), jnp.float32)],
        compiler_params=big,
        name="layers",
    )(absorber, cos_zenith, absorb_coef, weight)
    pair = jax.ShapeDtypeStruct((levels, 2, rows, width), jnp.float32)
    first_tend, second, span, second_strips, kappa_strips, fixed, mine, strips, factor = pl.pallas_call(
        state_kernel,
        out_shape=(tile(levels), pair, tile(2), plane, plane, plane, tile(2), tile(species + 1), plane),
        compiler_params=big,
        name="state",
    )(packet, other_packet)
    edge = pl.pallas_call(
        functools.partial(edge_kernel, levels), out_shape=plane, compiler_params=big, name="edges"
    )(upper, upper_other, left, strips, factor, second_strips, kappa_strips, fixed)
    wide = lax.axis_size("wide")
    from_before = lax.ppermute(edge, "wide", [(i, (i + 1) % wide) for i in range(wide)])
    from_after = lax.ppermute(edge, "wide", [((i + 1) % wide, i) for i in range(wide)])
    own_heat = pl.pallas_call(
        radiate_kernel, out_shape=tile(levels), compiler_params=big, name="radiate"
    )(left, drops, upper, cos_zenith, sunlit, thickness, edge)
    other_heat = swap(own_heat, "sub", [(0, 1)])
    base = pl.pallas_call(
        base_kernel, out_shape=tile(levels), compiler_params=big, name="base"
    )(packet, other_packet, own_heat, other_heat, first_tend, second)
    heat, new_state = pl.pallas_call(
        step_kernel, out_shape=(tile(levels), tile(levels)), compiler_params=big, name="step"
    )(from_before, from_after, span, kappa_strips, mine, base, own_heat)
    return (heat, new_state)


def solution(mesh):
    in_specs = (
        P("lev", ("grp", "sub"), "wide"),
        P(("grp", "sub"), "wide"),
        P(None, "lev", ("grp", "sub"), "wide"),
        P("lev", ("grp", "sub"), "wide"),
        P(("grp", "sub"), "wide"),
        P(("grp", "sub"), "wide"),
        P(),
        P(),
    )
    out_specs = (P("lev", ("grp", "sub"), "wide"), P("lev", ("grp", "sub"), "wide"))
    return jax.shard_map(shards, mesh=mesh, in_specs=in_specs, out_specs=out_specs, check_vma=False)
```

```python
import math

import jax
import jax.numpy as jnp
import numpy as np
from jax import lax
from jax.experimental import pallas as pl
from jax.experimental.pallas import tpu as pltpu
from jax.sharding import PartitionSpec as P

time_step = 0.004
points = 4
strip = 2 * points
log2e = 1.4426950408889634
gll_weights = (1.0 / 6.0, 5.0 / 6.0, 5.0 / 6.0, 1.0 / 6.0)
mass_points = (1.0 / 3.0, 5.0 / 6.0, 5.0 / 6.0, 1.0 / 3.0)


def derivative_table():
    root_five = math.sqrt(5.0)
    outer_big = (5.0 + 5.0 * root_five) / 4.0
    outer_small = (5.0 * root_five - 5.0) / 4.0
    inner_big = (1.0 + root_five) / 4.0
    inner_mid = root_five / 2.0
    inner_small = (root_five - 1.0) / 4.0
    return np.array(
        [
            [-3.0, outer_big, -outer_small, 0.5],
            [-inner_big, 0.0, inner_mid, -inner_small],
            [inner_small, -inner_mid, 0.0, inner_big],
            [-0.5, outer_small, -outer_big, 3.0],
        ]
    )


table = derivative_table()


def by_node(node, values):
    out = jnp.full(node.shape, values[3], jnp.float32)
    for i in (2, 1, 0):
        out = jnp.where(node == i, jnp.float32(values[i]), out)
    return out


class Stencil:
    def __init__(self, rows, width):
        self.shape = (rows, width)
        self.row = lax.broadcasted_iota(jnp.int32, (rows, width), 0)
        self.lane = lax.broadcasted_iota(jnp.int32, (rows, width), 1)
        node_y, node_x = self.row % points, self.lane % points
        self.nodes = (node_y, node_x)
        self.weight_x = by_node(node_x, gll_weights)
        self.weight_y = by_node(node_y, gll_weights)
        self.inv_mass_y = by_node(node_y, [1.0 / m for m in mass_points])
        self.inv_mass = self.inv_mass_y * by_node(node_x, [1.0 / m for m in mass_points])
        inner_first = (node_x == 0) & (self.lane > 0)
        inner_last = (node_x == points - 1) & (self.lane < width - 1)
        self.first_x = inner_first.astype(jnp.float32)
        self.last_x = inner_last.astype(jnp.float32)
        self.first_y = (node_y == 0).astype(jnp.float32)
        self.last_y = (node_y == points - 1).astype(jnp.float32)
        self.coefs = {}

    def coef(self, name, axis):
        if (name, axis) not in self.coefs:
            matrix = table if name == "d" else table.T
            self.coefs[name, axis] = [
                by_node(
                    self.nodes[axis],
                    [matrix[i, i + step] if 0 <= i + step < points else 0.0 for i in range(points)],
                )
                for step in range(-3, 4)
            ]
        return self.coefs[name, axis]

    def apply(self, name, axis, field):
        size = self.shape[axis]
        out = None
        for step, coef in zip(range(-3, 4), self.coef(name, axis)):
            moved = field if step == 0 else pltpu.roll(field, (-step) % size, field.ndim - 2 + axis)
            term = coef * moved
            out = term if out is None else out + term
        return out

    def residual(self, field, kappa):
        flux_x = kappa * self.weight_x * self.apply("d", 1, field)
        flux_y = kappa * self.weight_y * self.apply("d", 0, field)
        part_x = self.weight_y * self.apply("t", 1, flux_x)
        return -part_x - self.weight_x * self.apply("t", 0, flux_y)

    def rows_joined(self, own, other):
        rows = self.shape[0]
        axis = own.ndim - 2
        before = jnp.where(self.row == 0, pltpu.roll(other, 1, axis), pltpu.roll(own, 1, axis))
        after = jnp.where(
            self.row == rows - 1, pltpu.roll(other, rows - 1, axis), pltpu.roll(own, rows - 1, axis)
        )
        return own + self.first_y * before + self.last_y * after

    def columns_joined(self, field):
        width = self.shape[1]
        axis = field.ndim - 1
        before = pltpu.roll(field, 1, axis)
        after = pltpu.roll(field, width - 1, axis)
        return field + self.first_x * before + self.last_x * after


def to_strips(lane, start, values):
    width = lane.shape[1]
    for n, value in enumerate(values):
        if value is not None:
            moved = pltpu.roll(value, strip * n + points, 1)
            start = jnp.where(lane // strip == n, moved, start)
    return start


def split(value, pieces):
    out = []
    for _ in range(pieces):
        high = value.astype(jnp.bfloat16)
        out.append(high)
        value = value - high.astype(jnp.float32)
    return out


def fetch_kernel(*refs):
    air, diffusivity, absorber, thickness, zenith, lit, coef, weight = refs[:8]
    amount, state, absorber_out, thickness_out, zenith_out, lit_out, coef_out, weight_out, sems = refs[8:]
    levels = air.shape[0]
    species = absorber.shape[0]
    layers = [
        pltpu.make_async_copy(absorber.at[s], absorber_out.at[s], sems.at[8 + s])
        for s in range(species)
    ]
    copies = [
        pltpu.make_async_copy(air, state.at[pl.ds(0, levels)], sems.at[1]),
        pltpu.make_async_copy(diffusivity, state.at[levels], sems.at[2]),
        pltpu.make_async_copy(zenith, zenith_out, sems.at[3]),
        pltpu.make_async_copy(coef, coef_out, sems.at[4]),
        pltpu.make_async_copy(weight, weight_out, sems.at[5]),
        pltpu.make_async_copy(thickness, thickness_out, sems.at[6]),
        pltpu.make_async_copy(lit, lit_out, sems.at[7]),
    ]
    for copy in layers + copies:
        copy.start()
    for s in range(species):
        layers[s].wait()
        total = absorber_out[s, 0]
        for k in range(1, levels):
            total = total + absorber_out[s, k]
        amount[s] = total
    for copy in copies:
        copy.wait()


def amount_rows(totals, scale, depth, ones):
    value = jnp.concatenate([t * scale for t in totals], axis=0)
    hi, mid, lo = (p.astype(jnp.float32) for p in split(value, 3))
    rest = depth - 4 * value.shape[0]
    index = lax.broadcasted_iota(jnp.int32, (rest, value.shape[1]), 0)
    tail = jnp.where(index < ones, 1.0, 0.0)
    return jnp.concatenate([hi, mid, lo, hi, tail], axis=0).astype(jnp.bfloat16)


def layers_kernel(absorber, zenith, coef, weight, left, drops, spread):
    species, levels, rows, width = absorber.shape
    terms = coef.shape[1]
    group = species * rows
    depth = left.shape[1]
    c_pieces = split(coef[...], 2)
    w_pieces = split(jnp.log2(weight[...]), 3)
    lane = lax.broadcasted_iota(jnp.int32, (rows, depth), 1)
    row = lax.broadcasted_iota(jnp.int32, (rows, depth), 0)
    ones_at = 4 * group
    stack = jnp.concatenate([p.astype(jnp.float32) for p in c_pieces + w_pieces], axis=0)
    count = stack.shape[0]
    pick_row = lax.broadcasted_iota(jnp.int32, (count, depth), 0)
    pick_lane = lax.broadcasted_iota(jnp.int32, (count, depth), 1)
    kind = pick_lane // group
    wanted = jnp.where(kind == 3, species, 0) + (pick_lane % group) // rows
    wanted = jnp.where(kind >= 4, 2 * species + pick_lane - ones_at, wanted)
    pick = (pick_row == wanted).astype(jnp.bfloat16)
    spread[...] = lax.dot_general(
        stack.astype(jnp.bfloat16),
        pick,
        (((0,), (0,)), ((), ())),
        preferred_element_type=jnp.float32,
    )
    mask = ((lane % rows == row) | (lane >= ones_at)).astype(jnp.float32)
    for g in range(0, terms, 2):
        pair = [jnp.broadcast_to(spread[pl.ds(g + i, 1), :], (rows, depth)) * mask for i in (0, 1)]
        left[pl.ds(g * rows, 2 * rows), :] = jnp.concatenate(pair, axis=0).astype(jnp.bfloat16)

    scale = -log2e / zenith[...]
    totals = [jnp.zeros((rows, width), jnp.float32)] * species
    blocks = []
    for k in range(levels + 1):
        if k:
            totals = [totals[s] + absorber[s, k - 1] for s in range(species)]
        blocks.append(amount_rows(totals, scale, depth, 3))
    right = jnp.concatenate(blocks, axis=1)
    chunk = 448
    for start in range(0, terms * rows, chunk):
        out = jnp.exp2(
            jnp.dot(left[pl.ds(start, chunk), :], right, preferred_element_type=jnp.float32)
        )
        for k in range(levels):
            drop = out[:, k * width : (k + 1) * width] - out[:, (k + 1) * width : (k + 2) * width]
            drops[k, pl.ds(start, chunk), :] = drop


def radiate_kernel(left, drops, upper, zenith, lit, thickness, heat):
    levels, rows, width = heat.shape
    depth = left.shape[1]
    species = upper.shape[0]
    zen = zenith[...]
    below = lax.axis_index("lev") > 0
    totals = [jnp.where(below, upper[s], 0.0) for s in range(species)]
    right = amount_rows(totals, -log2e / zen, depth, 0)
    lit_zenith = jnp.where(lit[...] == 1, zen, 0.0)
    factors = [lit_zenith / thickness[k] for k in range(levels)]
    chunk = 448
    zero = jnp.zeros((rows, width), jnp.float32)
    sums = [[zero, zero] for _ in range(levels)]
    for start in range(0, left.shape[0], chunk):
        above = jnp.exp2(
            jnp.dot(left[pl.ds(start, chunk), :], right, preferred_element_type=jnp.float32)
        )
        for n, at in enumerate(range(0, chunk, rows)):
            part = above[at : at + rows]
            for k in range(levels):
                drop = drops[k, pl.ds(start + at, rows), :]
                sums[k][n % 2] = sums[k][n % 2] + part * drop
    for k in range(levels):
        heat[k] = factors[k] * (sums[k][0] + sums[k][1])


def edge_kernel(own_heat, other_heat, second, kappa, fixed, edge):
    levels, rows, width = own_heat.shape
    stencil = Stencil(rows, width)
    heats = [own_heat[k] for k in range(levels)] + [None] * (8 - levels)
    heats = heats + [other_heat[k] for k in range(levels)]
    strips = to_strips(stencil.lane, jnp.zeros((rows, width), jnp.float32), heats)
    r = second[...] + stencil.residual(strips, kappa[...])
    joined = stencil.rows_joined(r, pltpu.roll(r, width // 2, 1))
    node = stencil.lane % strip
    edge[...] = jnp.where((node == points - 1) | (node == points), joined, fixed[...])


def tiles_of(field):
    gap = [None] * (8 - field.shape[0])
    return [t for n in range(2) for t in [field[l, n] for l in range(field.shape[0])] + gap]


def state_kernel(own_state, other_state, first_tend, second, span_out, second_strips, kappa_strips, fixed, mine):
    levels = own_state.shape[0] - 1
    rows, width = own_state.shape[1:]
    stencil = Stencil(rows, width)
    lane = stencil.lane
    zero = jnp.zeros((rows, width), jnp.float32)
    air = jnp.stack([own_state[:levels], other_state[:levels]], axis=1)
    kappa = jnp.stack([own_state[levels], other_state[levels]], axis=0)
    r = stencil.residual(air, kappa)
    joined = stencil.rows_joined(r, jnp.concatenate([r[:, 1:], r[:, :1]], axis=1))
    tend = stencil.inv_mass * stencil.columns_joined(joined)
    first_tend[...] = tend[:, 0]
    r = stencil.residual(tend, kappa)
    second[...] = r
    second_strips[...] = to_strips(lane, zero, tiles_of(r))
    left_side = lane < width // 2
    node_x = stencil.nodes[1]
    to_edge = jnp.where(left_side, by_node(node_x, table[:, 0]), by_node(node_x, table[:, 3]))
    span = stencil.apply("t", 1, kappa * stencil.weight_x * to_edge)
    in_edge = (lane < points) | (lane >= width - points)
    span = jnp.where(in_edge, span, 0.0)
    span_out[...] = span
    own = to_strips(lane, zero, tiles_of(joined))
    by_level = lambda field: to_strips(
        lane, zero, tiles_of(jnp.broadcast_to(field[None], (levels,) + field.shape))
    )
    kappa_edge = by_level(kappa)
    kappa_strips[...] = kappa_edge
    out = zero
    node = lane % strip
    for step, value in ((1, own), (2, by_level(span)), (3, kappa_edge)):
        out = jnp.where(node == points - 1 - step, pltpu.roll(value, width - step, 1), out)
        out = jnp.where(node == points + step, pltpu.roll(value, step, 1), out)
    fixed[...] = out
    change = stencil.inv_mass_y * (1.0 / mass_points[0]) * own
    mine[0] = change
    mine[1] = stencil.weight_y * stencil.apply("d", 0, change)


def base_kernel(own_state, other_state, own_heat, other_heat, first_tend, second, heat_out, base):
    levels, rows, width = own_heat.shape
    stencil = Stencil(rows, width)
    own = own_heat[...]
    heat_out[...] = own
    heat = jnp.stack([own, other_heat[...]], axis=1)
    kappa = jnp.stack([own_state[levels], other_state[levels]], axis=0)
    r = second[...] + stencil.residual(heat, kappa)
    joined = stencil.rows_joined(r[:, 0], r[:, 1])
    base[...] = (
        own_state[:levels]
        + time_step * (first_tend[...] + own)
        + (0.5 * time_step * time_step) * (stencil.inv_mass * stencil.columns_joined(joined))
    )


def step_kernel(base, span, kappa, mine, from_before, from_after, out):
    levels, rows, width = base.shape
    half = width // 2
    stencil = Stencil(rows, width)
    lane = stencil.lane
    before, after = from_before[...], from_after[...]
    at_first = lane % strip == points

    def of_mates(step):
        return jnp.where(at_first, pltpu.roll(before, step, 1), pltpu.roll(after, width - step, 1))

    change = stencil.inv_mass_y * (1.0 / mass_points[0]) * of_mates(2)
    flux = of_mates(4) * mine[1] + stencil.weight_y * kappa[...] * stencil.apply("d", 0, change)
    r = -gll_weights[0] * stencil.apply("t", 0, flux) - stencil.weight_y * of_mates(3) * mine[0]
    add = of_mates(1) + stencil.rows_joined(r, pltpu.roll(r, half, 1))
    edges = (lane == 0) | (lane == width - 1)

    def spread(tile, at):
        low = jnp.broadcast_to(tile[:, at + points : at + points + 1], (rows, width))
        high = jnp.broadcast_to(tile[:, at + points - 1 : at + points], (rows, width))
        return jnp.where(lane < half, low, high)

    for l in range(levels):
        changes = [spread(change, t * half + strip * l) for t in range(2)]
        r = [-stencil.weight_y * span[t] * changes[t] for t in range(2)]
        moved = stencil.columns_joined(stencil.rows_joined(r[0], r[1]))
        moved = moved + jnp.where(edges, spread(add, strip * l), 0.0)
        out[l] = (
            base[l]
            + time_step * jnp.where(edges, changes[0], 0.0)
            + (0.5 * time_step * time_step) * stencil.inv_mass * moved
        )


def swap(value, axis, pairs):
    route = [(a, b) for a, b in pairs] + [(b, a) for a, b in pairs]
    return lax.ppermute(value, axis, route)


def shards(
    air_state, diffusivity, absorber, thickness, cos_zenith, sunlit, absorb_coef, solar_weight
):
    levels, rows, width = air_state.shape
    terms = absorb_coef.shape[1]
    tile = lambda n: jax.ShapeDtypeStruct((n, rows, width), jnp.float32)
    big = pltpu.CompilerParams(vmem_limit_bytes=32 * 1024 * 1024)
    weight = solar_weight[None]
    args = (air_state, diffusivity, absorber, thickness, cos_zenith, sunlit, absorb_coef, weight)
    args = tuple(pltpu.with_memory_space_constraint(x, pltpu.HBM) for x in args)
    same = lambda x: jax.ShapeDtypeStruct(x.shape, x.dtype)
    amount, own_state, absorber, thickness, cos_zenith, sunlit, absorb_coef, weight = pl.pallas_call(
        fetch_kernel,
        out_shape=(tile(absorber.shape[0]), tile(levels + 1)) + tuple(same(x) for x in args[2:]),
        in_specs=[pl.BlockSpec(memory_space=pltpu.HBM)] * len(args),
        scratch_shapes=[pltpu.SemaphoreType.DMA((len(args) + absorber.shape[0],))],
        compiler_params=pltpu.CompilerParams(vmem_limit_bytes=32 * 1024 * 1024),
        name="fetch",
    )(*args)
    size = lax.axis_size("lev")
    lev = lax.axis_index("lev")
    upper = None
    for step in range(1, size):
        moved = lax.ppermute(amount, "lev", [(i, (i + step) % size) for i in range(size)])
        if size > 2:
            moved = jnp.where(lev >= step, moved, 0.0)
        upper = moved if upper is None else upper + moved
    if upper is None:
        upper = jnp.zeros_like(amount)
    other_state = swap(own_state, "sub", [(0, 1)])
    plane = jax.ShapeDtypeStruct((rows, width), jnp.float32)
    left, drops = pl.pallas_call(
        layers_kernel,
        out_shape=(
            jax.ShapeDtypeStruct((terms * rows, 256), jnp.bfloat16),
            jax.ShapeDtypeStruct((levels, terms * rows, width), jnp.float32),
        ),
        scratch_shapes=[pltpu.VMEM((terms, 256), jnp.float32)],
        compiler_params=big,
        name="layers",
    )(absorber, cos_zenith, absorb_coef, weight)
    own_heat = pl.pallas_call(
        radiate_kernel, out_shape=tile(levels), compiler_params=big, name="radiate"
    )(left, drops, upper, cos_zenith, sunlit, thickness)
    other_heat = swap(own_heat, "sub", [(0, 1)])
    pair = jax.ShapeDtypeStruct((levels, 2, rows, width), jnp.float32)
    first_tend, second, span, second_strips, kappa_strips, fixed, mine = pl.pallas_call(
        state_kernel,
        out_shape=(tile(levels), pair, tile(2), plane, plane, plane, tile(2)),
        compiler_params=big,
        name="state",
    )(own_state, other_state)
    edge = pl.pallas_call(edge_kernel, out_shape=plane, compiler_params=big, name="edges")(
        own_heat, other_heat, second_strips, kappa_strips, fixed
    )
    wide = lax.axis_size("wide")
    from_before = lax.ppermute(edge, "wide", [(i, (i + 1) % wide) for i in range(wide)])
    from_after = lax.ppermute(edge, "wide", [((i + 1) % wide, i) for i in range(wide)])
    heat, base = pl.pallas_call(
        base_kernel, out_shape=(tile(levels), tile(levels)), compiler_params=big, name="base"
    )(own_state, other_state, own_heat, other_heat, first_tend, second)
    new_state = pl.pallas_call(
        step_kernel, out_shape=tile(levels), compiler_params=big, name="step"
    )(base, span, kappa_strips, mine, from_before, from_after)
    return (heat, new_state)


def solution(mesh):
    in_specs = (
        P("lev", ("grp", "sub"), "wide"),
        P(("grp", "sub"), "wide"),
        P(None, "lev", ("grp", "sub"), "wide"),
        P("lev", ("grp", "sub"), "wide"),
        P(("grp", "sub"), "wide"),
        P(("grp", "sub"), "wide"),
        P(),
        P(),
    )
    out_specs = (P("lev", ("grp", "sub"), "wide"), P("lev", ("grp", "sub"), "wide"))
    return jax.shard_map(shards, mesh=mesh, in_specs=in_specs, out_specs=out_specs, check_vma=False)
```

```python
import math

import jax
import jax.numpy as jnp
import numpy as np
from jax import lax
from jax.experimental import pallas as pl
from jax.experimental.pallas import tpu as pltpu
from jax.sharding import PartitionSpec as P

time_step = 0.004
points = 4
strip = 2 * points
log2e = 1.4426950408889634
gll_weights = (1.0 / 6.0, 5.0 / 6.0, 5.0 / 6.0, 1.0 / 6.0)
mass_points = (1.0 / 3.0, 5.0 / 6.0, 5.0 / 6.0, 1.0 / 3.0)


def derivative_table():
    root_five = math.sqrt(5.0)
    outer_big = (5.0 + 5.0 * root_five) / 4.0
    outer_small = (5.0 * root_five - 5.0) / 4.0
    inner_big = (1.0 + root_five) / 4.0
    inner_mid = root_five / 2.0
    inner_small = (root_five - 1.0) / 4.0
    return np.array(
        [
            [-3.0, outer_big, -outer_small, 0.5],
            [-inner_big, 0.0, inner_mid, -inner_small],
            [inner_small, -inner_mid, 0.0, inner_big],
            [-0.5, outer_small, -outer_big, 3.0],
        ]
    )


table = derivative_table()


def by_node(node, values):
    out = jnp.full(node.shape, values[3], jnp.float32)
    for i in (2, 1, 0):
        out = jnp.where(node == i, jnp.float32(values[i]), out)
    return out


class Stencil:
    def __init__(self, rows, width):
        self.shape = (rows, width)
        self.row = lax.broadcasted_iota(jnp.int32, (rows, width), 0)
        self.lane = lax.broadcasted_iota(jnp.int32, (rows, width), 1)
        node_y, node_x = self.row % points, self.lane % points
        self.nodes = (node_y, node_x)
        self.weight_x = by_node(node_x, gll_weights)
        self.weight_y = by_node(node_y, gll_weights)
        self.inv_mass_y = by_node(node_y, [1.0 / m for m in mass_points])
        self.inv_mass = self.inv_mass_y * by_node(node_x, [1.0 / m for m in mass_points])
        inner_first = (node_x == 0) & (self.lane > 0)
        inner_last = (node_x == points - 1) & (self.lane < width - 1)
        self.first_x = inner_first.astype(jnp.float32)
        self.last_x = inner_last.astype(jnp.float32)
        self.first_y = (node_y == 0).astype(jnp.float32)
        self.last_y = (node_y == points - 1).astype(jnp.float32)
        self.coefs = {}

    def coef(self, name, axis):
        if (name, axis) not in self.coefs:
            matrix = table if name == "d" else table.T
            self.coefs[name, axis] = [
                by_node(
                    self.nodes[axis],
                    [matrix[i, i + step] if 0 <= i + step < points else 0.0 for i in range(points)],
                )
                for step in range(-3, 4)
            ]
        return self.coefs[name, axis]

    def apply(self, name, axis, field):
        size = self.shape[axis]
        out = None
        for step, coef in zip(range(-3, 4), self.coef(name, axis)):
            moved = field if step == 0 else pltpu.roll(field, (-step) % size, field.ndim - 2 + axis)
            term = coef * moved
            out = term if out is None else out + term
        return out

    def residual(self, field, kappa):
        flux_x = kappa * self.weight_x * self.apply("d", 1, field)
        flux_y = kappa * self.weight_y * self.apply("d", 0, field)
        part_x = self.weight_y * self.apply("t", 1, flux_x)
        return -part_x - self.weight_x * self.apply("t", 0, flux_y)

    def rows_joined(self, own, other):
        rows = self.shape[0]
        axis = own.ndim - 2
        before = jnp.where(self.row == 0, pltpu.roll(other, 1, axis), pltpu.roll(own, 1, axis))
        after = jnp.where(
            self.row == rows - 1, pltpu.roll(other, rows - 1, axis), pltpu.roll(own, rows - 1, axis)
        )
        return own + self.first_y * before + self.last_y * after

    def columns_joined(self, field):
        width = self.shape[1]
        axis = field.ndim - 1
        before = pltpu.roll(field, 1, axis)
        after = pltpu.roll(field, width - 1, axis)
        return field + self.first_x * before + self.last_x * after


def to_strips(lane, start, values):
    width = lane.shape[1]
    for n, value in enumerate(values):
        if value is not None:
            moved = pltpu.roll(value, strip * n + points, 1)
            start = jnp.where(lane // strip == n, moved, start)
    return start


def split(value, pieces):
    out = []
    for _ in range(pieces):
        high = value.astype(jnp.bfloat16)
        out.append(high)
        value = value - high.astype(jnp.float32)
    return out


def fetch_kernel(*refs):
    air, diffusivity, absorber, thickness, zenith, lit, coef, weight = refs[:8]
    amount, state, absorber_out, thickness_out, zenith_out, lit_out, coef_out, weight_out, sems = refs[8:]
    levels = air.shape[0]
    copies = [
        pltpu.make_async_copy(absorber, absorber_out, sems.at[0]),
        pltpu.make_async_copy(air, state.at[pl.ds(0, levels)], sems.at[1]),
        pltpu.make_async_copy(diffusivity, state.at[levels], sems.at[2]),
        pltpu.make_async_copy(zenith, zenith_out, sems.at[3]),
        pltpu.make_async_copy(coef, coef_out, sems.at[4]),
        pltpu.make_async_copy(weight, weight_out, sems.at[5]),
        pltpu.make_async_copy(thickness, thickness_out, sems.at[6]),
        pltpu.make_async_copy(lit, lit_out, sems.at[7]),
    ]
    for copy in copies:
        copy.start()
    for copy in copies:
        copy.wait()
    for s in range(absorber_out.shape[0]):
        total = absorber_out[s, 0]
        for k in range(1, levels):
            total = total + absorber_out[s, k]
        amount[s] = total


def amount_rows(totals, scale, depth, ones):
    value = jnp.concatenate([t * scale for t in totals], axis=0)
    hi, mid, lo = (p.astype(jnp.float32) for p in split(value, 3))
    rest = depth - 4 * value.shape[0]
    index = lax.broadcasted_iota(jnp.int32, (rest, value.shape[1]), 0)
    tail = jnp.where(index < ones, 1.0, 0.0)
    return jnp.concatenate([hi, mid, lo, hi, tail], axis=0).astype(jnp.bfloat16)


def layers_kernel(absorber, zenith, coef, weight, left, drops, spread):
    species, levels, rows, width = absorber.shape
    terms = coef.shape[1]
    group = species * rows
    depth = left.shape[1]
    c_pieces = split(coef[...], 2)
    w_pieces = split(jnp.log2(weight[...]), 3)
    lane = lax.broadcasted_iota(jnp.int32, (rows, depth), 1)
    row = lax.broadcasted_iota(jnp.int32, (rows, depth), 0)
    ones_at = 4 * group
    stack = jnp.concatenate([p.astype(jnp.float32) for p in c_pieces + w_pieces], axis=0)
    count = stack.shape[0]
    pick_row = lax.broadcasted_iota(jnp.int32, (count, depth), 0)
    pick_lane = lax.broadcasted_iota(jnp.int32, (count, depth), 1)
    kind = pick_lane // group
    wanted = jnp.where(kind == 3, species, 0) + (pick_lane % group) // rows
    wanted = jnp.where(kind >= 4, 2 * species + pick_lane - ones_at, wanted)
    pick = (pick_row == wanted).astype(jnp.bfloat16)
    spread[...] = lax.dot_general(
        stack.astype(jnp.bfloat16),
        pick,
        (((0,), (0,)), ((), ())),
        preferred_element_type=jnp.float32,
    )
    mask = ((lane % rows == row) | (lane >= ones_at)).astype(jnp.float32)
    for g in range(0, terms, 2):
        pair = [jnp.broadcast_to(spread[pl.ds(g + i, 1), :], (rows, depth)) * mask for i in (0, 1)]
        left[pl.ds(g * rows, 2 * rows), :] = jnp.concatenate(pair, axis=0).astype(jnp.bfloat16)

    scale = -log2e / zenith[...]
    totals = [jnp.zeros((rows, width), jnp.float32)] * species
    blocks = []
    for k in range(levels + 1):
        if k:
            totals = [totals[s] + absorber[s, k - 1] for s in range(species)]
        blocks.append(amount_rows(totals, scale, depth, 3))
    right = jnp.concatenate(blocks, axis=1)
    chunk = 448
    for start in range(0, terms * rows, chunk):
        out = jnp.exp2(
            jnp.dot(left[pl.ds(start, chunk), :], right, preferred_element_type=jnp.float32)
        )
        for k in range(levels):
            drop = out[:, k * width : (k + 1) * width] - out[:, (k + 1) * width : (k + 2) * width]
            drops[k, pl.ds(start, chunk), :] = drop


def radiate_kernel(left, drops, upper, zenith, lit, thickness, heat):
    levels, rows, width = heat.shape
    depth = left.shape[1]
    species = upper.shape[0]
    zen = zenith[...]
    below = lax.axis_index("lev") > 0
    totals = [jnp.where(below, upper[s], 0.0) for s in range(species)]
    right = amount_rows(totals, -log2e / zen, depth, 0)
    lit_zenith = jnp.where(lit[...] == 1, zen, 0.0)
    factors = [lit_zenith / thickness[k] for k in range(levels)]
    chunk = 448
    sums = [jnp.zeros((rows, width), jnp.float32) for _ in range(levels)]
    for start in range(0, left.shape[0], chunk):
        above = jnp.exp2(
            jnp.dot(left[pl.ds(start, chunk), :], right, preferred_element_type=jnp.float32)
        )
        for k in range(levels):
            absorbed = above * drops[k, pl.ds(start, chunk), :]
            sums[k] = sums[k] + jnp.sum(absorbed.reshape(chunk // rows, rows, width), axis=0)
    for k in range(levels):
        heat[k] = factors[k] * sums[k]


def edge_kernel(own_heat, other_heat, second, kappa, fixed, edge):
    levels, rows, width = own_heat.shape
    stencil = Stencil(rows, width)
    heats = [own_heat[k] for k in range(levels)] + [None] * (8 - levels)
    heats = heats + [other_heat[k] for k in range(levels)]
    strips = to_strips(stencil.lane, jnp.zeros((rows, width), jnp.float32), heats)
    r = second[...] + stencil.residual(strips, kappa[...])
    joined = stencil.rows_joined(r, pltpu.roll(r, width // 2, 1))
    node = stencil.lane % strip
    edge[...] = jnp.where((node == points - 1) | (node == points), joined, fixed[...])


def tiles_of(field):
    gap = [None] * (8 - field.shape[0])
    return [t for n in range(2) for t in [field[l, n] for l in range(field.shape[0])] + gap]


def state_kernel(own_state, other_state, first_tend, second, span_out, second_strips, kappa_strips, fixed, mine):
    levels = own_state.shape[0] - 1
    rows, width = own_state.shape[1:]
    stencil = Stencil(rows, width)
    lane = stencil.lane
    zero = jnp.zeros((rows, width), jnp.float32)
    air = jnp.stack([own_state[:levels], other_state[:levels]], axis=1)
    kappa = jnp.stack([own_state[levels], other_state[levels]], axis=0)
    r = stencil.residual(air, kappa)
    joined = stencil.rows_joined(r, jnp.concatenate([r[:, 1:], r[:, :1]], axis=1))
    tend = stencil.inv_mass * stencil.columns_joined(joined)
    first_tend[...] = tend[:, 0]
    r = stencil.residual(tend, kappa)
    second[...] = r
    second_strips[...] = to_strips(lane, zero, tiles_of(r))
    left_side = lane < width // 2
    node_x = stencil.nodes[1]
    to_edge = jnp.where(left_side, by_node(node_x, table[:, 0]), by_node(node_x, table[:, 3]))
    span = stencil.apply("t", 1, kappa * stencil.weight_x * to_edge)
    in_edge = (lane < points) | (lane >= width - points)
    span = jnp.where(in_edge, span, 0.0)
    span_out[...] = span
    own = to_strips(lane, zero, tiles_of(joined))
    by_level = lambda field: to_strips(
        lane, zero, tiles_of(jnp.broadcast_to(field[None], (levels,) + field.shape))
    )
    kappa_edge = by_level(kappa)
    kappa_strips[...] = kappa_edge
    out = zero
    node = lane % strip
    for step, value in ((1, own), (2, by_level(span)), (3, kappa_edge)):
        out = jnp.where(node == points - 1 - step, pltpu.roll(value, width - step, 1), out)
        out = jnp.where(node == points + step, pltpu.roll(value, step, 1), out)
    fixed[...] = out
    change = stencil.inv_mass_y * (1.0 / mass_points[0]) * own
    mine[0] = change
    mine[1] = stencil.weight_y * stencil.apply("d", 0, change)


def base_kernel(own_state, other_state, own_heat, other_heat, first_tend, second, heat_out, base):
    levels, rows, width = own_heat.shape
    stencil = Stencil(rows, width)
    own = own_heat[...]
    heat_out[...] = own
    heat = jnp.stack([own, other_heat[...]], axis=1)
    kappa = jnp.stack([own_state[levels], other_state[levels]], axis=0)
    r = second[...] + stencil.residual(heat, kappa)
    joined = stencil.rows_joined(r[:, 0], r[:, 1])
    base[...] = (
        own_state[:levels]
        + time_step * (first_tend[...] + own)
        + (0.5 * time_step * time_step) * (stencil.inv_mass * stencil.columns_joined(joined))
    )


def step_kernel(base, span, kappa, mine, from_before, from_after, out):
    levels, rows, width = base.shape
    half = width // 2
    stencil = Stencil(rows, width)
    lane = stencil.lane
    before, after = from_before[...], from_after[...]
    at_first = lane % strip == points

    def of_mates(step):
        return jnp.where(at_first, pltpu.roll(before, step, 1), pltpu.roll(after, width - step, 1))

    change = stencil.inv_mass_y * (1.0 / mass_points[0]) * of_mates(2)
    flux = of_mates(4) * mine[1] + stencil.weight_y * kappa[...] * stencil.apply("d", 0, change)
    r = -gll_weights[0] * stencil.apply("t", 0, flux) - stencil.weight_y * of_mates(3) * mine[0]
    add = of_mates(1) + stencil.rows_joined(r, pltpu.roll(r, half, 1))
    edges = (lane == 0) | (lane == width - 1)

    def spread(tile, at):
        low = jnp.broadcast_to(tile[:, at + points : at + points + 1], (rows, width))
        high = jnp.broadcast_to(tile[:, at + points - 1 : at + points], (rows, width))
        return jnp.where(lane < half, low, high)

    for l in range(levels):
        changes = [spread(change, t * half + strip * l) for t in range(2)]
        r = [-stencil.weight_y * span[t] * changes[t] for t in range(2)]
        moved = stencil.columns_joined(stencil.rows_joined(r[0], r[1]))
        moved = moved + jnp.where(edges, spread(add, strip * l), 0.0)
        out[l] = (
            base[l]
            + time_step * jnp.where(edges, changes[0], 0.0)
            + (0.5 * time_step * time_step) * stencil.inv_mass * moved
        )


def swap(value, axis, pairs):
    route = [(a, b) for a, b in pairs] + [(b, a) for a, b in pairs]
    return lax.ppermute(value, axis, route)


def shards(
    air_state, diffusivity, absorber, thickness, cos_zenith, sunlit, absorb_coef, solar_weight
):
    levels, rows, width = air_state.shape
    terms = absorb_coef.shape[1]
    tile = lambda n: jax.ShapeDtypeStruct((n, rows, width), jnp.float32)
    big = pltpu.CompilerParams(vmem_limit_bytes=32 * 1024 * 1024)
    weight = solar_weight[None]
    args = (air_state, diffusivity, absorber, thickness, cos_zenith, sunlit, absorb_coef, weight)
    args = tuple(pltpu.with_memory_space_constraint(x, pltpu.HBM) for x in args)
    same = lambda x: jax.ShapeDtypeStruct(x.shape, x.dtype)
    amount, own_state, absorber, thickness, cos_zenith, sunlit, absorb_coef, weight = pl.pallas_call(
        fetch_kernel,
        out_shape=(tile(absorber.shape[0]), tile(levels + 1)) + tuple(same(x) for x in args[2:]),
        in_specs=[pl.BlockSpec(memory_space=pltpu.HBM)] * len(args),
        scratch_shapes=[pltpu.SemaphoreType.DMA((len(args),))],
        compiler_params=pltpu.CompilerParams(vmem_limit_bytes=32 * 1024 * 1024),
        name="fetch",
    )(*args)
    size = lax.axis_size("lev")
    lev = lax.axis_index("lev")
    upper = None
    for step in range(1, size):
        moved = lax.ppermute(amount, "lev", [(i, (i + step) % size) for i in range(size)])
        if size > 2:
            moved = jnp.where(lev >= step, moved, 0.0)
        upper = moved if upper is None else upper + moved
    if upper is None:
        upper = jnp.zeros_like(amount)
    other_state = swap(own_state, "sub", [(0, 1)])
    plane = jax.ShapeDtypeStruct((rows, width), jnp.float32)
    left, drops = pl.pallas_call(
        layers_kernel,
        out_shape=(
            jax.ShapeDtypeStruct((terms * rows, 256), jnp.bfloat16),
            jax.ShapeDtypeStruct((levels, terms * rows, width), jnp.float32),
        ),
        scratch_shapes=[pltpu.VMEM((terms, 256), jnp.float32)],
        compiler_params=big,
        name="layers",
    )(absorber, cos_zenith, absorb_coef, weight)
    own_heat = pl.pallas_call(
        radiate_kernel, out_shape=tile(levels), compiler_params=big, name="radiate"
    )(left, drops, upper, cos_zenith, sunlit, thickness)
    other_heat = swap(own_heat, "sub", [(0, 1)])
    pair = jax.ShapeDtypeStruct((levels, 2, rows, width), jnp.float32)
    first_tend, second, span, second_strips, kappa_strips, fixed, mine = pl.pallas_call(
        state_kernel,
        out_shape=(tile(levels), pair, tile(2), plane, plane, plane, tile(2)),
        compiler_params=big,
        name="state",
    )(own_state, other_state)
    edge = pl.pallas_call(edge_kernel, out_shape=plane, compiler_params=big, name="edges")(
        own_heat, other_heat, second_strips, kappa_strips, fixed
    )
    wide = lax.axis_size("wide")
    from_before = lax.ppermute(edge, "wide", [(i, (i + 1) % wide) for i in range(wide)])
    from_after = lax.ppermute(edge, "wide", [((i + 1) % wide, i) for i in range(wide)])
    heat, base = pl.pallas_call(
        base_kernel, out_shape=(tile(levels), tile(levels)), compiler_params=big, name="base"
    )(own_state, other_state, own_heat, other_heat, first_tend, second)
    new_state = pl.pallas_call(
        step_kernel, out_shape=tile(levels), compiler_params=big, name="step"
    )(base, span, kappa_strips, mine, from_before, from_after)
    return (heat, new_state)


def solution(mesh):
    in_specs = (
        P("lev", ("grp", "sub"), "wide"),
        P(("grp", "sub"), "wide"),
        P(None, "lev", ("grp", "sub"), "wide"),
        P("lev", ("grp", "sub"), "wide"),
        P(("grp", "sub"), "wide"),
        P(("grp", "sub"), "wide"),
        P(),
        P(),
    )
    out_specs = (P("lev", ("grp", "sub"), "wide"), P("lev", ("grp", "sub"), "wide"))
    return jax.shard_map(shards, mesh=mesh, in_specs=in_specs, out_specs=out_specs, check_vma=False)
```
